32 devices in a mesh: rows: 2 (over x), chan: 16 (over z, y, core).
Axes of the slice: x: 2, y: 2, z: 4, core: 2. Of those that a mesh axis runs over, the one named last changes fastest.
Arguments:
- activations: bfloat16 [64, 7, 7, 512], P('rows', None, None, 'chan'), may hold values from 0 to 2
- cotangents: bfloat16 [64, 512, 49], P('rows', 'chan'), may hold values from -0.0005859375 to 0.0005859375
- ordering: int32 [2, 32], P('rows'), may hold values from 0 to 31, each once within a row
- ridge: float32 [32], replicated, may hold values from 0.2 to 2
Outputs:
- gram_panel: float32 [64, 32], P('rows')
- factor_panel: float32 [64, 32], P('rows')
The draws below stay inside these ranges and needn't reach their ends.
Inputs may be any that keep to these rules, and one draw needn't show every extreme that they name: Each row of ordering lists every one of the group's 32 examples once.
All inputs are finite; a program needn't handle non-finite values.
Results may differ from the reference program's by a relative error of at most 0.0003.
Values may be sent and summed in bfloat16 or wider, within the bound.
No kernel may reach another device: no remote copies, remote signals or barrier semaphores. Data moves between devices by JAX's collectives and lax.ppermute only.
A program may use at most 64 MiB of HBM per device.

```python
import math
import jax
import jax.numpy as jnp
from jax import lax

CIN = 512
COUT = 512
SIDE = 7
ROW_DEV = 32
PIV_DEV = 16
HW = 49
GROUPS = 2
ROWS = 64
PIV = 32


def draw_cotangents(key, part):
    scale_base = 0.0413 / math.sqrt(COUT * CIN)
    shared = jax.random.uniform(jax.random.fold_in(key, 7), (COUT, HW), jnp.float32, -1.7, 1.7)
    own_part = jnp.clip(jax.random.normal(key, (ROWS, COUT, HW), jnp.float32), -1.7, 1.7)
    row_scale = jnp.ones((ROWS, 1, 1), jnp.float32)
    values = scale_base * row_scale * (0.6 * shared[None, :, :] + 0.8 * own_part)
    return values.astype(jnp.bfloat16)


def steps_of(own_key, extent, shards, smallest, high):
    factor_of, own = 1.0, jax.random.fold_in(own_key, 6)
    for dim, shards_of in shards:
        steps = jnp.exp(jax.random.uniform(jax.random.fold_in(own, dim), (shards_of,), jnp.float32, smallest / len(shards), high / len(shards)))
        factor_of = factor_of * jnp.repeat(steps, extent[dim] // shards_of).reshape([-1 if axis == dim else 1 for axis in range(len(extent))])
    return factor_of


def setup_inputs(seed: int = 0) -> dict:
    arg_keys = jax.random.split(jax.random.key(seed), 5)
    activations = jnp.clip(2.0 * jax.random.uniform(arg_keys[0], (ROWS, SIDE, SIDE, CIN), jnp.float32) ** steps_of(arg_keys[0], (ROWS, SIDE, SIDE, CIN), ((0, 2), (3, 16)), -0.2, 0.2), 0.0, 2.0).astype(jnp.bfloat16)
    cotangents = draw_cotangents(jax.random.fold_in(arg_keys[4], 71), 0)
    ordering = jax.vmap(lambda own: jax.random.permutation(own, ROW_DEV))(jax.random.split(arg_keys[2], GROUPS)).reshape((GROUPS, ROW_DEV)).astype(jnp.int32)
    ridge = jnp.clip(jnp.exp(jax.random.uniform(arg_keys[3], (PIV,), jnp.float32, math.log(0.2), math.log(2.0))), 0.2, 2.0)
    return {"activations": activations, "cotangents": cotangents, "ordering": ordering, "ridge": ridge}


def jacobian(grad_rows, input_rows):
    example_count = input_rows.shape[0]
    side_len = input_rows.shape[1]
    channel_count = input_rows.shape[3]
    padded = jnp.pad(input_rows.astype(jnp.float32), ((0, 0), (1, 1), (1, 1), (0, 0)))
    grads_wide = grad_rows.astype(jnp.float32)
    columns = []
    for row_shift in range(3):
        for col_shift in range(3):
            window = padded[:, row_shift:row_shift + side_len, col_shift:col_shift + side_len, :]
            window = window.reshape(example_count, side_len * side_len, channel_count)
            columns.append(jnp.einsum('ncp,npq->ncq', grads_wide, window))
    stacked = jnp.stack(columns, axis=2).astype(jnp.bfloat16)
    return stacked.reshape(example_count, -1)

def reference(activations, cotangents, ordering, ridge):
    bases = jnp.arange(GROUPS, dtype=jnp.int32)[:, None] * ROW_DEV
    row_index = (bases + ordering.astype(jnp.int32)).reshape(-1)
    pivot_index = (bases + jnp.arange(PIV_DEV, dtype=jnp.int32)[None, :]).reshape(-1)
    row_inputs = jnp.take(activations, row_index, axis=0)
    row_grads = jnp.take(cotangents, row_index, axis=0)
    pivot_inputs = jnp.take(row_inputs, pivot_index, axis=0)
    pivot_grads = jnp.take(row_grads, pivot_index, axis=0)
    block_width = 16 if COUT % 16 == 0 else COUT

    def accumulate(running, block_index):
        first_channel = (block_index * block_width).astype(jnp.int32)
        own_block = lax.dynamic_slice_in_dim(row_grads, first_channel, block_width, 1)
        pivot_block = lax.dynamic_slice_in_dim(pivot_grads, first_channel, block_width, 1)
        own_jac = jacobian(own_block, row_inputs)
        pivot_jac = jacobian(pivot_block, pivot_inputs)
        product = lax.dot_general(own_jac.astype(jnp.float32), pivot_jac.astype(jnp.float32), (((1,), (1,)), ((), ())), preferred_element_type=jnp.float32)
        return (running + product, None)
    gram_panel, _ = lax.scan(accumulate, jnp.zeros((ROWS, PIV), jnp.float32), jnp.arange(COUT // block_width, dtype=jnp.int32))
    diag_block = jnp.take(gram_panel, pivot_index, axis=0)
    system = 0.5 * (diag_block + diag_block.T) + jnp.diag(ridge)
    lower = jnp.linalg.cholesky(system)
    factor_panel = jax.scipy.linalg.solve_triangular(lower, gram_panel.T, lower=True).T
    return (gram_panel, factor_panel)
```

```python
import functools

import jax
import jax.numpy as jnp
from jax import lax
from jax.experimental import pallas as pl
from jax.experimental.pallas import tpu as pltpu
from jax.sharding import PartitionSpec as P

PIV_DEV = 16

SIDE = 7
PITCH = 8
GROUPS4 = 14
CH = 32
EX = 32
LANES = 128
F32 = jnp.float32
BF16 = jnp.bfloat16


def prep_kernel(order_ref, x_ref, g_ref, xo_ref, go_ref, xp_ref, gp_ref, gs, gt, gout):
    row_id = lax.broadcasted_iota(jnp.int32, (EX, EX), 0)
    col_id = lax.broadcasted_iota(jnp.int32, (EX, EX), 1)
    onehot = jnp.zeros((EX, EX), F32)
    for k in range(EX):
        example = order_ref[0, k]
        onehot = jnp.where((row_id == k) & (col_id == example), 1.0, onehot)
        gs[k * CH:(k + 1) * CH, 0:SIDE * SIDE] = g_ref[example].astype(F32)
    onehot = onehot.astype(BF16)
    zero_block = jnp.zeros((EX, CH), BF16)
    for group in range(GROUPS4):
        pieces = []
        for j in range(4):
            py, px = group // 2, (group % 2) * 4 + j
            pieces.append(x_ref[py * SIDE + px] if px < SIDE else zero_block)
        packed = jnp.concatenate(pieces, axis=1)
        ordered = jnp.dot(onehot, packed, preferred_element_type=F32).astype(BF16)
        xo_ref[group] = ordered
        xp_ref[group] = ordered[:PIV_DEV]
    block_id = lax.broadcasted_iota(jnp.int32, (GROUPS4, LANES), 1) // CH
    for quad in range(EX // 4):
        flipped = jnp.transpose(gs[quad * LANES:(quad + 1) * LANES, :])
        for py in range(SIDE):
            gt[py * PITCH:py * PITCH + SIDE, :] = flipped[py * SIDE:(py + 1) * SIDE, :]
            gt[py * PITCH + SIDE:(py + 1) * PITCH, :] = jnp.zeros((1, LANES), F32)
        parts = [gt[pl.ds(j, GROUPS4, stride=4), :] for j in range(4)]
        for e in range(4):
            merged = jnp.zeros((GROUPS4, LANES), F32)
            for j in range(4):
                shift = (CH * (j - e)) % LANES
                moved = pltpu.roll(parts[j], shift, 1) if shift else parts[j]
                merged = jnp.where(block_id == j, moved, merged)
            gout[pl.ds(quad * 4 + e, GROUPS4, stride=EX), :] = merged
    for group in range(GROUPS4):
        ordered = gout[group * EX:(group + 1) * EX, :].astype(BF16)
        go_ref[group] = ordered
        gp_ref[group] = ordered[:PIV_DEV]


def prep(order, x, g):
    full = jax.ShapeDtypeStruct((GROUPS4, EX, LANES), BF16)
    part = jax.ShapeDtypeStruct((GROUPS4, PIV_DEV, LANES), BF16)
    vmem = pl.BlockSpec(memory_space=pltpu.VMEM)
    return pl.pallas_call(
        prep_kernel,
        out_shape=(full, full, part, part),
        in_specs=[pl.BlockSpec(memory_space=pltpu.SMEM), vmem, vmem],
        out_specs=(vmem,) * 4,
        scratch_shapes=[
            pltpu.VMEM((EX * CH, LANES), F32),
            pltpu.VMEM((SIDE * PITCH, LANES), F32),
            pltpu.VMEM((GROUPS4 * EX, LANES), F32),
        ],
        compiler_params=pltpu.CompilerParams(vmem_limit_bytes=16 << 20),
        name="prep",
    )(order, x, g)


def unpack(refs, group):
    values = [ref[group] for ref in refs]
    return [
        jnp.concatenate([v[:, j * CH:(j + 1) * CH] for v in values], axis=1)
        for j in range(4)
    ]


ROWB = SIDE * EX
COLB = PITCH * EX


def main_kernel(*refs):
    xo, xc, go, gc = refs[0:4], refs[4:8], refs[8:12], refs[12:16]
    out_ref, lx, rx, lg, rg, t = refs[16:]
    zero_rows = jnp.zeros((EX, LANES), BF16)
    for py in range(SIDE):
        first, last = py * ROWB, py * ROWB + ROWB - EX
        lx[first:first + EX, 0:LANES] = zero_rows
        lx[last:last + EX, 2 * LANES:3 * LANES] = zero_rows
        first, last = py * COLB, py * COLB + COLB - EX
        rx[first:first + EX, 0:LANES] = zero_rows
        rx[last - EX:last, 2 * LANES:3 * LANES] = zero_rows
        for d in range(3):
            rx[last:last + EX, d * LANES:(d + 1) * LANES] = zero_rows
        rg[last:last + EX, :] = zero_rows
    for group in range(GROUPS4):
        own_x, other_x = unpack(xo, group), unpack(xc, group)
        own_g, other_g = unpack(go, group), unpack(gc, group)
        for j in range(4):
            py, px = group // 2, (group % 2) * 4 + j
            if px == SIDE:
                continue
            row, col = (py * SIDE + px) * EX, (py * PITCH + px) * EX
            piv_x = jnp.concatenate([own_x[j][:PIV_DEV], other_x[j]], axis=0)
            for d in (-1, 0, 1):
                if 0 <= px - d < SIDE:
                    lanes = slice((d + 1) * LANES, (d + 2) * LANES)
                    lx[row - d * EX:row - d * EX + EX, lanes] = own_x[j]
                    rx[col - d * EX:col - d * EX + EX, lanes] = piv_x
            lg[row:row + EX, :] = own_g[j]
            rg[col:col + EX, :] = jnp.concatenate([own_g[j][:PIV_DEV], other_g[j]], axis=0)

    contract = (((1,), (1,)), ((), ()))
    for qy in range(SIDE):
        right = rx[qy * COLB:(qy + 1) * COLB, :]
        for py in range(SIDE):
            left = lx[py * ROWB:(py + 1) * ROWB, :]
            t[py * SIDE + qy] = lax.dot_general(left, right, contract, preferred_element_type=F32)
    acc = jnp.zeros((EX, COLB), F32)
    for qy in range(SIDE):
        right = rg[qy * COLB:(qy + 1) * COLB, :]
        for py in range(SIDE):
            left = lg[py * ROWB:(py + 1) * ROWB, :]
            gg = lax.dot_general(left, right, contract, preferred_element_type=F32)
            for px in range(SIDE):
                rows = slice(px * EX, (px + 1) * EX)
                total = t[py * SIDE + qy, rows, :]
                if py > 0 and qy > 0:
                    total = total + t[(py - 1) * SIDE + qy - 1, rows, :]
                if py < SIDE - 1 and qy < SIDE - 1:
                    total = total + t[(py + 1) * SIDE + qy + 1, rows, :]
                acc = acc + gg[rows, :] * total
    folded = acc[:, :LANES] + acc[:, LANES:]
    folded = folded + pltpu.roll(folded, 64, 1)
    folded = folded + pltpu.roll(folded, 32, 1)
    folded = jnp.where(lax.axis_index("rows") == 1, pltpu.roll(folded, 16, 1), folded)
    block_id = lax.broadcasted_iota(jnp.int32, (8, LANES), 1) // EX
    packed = folded[0:8]
    for j in range(1, 4):
        packed = jnp.where(block_id == j, folded[8 * j:8 * j + 8], packed)
    out_ref[...] = packed


def main(arrays):
    vmem = pl.BlockSpec(memory_space=pltpu.VMEM)
    rows, cols = SIDE * ROWB, SIDE * COLB
    return pl.pallas_call(
        main_kernel,
        out_shape=jax.ShapeDtypeStruct((8, LANES), F32),
        in_specs=[vmem] * 16,
        out_specs=vmem,
        scratch_shapes=[
            pltpu.VMEM((rows, 3 * LANES), BF16),
            pltpu.VMEM((cols, 3 * LANES), BF16),
            pltpu.VMEM((rows, LANES), BF16),
            pltpu.VMEM((cols, LANES), BF16),
            pltpu.VMEM((SIDE * SIDE, ROWB, COLB), F32),
        ],
        compiler_params=pltpu.CompilerParams(vmem_limit_bytes=40 << 20),
        name="terms",
    )(*arrays)


def rows_of(packed, count):
    return jnp.concatenate(
        [packed[:, EX * j:EX * (j + 1)] for j in range(count)], axis=0
    )


def final_kernel(*refs):
    own, other = refs[0:4], refs[4:8]
    ridge_ref, gram_ref, factor_ref = refs[8:]
    panel = rows_of((own[0][...] + own[1][...]) + (own[2][...] + own[3][...]), 4)
    cross = rows_of((other[0][...] + other[1][...]) + (other[2][...] + other[3][...]), 2)
    gram_ref[...] = panel
    first = lax.axis_index("rows") == 0
    mine = panel[:PIV_DEV]
    diag = jnp.concatenate([jnp.where(first, mine, cross), jnp.where(first, cross, mine)], axis=0)
    row_id = lax.broadcasted_iota(jnp.int32, (EX, EX), 0)
    col_id = lax.broadcasted_iota(jnp.int32, (EX, EX), 1)
    ridge = jnp.where(row_id == col_id, jnp.broadcast_to(ridge_ref[...], (EX, EX)), 0.0)
    system = 0.5 * (diag + jnp.transpose(diag)) + ridge
    factor = jnp.zeros((EX, EX), F32)
    for j in range(EX):
        scale = lax.rsqrt(system[j:j + 1, j:j + 1])
        line = system[j:j + 1, :] * scale
        below = system[:, j:j + 1] * scale
        solved = panel[:, j:j + 1] * scale
        factor = jnp.where(col_id == j, solved, factor)
        if j < EX - 1:
            system = system - below * line
            panel = panel - solved * line
    factor_ref[...] = factor


def final(own, other, ridge):
    vmem = pl.BlockSpec(memory_space=pltpu.VMEM)
    out = jax.ShapeDtypeStruct((EX, EX), F32)
    return pl.pallas_call(
        final_kernel,
        out_shape=(out, out),
        in_specs=[vmem] * 9,
        out_specs=(vmem, vmem),
        name="solve",
    )(*own, *other, ridge.reshape(1, EX))


def exchange(value, count, flip):
    return lax.ppermute(value, "chan", [(i, i ^ flip) for i in range(count)])


def exchange_across(value, count, flip):
    pairs = [(g * count + i, (1 - g) * count + (i ^ flip)) for g in range(2) for i in range(count)]
    return lax.ppermute(value, ("rows", "chan"), pairs)


def local_packed(count, activations, cotangents, ordering, ridge):
    near, far = (1, 2, 3), (4, 8, 12)
    x = jnp.transpose(activations, (1, 2, 0, 3)).reshape(SIDE * SIDE, EX, CH)
    xo, go, xp, gp = prep(ordering, x, cotangents)
    own_g = [go] + [exchange(go, count, f) for f in far]
    other_g = [exchange_across(gp, count, f) for f in (0,) + far]
    own_x = [xo] + [exchange(xo, count, f) for f in near]
    other_x = [exchange_across(xp, count, f) for f in (0,) + near]
    term = main(own_x + other_x + own_g + other_g)
    terms = [term] + [exchange(term, count, f) for f in near]
    part = (terms[0] + terms[1]) + (terms[2] + terms[3])
    own = [part] + [exchange(part, count, f) for f in far]
    other = [exchange_across(part, count, f) for f in (0,) + far]
    return final(own, other, ridge)


def jacobian_block(grad_rows, input_rows):
    example_count = input_rows.shape[0]
    side_len = input_rows.shape[1]
    channel_count = input_rows.shape[3]
    grad_count = grad_rows.shape[1]
    grid_grads = grad_rows.reshape(example_count, grad_count, side_len, side_len)
    padded_grads = jnp.pad(grid_grads, ((0, 0), (0, 0), (1, 1), (1, 1)))
    shifted = []
    for row_shift in range(3):
        for col_shift in range(3):
            window = padded_grads[
                :,
                :,
                2 - row_shift : 2 - row_shift + side_len,
                2 - col_shift : 2 - col_shift + side_len,
            ]
            shifted.append(window.reshape(example_count, grad_count, side_len * side_len))
    stacked_grads = jnp.stack(shifted, axis=2).reshape(
        example_count, grad_count * 9, side_len * side_len
    )
    flat_inputs = input_rows.reshape(example_count, side_len * side_len, channel_count)
    product = jnp.einsum(
        "nkp,npq->nkq", stacked_grads, flat_inputs, preferred_element_type=jnp.float32
    )
    return product.astype(jnp.bfloat16).reshape(example_count, -1)


def gram_block(left_rows, right_rows):
    return lax.dot_general(
        left_rows, right_rows, (((1,), (1,)), ((), ())), preferred_element_type=jnp.float32
    )


def local(activations, cotangents, ordering, ridge):
    local_order = ordering[0]
    own_inputs = jnp.take(activations, local_order, axis=0)
    own_grads = jnp.take(cotangents, local_order, axis=0)
    pivot_count = PIV_DEV
    pivot_inputs, pivot_grads = (
        lax.all_gather(own_inputs[:pivot_count], "rows", axis=0, tiled=True),
        lax.all_gather(own_grads[:pivot_count], "rows", axis=0, tiled=True),
    )
    full_own, full_pivot = (
        lax.all_gather(own_inputs, "chan", axis=3, tiled=True),
        lax.all_gather(pivot_inputs, "chan", axis=3, tiled=True),
    )
    own_jac = jacobian_block(own_grads, full_own)
    pivot_jac = jacobian_block(pivot_grads, full_pivot)
    partial_panel = gram_block(own_jac, pivot_jac)
    gram_panel = lax.psum(partial_panel, "chan")
    diag_block = lax.all_gather(gram_panel[:pivot_count], "rows", axis=0, tiled=True)
    system = 0.5 * (diag_block + diag_block.T) + jnp.diag(ridge)
    lower = jnp.linalg.cholesky(system)
    factor_panel = jax.scipy.linalg.solve_triangular(lower, gram_panel.T, lower=True).T
    return (gram_panel, factor_panel)


def solution(mesh):
    row_groups, count = mesh.shape["rows"], mesh.shape["chan"]
    packed = row_groups == 2 and count == 16
    return jax.shard_map(
        functools.partial(local_packed, count) if packed else local,
        mesh=mesh,
        in_specs=(P("rows", None, None, "chan"), P("rows", "chan", None), P("rows", None), P()),
        out_specs=(P("rows", None), P("rows", None)),
        check_vma=False,
    )
```

```python
import functools

import jax
import jax.numpy as jnp
from jax import lax
from jax.experimental import pallas as pl
from jax.experimental.pallas import tpu as pltpu
from jax.sharding import PartitionSpec as P

PIV_DEV = 16

SIDE = 7
PITCH = 8
GROUPS4 = 14
CH = 32
EX = 32
LANES = 128
F32 = jnp.float32
BF16 = jnp.bfloat16


def prep_kernel(order_ref, x_ref, g_ref, xo_ref, go_ref, xp_ref, gp_ref, gs, gt, gout):
    row_id = lax.broadcasted_iota(jnp.int32, (EX, EX), 0)
    col_id = lax.broadcasted_iota(jnp.int32, (EX, EX), 1)
    onehot = jnp.zeros((EX, EX), F32)
    for k in range(EX):
        example = order_ref[0, k]
        onehot = jnp.where((row_id == k) & (col_id == example), 1.0, onehot)
        gs[k * CH:(k + 1) * CH, 0:SIDE * SIDE] = g_ref[example].astype(F32)
    onehot = onehot.astype(BF16)
    zero_block = jnp.zeros((EX, CH), BF16)
    for group in range(GROUPS4):
        pieces = []
        for j in range(4):
            py, px = group // 2, (group % 2) * 4 + j
            pieces.append(x_ref[py * SIDE + px] if px < SIDE else zero_block)
        packed = jnp.concatenate(pieces, axis=1)
        ordered = jnp.dot(onehot, packed, preferred_element_type=F32).astype(BF16)
        xo_ref[group] = ordered
        xp_ref[group] = ordered[:PIV_DEV]
    block_id = lax.broadcasted_iota(jnp.int32, (GROUPS4, LANES), 1) // CH
    for quad in range(EX // 4):
        flipped = jnp.transpose(gs[quad * LANES:(quad + 1) * LANES, :])
        for py in range(SIDE):
            gt[py * PITCH:py * PITCH + SIDE, :] = flipped[py * SIDE:(py + 1) * SIDE, :]
            gt[py * PITCH + SIDE:(py + 1) * PITCH, :] = jnp.zeros((1, LANES), F32)
        parts = [gt[pl.ds(j, GROUPS4, stride=4), :] for j in range(4)]
        for e in range(4):
            merged = jnp.zeros((GROUPS4, LANES), F32)
            for j in range(4):
                shift = (CH * (j - e)) % LANES
                moved = pltpu.roll(parts[j], shift, 1) if shift else parts[j]
                merged = jnp.where(block_id == j, moved, merged)
            gout[pl.ds(quad * 4 + e, GROUPS4, stride=EX), :] = merged
    for group in range(GROUPS4):
        ordered = gout[group * EX:(group + 1) * EX, :].astype(BF16)
        go_ref[group] = ordered
        gp_ref[group] = ordered[:PIV_DEV]


def prep(order, x, g):
    full = jax.ShapeDtypeStruct((GROUPS4, EX, LANES), BF16)
    part = jax.ShapeDtypeStruct((GROUPS4, PIV_DEV, LANES), BF16)
    vmem = pl.BlockSpec(memory_space=pltpu.VMEM)
    return pl.pallas_call(
        prep_kernel,
        out_shape=(full, full, part, part),
        in_specs=[pl.BlockSpec(memory_space=pltpu.SMEM), vmem, vmem],
        out_specs=(vmem,) * 4,
        scratch_shapes=[
            pltpu.VMEM((EX * CH, LANES), F32),
            pltpu.VMEM((SIDE * PITCH, LANES), F32),
            pltpu.VMEM((GROUPS4 * EX, LANES), F32),
        ],
        compiler_params=pltpu.CompilerParams(vmem_limit_bytes=16 << 20),
        name="prep",
    )(order, x, g)


def unpack(refs, group):
    values = [ref[group] for ref in refs]
    return [
        jnp.concatenate([v[:, j * CH:(j + 1) * CH] for v in values], axis=1)
        for j in range(4)
    ]


ROWB = SIDE * EX
COLB = PITCH * EX


def main_kernel(*refs):
    xo, xc, go, gc = refs[0:4], refs[4:8], refs[8:12], refs[12:16]
    out_ref, lx, rx, lg, rg, t = refs[16:]
    zero_rows = jnp.zeros((EX, LANES), BF16)
    for py in range(SIDE):
        first, last = py * ROWB, py * ROWB + ROWB - EX
        lx[first:first + EX, 0:LANES] = zero_rows
        lx[last:last + EX, 2 * LANES:3 * LANES] = zero_rows
        first, last = py * COLB, py * COLB + COLB - EX
        rx[first:first + EX, 0:LANES] = zero_rows
        rx[last - EX:last, 2 * LANES:3 * LANES] = zero_rows
        for d in range(3):
            rx[last:last + EX, d * LANES:(d + 1) * LANES] = zero_rows
        rg[last:last + EX, :] = zero_rows
    for group in range(GROUPS4):
        own_x, other_x = unpack(xo, group), unpack(xc, group)
        own_g, other_g = unpack(go, group), unpack(gc, group)
        for j in range(4):
            py, px = group // 2, (group % 2) * 4 + j
            if px == SIDE:
                continue
            row, col = (py * SIDE + px) * EX, (py * PITCH + px) * EX
            piv_x = jnp.concatenate([own_x[j][:PIV_DEV], other_x[j]], axis=0)
            for d in (-1, 0, 1):
                if 0 <= px - d < SIDE:
                    lanes = slice((d + 1) * LANES, (d + 2) * LANES)
                    lx[row - d * EX:row - d * EX + EX, lanes] = own_x[j]
                    rx[col - d * EX:col - d * EX + EX, lanes] = piv_x
            lg[row:row + EX, :] = own_g[j]
            rg[col:col + EX, :] = jnp.concatenate([own_g[j][:PIV_DEV], other_g[j]], axis=0)

    contract = (((1,), (1,)), ((), ()))
    for qy in range(SIDE):
        right = rx[qy * COLB:(qy + 1) * COLB, :]
        for py in range(SIDE):
            left = lx[py * ROWB:(py + 1) * ROWB, :]
            t[py * SIDE + qy] = lax.dot_general(left, right, contract, preferred_element_type=F32)
    acc = jnp.zeros((EX, COLB), F32)
    for qy in range(SIDE):
        right = rg[qy * COLB:(qy + 1) * COLB, :]
        for py in range(SIDE):
            left = lg[py * ROWB:(py + 1) * ROWB, :]
            gg = lax.dot_general(left, right, contract, preferred_element_type=F32)
            for px in range(SIDE):
                rows = slice(px * EX, (px + 1) * EX)
                total = t[py * SIDE + qy, rows, :]
                if py > 0 and qy > 0:
                    total = total + t[(py - 1) * SIDE + qy - 1, rows, :]
                if py < SIDE - 1 and qy < SIDE - 1:
                    total = total + t[(py + 1) * SIDE + qy + 1, rows, :]
                acc = acc + gg[rows, :] * total
    folded = acc[:, :LANES] + acc[:, LANES:]
    folded = folded + pltpu.roll(folded, 64, 1)
    folded = folded + pltpu.roll(folded, 32, 1)
    folded = jnp.where(lax.axis_index("rows") == 1, pltpu.roll(folded, 16, 1), folded)
    block_id = lax.broadcasted_iota(jnp.int32, (8, LANES), 1) // EX
    packed = folded[0:8]
    for j in range(1, 4):
        packed = jnp.where(block_id == j, folded[8 * j:8 * j + 8], packed)
    out_ref[...] = packed


def main(arrays):
    vmem = pl.BlockSpec(memory_space=pltpu.VMEM)
    rows, cols = SIDE * ROWB, SIDE * COLB
    return pl.pallas_call(
        main_kernel,
        out_shape=jax.ShapeDtypeStruct((8, LANES), F32),
        in_specs=[vmem] * 16,
        out_specs=vmem,
        scratch_shapes=[
            pltpu.VMEM((rows, 3 * LANES), BF16),
            pltpu.VMEM((cols, 3 * LANES), BF16),
            pltpu.VMEM((rows, LANES), BF16),
            pltpu.VMEM((cols, LANES), BF16),
            pltpu.VMEM((SIDE * SIDE, ROWB, COLB), F32),
        ],
        compiler_params=pltpu.CompilerParams(vmem_limit_bytes=40 << 20),
        name="terms",
    )(*arrays)


def rows_of(packed, count):
    return jnp.concatenate(
        [packed[:, EX * j:EX * (j + 1)] for j in range(count)], axis=0
    )


def tree_sum(values):
    while len(values) > 1:
        values = [a + b for a, b in zip(values[0::2], values[1::2])]
    return values[0]


def final_kernel(terms_ref, ridge_ref, gram_ref, factor_ref):
    count = terms_ref.shape[0] // 2
    sums = [tree_sum([terms_ref[g * count + i] for i in range(count)]) for g in range(2)]
    first = lax.axis_index("rows") == 0
    panel = rows_of(jnp.where(first, sums[0], sums[1]), 4)
    gram_ref[...] = panel
    diag = jnp.concatenate([rows_of(total, 2) for total in sums], axis=0)
    row_id = lax.broadcasted_iota(jnp.int32, (EX, EX), 0)
    col_id = lax.broadcasted_iota(jnp.int32, (EX, EX), 1)
    ridge = jnp.where(row_id == col_id, jnp.broadcast_to(ridge_ref[...], (EX, EX)), 0.0)
    system = 0.5 * (diag + jnp.transpose(diag)) + ridge
    factor = jnp.zeros((EX, EX), F32)
    for j in range(EX):
        scale = lax.rsqrt(system[j:j + 1, j:j + 1])
        line = system[j:j + 1, :] * scale
        below = system[:, j:j + 1] * scale
        solved = panel[:, j:j + 1] * scale
        factor = jnp.where(col_id == j, solved, factor)
        if j < EX - 1:
            system = system - below * line
            panel = panel - solved * line
    factor_ref[...] = factor


def final(terms, ridge):
    vmem = pl.BlockSpec(memory_space=pltpu.VMEM)
    out = jax.ShapeDtypeStruct((EX, EX), F32)
    return pl.pallas_call(
        final_kernel,
        out_shape=(out, out),
        in_specs=[vmem] * 2,
        out_specs=(vmem, vmem),
        name="solve",
    )(terms, ridge.reshape(1, EX))


def exchange(value, count, flip):
    return lax.ppermute(value, "chan", [(i, i ^ flip) for i in range(count)])


def exchange_across(value, count, flip):
    pairs = [(g * count + i, (1 - g) * count + (i ^ flip)) for g in range(2) for i in range(count)]
    return lax.ppermute(value, ("rows", "chan"), pairs)


def local_packed(count, activations, cotangents, ordering, ridge):
    near, far = (1, 2, 3), (4, 8, 12)
    x = jnp.transpose(activations, (1, 2, 0, 3)).reshape(SIDE * SIDE, EX, CH)
    xo, go, xp, gp = prep(ordering, x, cotangents)
    own_g = [go] + [exchange(go, count, f) for f in far]
    other_g = [exchange_across(gp, count, f) for f in (0,) + far]
    own_x = [xo] + [exchange(xo, count, f) for f in near]
    other_x = [exchange_across(xp, count, f) for f in (0,) + near]
    term = main(own_x + other_x + own_g + other_g)
    terms = lax.all_to_all(jnp.broadcast_to(term, (2 * count, 8, LANES)), ("rows", "chan"), 0, 0)
    return final(terms, ridge)


def jacobian_block(grad_rows, input_rows):
    example_count = input_rows.shape[0]
    side_len = input_rows.shape[1]
    channel_count = input_rows.shape[3]
    grad_count = grad_rows.shape[1]
    grid_grads = grad_rows.reshape(example_count, grad_count, side_len, side_len)
    padded_grads = jnp.pad(grid_grads, ((0, 0), (0, 0), (1, 1), (1, 1)))
    shifted = []
    for row_shift in range(3):
        for col_shift in range(3):
            window = padded_grads[
                :,
                :,
                2 - row_shift : 2 - row_shift + side_len,
                2 - col_shift : 2 - col_shift + side_len,
            ]
            shifted.append(window.reshape(example_count, grad_count, side_len * side_len))
    stacked_grads = jnp.stack(shifted, axis=2).reshape(
        example_count, grad_count * 9, side_len * side_len
    )
    flat_inputs = input_rows.reshape(example_count, side_len * side_len, channel_count)
    product = jnp.einsum(
        "nkp,npq->nkq", stacked_grads, flat_inputs, preferred_element_type=jnp.float32
    )
    return product.astype(jnp.bfloat16).reshape(example_count, -1)


def gram_block(left_rows, right_rows):
    return lax.dot_general(
        left_rows, right_rows, (((1,), (1,)), ((), ())), preferred_element_type=jnp.float32
    )


def local(activations, cotangents, ordering, ridge):
    local_order = ordering[0]
    own_inputs = jnp.take(activations, local_order, axis=0)
    own_grads = jnp.take(cotangents, local_order, axis=0)
    pivot_count = PIV_DEV
    pivot_inputs, pivot_grads = (
        lax.all_gather(own_inputs[:pivot_count], "rows", axis=0, tiled=True),
        lax.all_gather(own_grads[:pivot_count], "rows", axis=0, tiled=True),
    )
    full_own, full_pivot = (
        lax.all_gather(own_inputs, "chan", axis=3, tiled=True),
        lax.all_gather(pivot_inputs, "chan", axis=3, tiled=True),
    )
    own_jac = jacobian_block(own_grads, full_own)
    pivot_jac = jacobian_block(pivot_grads, full_pivot)
    partial_panel = gram_block(own_jac, pivot_jac)
    gram_panel = lax.psum(partial_panel, "chan")
    diag_block = lax.all_gather(gram_panel[:pivot_count], "rows", axis=0, tiled=True)
    system = 0.5 * (diag_block + diag_block.T) + jnp.diag(ridge)
    lower = jnp.linalg.cholesky(system)
    factor_panel = jax.scipy.linalg.solve_triangular(lower, gram_panel.T, lower=True).T
    return (gram_panel, factor_panel)


def solution(mesh):
    row_groups, count = mesh.shape["rows"], mesh.shape["chan"]
    packed = row_groups == 2 and count == 16
    return jax.shard_map(
        functools.partial(local_packed, count) if packed else local,
        mesh=mesh,
        in_specs=(P("rows", None, None, "chan"), P("rows", "chan", None), P("rows", None), P()),
        out_specs=(P("rows", None), P("rows", None)),
        check_vma=False,
    )
```

```python
import functools

import jax
import jax.numpy as jnp
from jax import lax
from jax.experimental import pallas as pl
from jax.experimental.pallas import tpu as pltpu
from jax.sharding import PartitionSpec as P

PIV_DEV = 16

SIDE = 7
PITCH = 8
GROUPS4 = 14
CH = 32
EX = 32
LANES = 128
F32 = jnp.float32
BF16 = jnp.bfloat16


def prep_kernel(order_ref, x_ref, g_ref, xo_ref, go_ref, gs, gt, gout):
    row_id = lax.broadcasted_iota(jnp.int32, (EX, EX), 0)
    col_id = lax.broadcasted_iota(jnp.int32, (EX, EX), 1)
    onehot = jnp.zeros((EX, EX), F32)
    for k in range(EX):
        example = order_ref[0, k]
        onehot = jnp.where((row_id == k) & (col_id == example), 1.0, onehot)
        gs[k * CH:(k + 1) * CH, 0:SIDE * SIDE] = g_ref[example].astype(F32)
    onehot = onehot.astype(BF16)
    zero_block = jnp.zeros((EX, CH), BF16)
    for group in range(GROUPS4):
        pieces = []
        for j in range(4):
            py, px = group // 2, (group % 2) * 4 + j
            pieces.append(x_ref[py * SIDE + px] if px < SIDE else zero_block)
        packed = jnp.concatenate(pieces, axis=1)
        xo_ref[group] = jnp.dot(onehot, packed, preferred_element_type=F32).astype(BF16)
    block_id = lax.broadcasted_iota(jnp.int32, (GROUPS4, LANES), 1) // CH
    for quad in range(EX // 4):
        flipped = jnp.transpose(gs[quad * LANES:(quad + 1) * LANES, :])
        for py in range(SIDE):
            gt[py * PITCH:py * PITCH + SIDE, :] = flipped[py * SIDE:(py + 1) * SIDE, :]
            gt[py * PITCH + SIDE:(py + 1) * PITCH, :] = jnp.zeros((1, LANES), F32)
        parts = [gt[pl.ds(j, GROUPS4, stride=4), :] for j in range(4)]
        for e in range(4):
            merged = jnp.zeros((GROUPS4, LANES), F32)
            for j in range(4):
                shift = (CH * (j - e)) % LANES
                moved = pltpu.roll(parts[j], shift, 1) if shift else parts[j]
                merged = jnp.where(block_id == j, moved, merged)
            gout[pl.ds(quad * 4 + e, GROUPS4, stride=EX), :] = merged
    for group in range(GROUPS4):
        go_ref[group] = gout[group * EX:(group + 1) * EX, :].astype(BF16)


def prep(order, x, g):
    full = jax.ShapeDtypeStruct((GROUPS4, EX, LANES), BF16)
    vmem = pl.BlockSpec(memory_space=pltpu.VMEM)
    return pl.pallas_call(
        prep_kernel,
        out_shape=(full, full),
        in_specs=[pl.BlockSpec(memory_space=pltpu.SMEM), vmem, vmem],
        out_specs=(vmem,) * 2,
        scratch_shapes=[
            pltpu.VMEM((EX * CH, LANES), F32),
            pltpu.VMEM((SIDE * PITCH, LANES), F32),
            pltpu.VMEM((GROUPS4 * EX, LANES), F32),
        ],
        compiler_params=pltpu.CompilerParams(vmem_limit_bytes=16 << 20),
        name="prep",
    )(order, x, g)


SPOTS = SIDE * SIDE
ROWB = SIDE * EX
COLB = PITCH * PIV_DEV


def cost(flops, moved):
    return pl.CostEstimate(flops=flops, bytes_accessed=moved, transcendentals=0)


def unpack_kernel(*refs):
    sources, all_ref, piv_ref = refs[:4], refs[4], refs[5]
    for group in range(GROUPS4):
        values = [ref[group] for ref in sources]
        for j in range(4):
            py, px = group // 2, (group % 2) * 4 + j
            if px == SIDE:
                continue
            spot = jnp.concatenate([v[:, j * CH:(j + 1) * CH] for v in values], axis=1)
            all_ref[py * SIDE + px] = spot
            piv_ref[py * SIDE + px] = spot[:PIV_DEV]


def unpack(arrays, name):
    vmem = pl.BlockSpec(memory_space=pltpu.VMEM)
    return pl.pallas_call(
        unpack_kernel,
        out_shape=(
            jax.ShapeDtypeStruct((SPOTS, EX, LANES), BF16),
            jax.ShapeDtypeStruct((SPOTS, PIV_DEV, LANES), BF16),
        ),
        in_specs=[vmem] * 4,
        out_specs=(vmem,) * 2,
        cost_estimate=cost(0, 1 << 20),
        name=name,
    )(*arrays)


def panel_terms(x, g, xp, gp, lx, rx, rg, t):
    for py in range(SIDE):
        for px in range(PITCH):
            row, col = (py * SIDE + px) * EX, (py * PITCH + px) * PIV_DEV
            for d in range(3):
                from_x = px + d - 1
                inside = 0 <= from_x < SIDE and px < SIDE
                lanes = slice(d * LANES, (d + 1) * LANES)
                spot = py * SIDE + from_x
                rx[col:col + PIV_DEV, lanes] = xp[spot] if inside else jnp.zeros((PIV_DEV, LANES), BF16)
                if px < SIDE:
                    lx[row:row + EX, lanes] = x[spot] if inside else jnp.zeros((EX, LANES), BF16)
            rg[col:col + PIV_DEV, :] = gp[py * SIDE + px] if px < SIDE else jnp.zeros((PIV_DEV, LANES), BF16)

    contract = (((1,), (1,)), ((), ()))
    spans = [(qy, min(qy + 2, SIDE)) for qy in range(0, SIDE, 2)]
    for start, stop in spans:
        right = rx[start * COLB:stop * COLB, :]
        for py in range(SIDE):
            left = lx[py * ROWB:(py + 1) * ROWB, :]
            t[py, :, start * COLB:stop * COLB] = lax.dot_general(left, right, contract, preferred_element_type=F32)
    acc = jnp.zeros((EX, COLB), F32)
    for start, stop in spans:
        right = rg[start * COLB:stop * COLB, :]
        for py in range(SIDE):
            left = g[py * SIDE:(py + 1) * SIDE].reshape(ROWB, LANES)
            gg = lax.dot_general(left, right, contract, preferred_element_type=F32)
            for qy in range(start, stop):
                for px in range(SIDE):
                    rows = slice(px * EX, (px + 1) * EX)
                    total = t[py, rows, qy * COLB:(qy + 1) * COLB]
                    if py > 0 and qy > 0:
                        total = total + t[py - 1, rows, (qy - 1) * COLB:qy * COLB]
                    if py < SIDE - 1 and qy < SIDE - 1:
                        total = total + t[py + 1, rows, (qy + 1) * COLB:(qy + 2) * COLB]
                    acc = acc + gg[rows, (qy - start) * COLB:(qy - start + 1) * COLB] * total
    acc = acc + pltpu.roll(acc, 64, 1)
    acc = acc + pltpu.roll(acc, 32, 1)
    return acc + pltpu.roll(acc, 16, 1)


def own_kernel(x, g, xp, gp, out_ref, lx, rx, rg, t):
    out_ref[...] = panel_terms(x, g, xp, gp, lx, rx, rg, t)


def cross_kernel(x, g, xp, gp, own_ref, out_ref, lx, rx, rg, t):
    across = panel_terms(x, g, xp, gp, lx, rx, rg, t)
    lane = lax.broadcasted_iota(jnp.int32, (8, LANES), 1)
    is_own = (lane // PIV_DEV) % 2 == lax.axis_index("rows")
    packed = jnp.zeros((8, LANES), F32)
    for j in range(4):
        rows = slice(8 * j, 8 * j + 8)
        packed = jnp.where(lane // EX == j, jnp.where(is_own, own_ref[rows, :], across[rows]), packed)
    out_ref[...] = packed


def terms(kernel, arrays, shape, name):
    vmem = pl.BlockSpec(memory_space=pltpu.VMEM)
    rows, cols = SIDE * ROWB, SIDE * COLB
    return pl.pallas_call(
        kernel,
        out_shape=jax.ShapeDtypeStruct(shape, F32),
        in_specs=[vmem] * len(arrays),
        out_specs=vmem,
        scratch_shapes=[
            pltpu.VMEM((rows, 3 * LANES), BF16),
            pltpu.VMEM((cols, 3 * LANES), BF16),
            pltpu.VMEM((cols, LANES), BF16),
            pltpu.VMEM((SIDE, ROWB, cols), F32),
        ],
        compiler_params=pltpu.CompilerParams(vmem_limit_bytes=24 << 20),
        cost_estimate=cost(2 * rows * cols * 4 * LANES, 8 << 20),
        name=name,
    )(*arrays)


def rows_of(packed, count):
    return jnp.concatenate(
        [packed[:, EX * j:EX * (j + 1)] for j in range(count)], axis=0
    )


def tree_sum(values):
    while len(values) > 1:
        values = [a + b for a, b in zip(values[0::2], values[1::2])]
    return values[0]


def final_kernel(terms_ref, ridge_ref, gram_ref, factor_ref):
    count = terms_ref.shape[0] // 2
    sums = [tree_sum([terms_ref[g * count + i] for i in range(count)]) for g in range(2)]
    first = lax.axis_index("rows") == 0
    panel = rows_of(jnp.where(first, sums[0], sums[1]), 4)
    gram_ref[...] = panel
    diag = jnp.concatenate([rows_of(total, 2) for total in sums], axis=0)
    row_id = lax.broadcasted_iota(jnp.int32, (EX, EX), 0)
    col_id = lax.broadcasted_iota(jnp.int32, (EX, EX), 1)
    ridge = jnp.where(row_id == col_id, jnp.broadcast_to(ridge_ref[...], (EX, EX)), 0.0)
    system = 0.5 * (diag + jnp.transpose(diag)) + ridge
    factor = jnp.zeros((EX, EX), F32)
    for j in range(EX):
        scale = lax.rsqrt(system[j:j + 1, j:j + 1])
        line = system[j:j + 1, :] * scale
        below = system[:, j:j + 1] * scale
        solved = panel[:, j:j + 1] * scale
        factor = jnp.where(col_id == j, solved, factor)
        if j < EX - 1:
            system = system - below * line
            panel = panel - solved * line
    factor_ref[...] = factor


def final(terms, ridge):
    vmem = pl.BlockSpec(memory_space=pltpu.VMEM)
    out = jax.ShapeDtypeStruct((EX, EX), F32)
    return pl.pallas_call(
        final_kernel,
        out_shape=(out, out),
        in_specs=[vmem] * 2,
        out_specs=(vmem, vmem),
        name="solve",
    )(terms, ridge.reshape(1, EX))


def exchange(value, count, flip):
    return lax.ppermute(value, "chan", [(i, i ^ flip) for i in range(count)])


def exchange_across(value, count):
    pairs = [(g * count + i, (1 - g) * count + i) for g in range(2) for i in range(count)]
    return lax.ppermute(value, ("rows", "chan"), pairs)


def local_packed(count, activations, cotangents, ordering, ridge):
    near, far = (1, 2, 3), (4, 8, 12)
    x = jnp.transpose(activations, (1, 2, 0, 3)).reshape(SIDE * SIDE, EX, CH)
    xo, go = prep(ordering, x, cotangents)
    own_g = [go] + [exchange(go, count, f) for f in far]
    own_x = [xo] + [exchange(xo, count, f) for f in near]
    x_all, x_piv = unpack(own_x, "unpack_x")
    x_cross = exchange_across(x_piv, count)
    g_all, g_piv = unpack(own_g, "unpack_g")
    g_cross = exchange_across(g_piv, count)
    own_term = terms(own_kernel, (x_all, g_all, x_piv, g_piv), (EX, LANES), "terms_own")
    term = terms(cross_kernel, (x_all, g_all, x_cross, g_cross, own_term), (8, LANES), "terms_cross")
    gathered = lax.all_to_all(jnp.broadcast_to(term, (2 * count, 8, LANES)), ("rows", "chan"), 0, 0)
    return final(gathered, ridge)


def jacobian_block(grad_rows, input_rows):
    example_count = input_rows.shape[0]
    side_len = input_rows.shape[1]
    channel_count = input_rows.shape[3]
    grad_count = grad_rows.shape[1]
    grid_grads = grad_rows.reshape(example_count, grad_count, side_len, side_len)
    padded_grads = jnp.pad(grid_grads, ((0, 0), (0, 0), (1, 1), (1, 1)))
    shifted = []
    for row_shift in range(3):
        for col_shift in range(3):
            window = padded_grads[
                :,
                :,
                2 - row_shift : 2 - row_shift + side_len,
                2 - col_shift : 2 - col_shift + side_len,
            ]
            shifted.append(window.reshape(example_count, grad_count, side_len * side_len))
    stacked_grads = jnp.stack(shifted, axis=2).reshape(
        example_count, grad_count * 9, side_len * side_len
    )
    flat_inputs = input_rows.reshape(example_count, side_len * side_len, channel_count)
    product = jnp.einsum(
        "nkp,npq->nkq", stacked_grads, flat_inputs, preferred_element_type=jnp.float32
    )
    return product.astype(jnp.bfloat16).reshape(example_count, -1)


def gram_block(left_rows, right_rows):
    return lax.dot_general(
        left_rows, right_rows, (((1,), (1,)), ((), ())), preferred_element_type=jnp.float32
    )


def local(activations, cotangents, ordering, ridge):
    local_order = ordering[0]
    own_inputs = jnp.take(activations, local_order, axis=0)
    own_grads = jnp.take(cotangents, local_order, axis=0)
    pivot_count = PIV_DEV
    pivot_inputs, pivot_grads = (
        lax.all_gather(own_inputs[:pivot_count], "rows", axis=0, tiled=True),
        lax.all_gather(own_grads[:pivot_count], "rows", axis=0, tiled=True),
    )
    full_own, full_pivot = (
        lax.all_gather(own_inputs, "chan", axis=3, tiled=True),
        lax.all_gather(pivot_inputs, "chan", axis=3, tiled=True),
    )
    own_jac = jacobian_block(own_grads, full_own)
    pivot_jac = jacobian_block(pivot_grads, full_pivot)
    partial_panel = gram_block(own_jac, pivot_jac)
    gram_panel = lax.psum(partial_panel, "chan")
    diag_block = lax.all_gather(gram_panel[:pivot_count], "rows", axis=0, tiled=True)
    system = 0.5 * (diag_block + diag_block.T) + jnp.diag(ridge)
    lower = jnp.linalg.cholesky(system)
    factor_panel = jax.scipy.linalg.solve_triangular(lower, gram_panel.T, lower=True).T
    return (gram_panel, factor_panel)


def solution(mesh):
    row_groups, count = mesh.shape["rows"], mesh.shape["chan"]
    packed = row_groups == 2 and count == 16
    return jax.shard_map(
        functools.partial(local_packed, count) if packed else local,
        mesh=mesh,
        in_specs=(P("rows", None, None, "chan"), P("rows", "chan", None), P("rows", None), P()),
        out_specs=(P("rows", None), P("rows", None)),
        check_vma=False,
    )
```

```python
import functools

import jax
import jax.numpy as jnp
from jax import lax
from jax.experimental import pallas as pl
from jax.experimental.pallas import tpu as pltpu
from jax.sharding import PartitionSpec as P

PIV_DEV = 16

SIDE = 7
PITCH = 8
GROUPS4 = 14
CH = 32
EX = 32
LANES = 128
F32 = jnp.float32
BF16 = jnp.bfloat16


def fetch(sources, targets, sems):
    copies = [pltpu.make_async_copy(a, b, sems.at[i]) for i, (a, b) in enumerate(zip(sources, targets))]
    for copy in copies:
        copy.start()
    return copies


def prep_kernel(order_hbm, x_hbm, g_hbm, xo_ref, go_ref, order_ref, x_ref, g_ref, sems, gs, gt, gout):
    for copy in fetch((order_hbm, x_hbm, g_hbm), (order_ref, x_ref, g_ref), sems):
        copy.wait()
    row_id = lax.broadcasted_iota(jnp.int32, (EX, EX), 0)
    col_id = lax.broadcasted_iota(jnp.int32, (EX, EX), 1)
    onehot = jnp.zeros((EX, EX), F32)
    for k in range(EX):
        example = order_ref[0, k]
        onehot = jnp.where((row_id == k) & (col_id == example), 1.0, onehot)
        gs[k * CH:(k + 1) * CH, 0:SIDE * SIDE] = g_ref[example].astype(F32)
    onehot = onehot.astype(BF16)
    zero_block = jnp.zeros((EX, CH), BF16)
    for group in range(GROUPS4):
        pieces = []
        for j in range(4):
            py, px = group // 2, (group % 2) * 4 + j
            pieces.append(x_ref[py * SIDE + px] if px < SIDE else zero_block)
        packed = jnp.concatenate(pieces, axis=1)
        xo_ref[group] = jnp.dot(onehot, packed, preferred_element_type=F32).astype(BF16)
    block_id = lax.broadcasted_iota(jnp.int32, (GROUPS4, LANES), 1) // CH
    for quad in range(EX // 4):
        flipped = jnp.transpose(gs[quad * LANES:(quad + 1) * LANES, :])
        for py in range(SIDE):
            gt[py * PITCH:py * PITCH + SIDE, :] = flipped[py * SIDE:(py + 1) * SIDE, :]
            gt[py * PITCH + SIDE:(py + 1) * PITCH, :] = jnp.zeros((1, LANES), F32)
        parts = [gt[pl.ds(j, GROUPS4, stride=4), :] for j in range(4)]
        for e in range(4):
            merged = jnp.zeros((GROUPS4, LANES), F32)
            for j in range(4):
                shift = (CH * (j - e)) % LANES
                moved = pltpu.roll(parts[j], shift, 1) if shift else parts[j]
                merged = jnp.where(block_id == j, moved, merged)
            gout[pl.ds(quad * 4 + e, GROUPS4, stride=EX), :] = merged
    for group in range(GROUPS4):
        go_ref[group] = gout[group * EX:(group + 1) * EX, :].astype(BF16)


def prep(order, x, g):
    full = jax.ShapeDtypeStruct((GROUPS4, EX, LANES), BF16)
    vmem = pl.BlockSpec(memory_space=pltpu.VMEM)
    return pl.pallas_call(
        prep_kernel,
        out_shape=(full, full),
        in_specs=[pl.BlockSpec(memory_space=pl.ANY)] * 3,
        out_specs=(vmem,) * 2,
        scratch_shapes=[
            pltpu.SMEM(order.shape, order.dtype),
            pltpu.VMEM(x.shape, x.dtype),
            pltpu.VMEM(g.shape, g.dtype),
            pltpu.SemaphoreType.DMA((3,)),
            pltpu.VMEM((EX * CH, LANES), F32),
            pltpu.VMEM((SIDE * PITCH, LANES), F32),
            pltpu.VMEM((GROUPS4 * EX, LANES), F32),
        ],
        compiler_params=pltpu.CompilerParams(vmem_limit_bytes=56 << 20),
        name="prep",
    )(order, x, g)


SPOTS = SIDE * SIDE
ROWB = SIDE * EX
COLB = PITCH * PIV_DEV


def cost(flops, moved):
    return pl.CostEstimate(flops=flops, bytes_accessed=moved, transcendentals=0)


def unpack_kernel(*refs):
    all_ref, piv_ref, packed, sems = refs[4:]
    copies = fetch(refs[:4], [packed.at[i] for i in range(4)], sems)
    row = lax.broadcasted_iota(jnp.int32, (4 * LANES, 4 * LANES), 0)
    col = lax.broadcasted_iota(jnp.int32, (4 * LANES, 4 * LANES), 1)
    target = (row // CH) % 4 * LANES + row // LANES * CH + row % CH
    move = jnp.where(col == target, 1.0, 0.0).astype(BF16)
    for copy in copies:
        copy.wait()
    flat = jnp.concatenate([packed[i].reshape(GROUPS4 * EX, LANES) for i in range(4)], axis=1)
    moved = jnp.dot(flat, move, preferred_element_type=F32).astype(BF16)
    for group in range(GROUPS4):
        for j in range(4):
            py, px = group // 2, (group % 2) * 4 + j
            if px == SIDE:
                continue
            spot = moved[group * EX:(group + 1) * EX, j * LANES:(j + 1) * LANES]
            all_ref[py * SIDE + px] = spot
            piv_ref[py * SIDE + px] = spot[:PIV_DEV]


def unpack(arrays, name):
    vmem = pl.BlockSpec(memory_space=pltpu.VMEM)
    return pl.pallas_call(
        unpack_kernel,
        out_shape=(
            jax.ShapeDtypeStruct((SPOTS, EX, LANES), BF16),
            jax.ShapeDtypeStruct((SPOTS, PIV_DEV, LANES), BF16),
        ),
        in_specs=[pl.BlockSpec(memory_space=pl.ANY)] * 4,
        out_specs=(vmem,) * 2,
        scratch_shapes=[pltpu.VMEM((4, GROUPS4, EX, LANES), BF16), pltpu.SemaphoreType.DMA((4,))],
        compiler_params=pltpu.CompilerParams(vmem_limit_bytes=56 << 20),
        cost_estimate=cost(0, 1 << 20),
        name=name,
    )(*arrays)


def panel_terms(x, g, xp, gp, lx, rx, rg, t):
    for py in range(SIDE):
        for px in range(PITCH):
            row, col = (py * SIDE + px) * EX, (py * PITCH + px) * PIV_DEV
            for d in range(3):
                from_x = px + d - 1
                inside = 0 <= from_x < SIDE and px < SIDE
                lanes = slice(d * LANES, (d + 1) * LANES)
                spot = py * SIDE + from_x
                rx[col:col + PIV_DEV, lanes] = xp[spot] if inside else jnp.zeros((PIV_DEV, LANES), BF16)
                if px < SIDE:
                    lx[row:row + EX, lanes] = x[spot] if inside else jnp.zeros((EX, LANES), BF16)
            rg[col:col + PIV_DEV, :] = gp[py * SIDE + px] if px < SIDE else jnp.zeros((PIV_DEV, LANES), BF16)

    contract = (((1,), (1,)), ((), ()))
    spans = [(qy, min(qy + 2, SIDE)) for qy in range(0, SIDE, 2)]
    for start, stop in spans:
        right = rx[start * COLB:stop * COLB, :]
        for py in range(SIDE):
            left = lx[py * ROWB:(py + 1) * ROWB, :]
            t[py, :, start * COLB:stop * COLB] = lax.dot_general(left, right, contract, preferred_element_type=F32)
    acc = jnp.zeros((EX, COLB), F32)
    for start, stop in spans:
        right = rg[start * COLB:stop * COLB, :]
        for py in range(SIDE):
            left = g[py * SIDE:(py + 1) * SIDE].reshape(ROWB, LANES)
            gg = lax.dot_general(left, right, contract, preferred_element_type=F32)
            for qy in range(start, stop):
                for px in range(SIDE):
                    rows = slice(px * EX, (px + 1) * EX)
                    total = t[py, rows, qy * COLB:(qy + 1) * COLB]
                    if py > 0 and qy > 0:
                        total = total + t[py - 1, rows, (qy - 1) * COLB:qy * COLB]
                    if py < SIDE - 1 and qy < SIDE - 1:
                        total = total + t[py + 1, rows, (qy + 1) * COLB:(qy + 2) * COLB]
                    acc = acc + gg[rows, (qy - start) * COLB:(qy - start + 1) * COLB] * total
    acc = acc + pltpu.roll(acc, 64, 1)
    acc = acc + pltpu.roll(acc, 32, 1)
    return acc + pltpu.roll(acc, 16, 1)


def own_kernel(*refs):
    out_ref, local, sems, work = refs[4], refs[5:9], refs[9], refs[10:]
    for copy in fetch(refs[:4], local, sems):
        copy.wait()
    out_ref[...] = panel_terms(*local, *work)


def cross_kernel(*refs):
    own_ref, out_ref, local, sems, work = refs[4], refs[5], refs[6:10], refs[10], refs[11:]
    for copy in fetch(refs[:4], local, sems):
        copy.wait()
    across = panel_terms(*local, *work)
    lane = lax.broadcasted_iota(jnp.int32, (8, LANES), 1)
    is_own = (lane // PIV_DEV) % 2 == lax.axis_index("rows")
    packed = jnp.zeros((8, LANES), F32)
    for j in range(4):
        rows = slice(8 * j, 8 * j + 8)
        packed = jnp.where(lane // EX == j, jnp.where(is_own, own_ref[rows, :], across[rows]), packed)
    out_ref[...] = packed


def terms(kernel, arrays, shape, name):
    vmem = pl.BlockSpec(memory_space=pltpu.VMEM)
    rows, cols = SIDE * ROWB, SIDE * COLB
    return pl.pallas_call(
        kernel,
        out_shape=jax.ShapeDtypeStruct(shape, F32),
        in_specs=[pl.BlockSpec(memory_space=pl.ANY)] * 4 + [vmem] * (len(arrays) - 4),
        out_specs=vmem,
        scratch_shapes=[pltpu.VMEM(array.shape, array.dtype) for array in arrays[:4]] + [
            pltpu.SemaphoreType.DMA((4,)),
            pltpu.VMEM((rows, 3 * LANES), BF16),
            pltpu.VMEM((cols, 3 * LANES), BF16),
            pltpu.VMEM((cols, LANES), BF16),
            pltpu.VMEM((SIDE, ROWB, cols), F32),
        ],
        compiler_params=pltpu.CompilerParams(vmem_limit_bytes=56 << 20),
        cost_estimate=cost(2 * rows * cols * 4 * LANES, 8 << 20),
        name=name,
    )(*arrays)


def rows_of(packed, count):
    return jnp.concatenate(
        [packed[:, EX * j:EX * (j + 1)] for j in range(count)], axis=0
    )


def tree_sum(values):
    while len(values) > 1:
        values = [a + b for a, b in zip(values[0::2], values[1::2])]
    return values[0]


def final_kernel(terms_ref, ridge_ref, gram_ref, factor_ref):
    count = terms_ref.shape[0] // 2
    sums = [tree_sum([terms_ref[g * count + i] for i in range(count)]) for g in range(2)]
    first = lax.axis_index("rows") == 0
    panel = rows_of(jnp.where(first, sums[0], sums[1]), 4)
    gram_ref[...] = panel
    diag = jnp.concatenate([rows_of(total, 2) for total in sums], axis=0)
    row_id = lax.broadcasted_iota(jnp.int32, (EX, EX), 0)
    col_id = lax.broadcasted_iota(jnp.int32, (EX, EX), 1)
    ridge = jnp.where(row_id == col_id, jnp.broadcast_to(ridge_ref[...], (EX, EX)), 0.0)
    system = 0.5 * (diag + jnp.transpose(diag)) + ridge
    factor = jnp.zeros((EX, EX), F32)
    step = 4
    for j in range(0, EX, step):
        sys_cols = [jnp.broadcast_to(system[:, j + k:j + k + 1], (EX, EX)) for k in range(step)]
        pan_cols = [jnp.broadcast_to(panel[:, j + k:j + k + 1], (EX, EX)) for k in range(step)]
        sys_rows = [system[j + k:j + k + 1, :] for k in range(step)]
        for k in range(step):
            scale = lax.rsqrt(sys_cols[k][j + k:j + k + 1, :])
            sys_cols[k], pan_cols[k], sys_rows[k] = sys_cols[k] * scale, pan_cols[k] * scale, sys_rows[k] * scale
            factor = jnp.where(col_id == j + k, pan_cols[k], factor)
            for m in range(k + 1, step):
                entry = sys_cols[k][j + m:j + m + 1, :]
                sys_cols[m] = sys_cols[m] - sys_cols[k] * entry
                pan_cols[m] = pan_cols[m] - pan_cols[k] * entry
                sys_rows[m] = sys_rows[m] - sys_rows[k] * entry
        if j + step < EX:
            for k in range(step):
                system = system - sys_cols[k] * sys_rows[k]
                panel = panel - pan_cols[k] * sys_rows[k]
    factor_ref[...] = factor


def final(terms, ridge):
    vmem = pl.BlockSpec(memory_space=pltpu.VMEM)
    out = jax.ShapeDtypeStruct((EX, EX), F32)
    return pl.pallas_call(
        final_kernel,
        out_shape=(out, out),
        in_specs=[vmem] * 2,
        out_specs=(vmem, vmem),
        name="solve",
    )(terms, ridge.reshape(1, EX))


def exchange(value, count, flip):
    return lax.ppermute(value, "chan", [(i, i ^ flip) for i in range(count)])


def exchange_across(value, count):
    pairs = [(g * count + i, (1 - g) * count + i) for g in range(2) for i in range(count)]
    return lax.ppermute(value, ("rows", "chan"), pairs)


def local_packed(count, activations, cotangents, ordering, ridge):
    near, far = (1, 2, 3), (4, 8, 12)
    x = jnp.transpose(activations, (1, 2, 0, 3)).reshape(SIDE * SIDE, EX, CH)
    xo, go = prep(ordering, x, cotangents)
    own_g = [go] + [exchange(go, count, f) for f in near]
    own_x = [xo] + [exchange(xo, count, f) for f in far]
    x_all, x_piv = unpack(own_x, "unpack_x")
    x_cross = exchange_across(x_piv, count)
    g_all, g_piv = unpack(own_g, "unpack_g")
    g_cross = exchange_across(g_piv, count)
    own_term = terms(own_kernel, (x_all, g_all, x_piv, g_piv), (EX, LANES), "terms_own")
    term = terms(cross_kernel, (x_all, g_all, x_cross, g_cross, own_term), (8, LANES), "terms_cross")
    quads = [[4 * i + k for k in range(4)] for i in range(count // 4)]
    parts = lax.all_to_all(jnp.broadcast_to(term, (4, 8, LANES)), "chan", 0, 0, axis_index_groups=quads)
    part = (parts[0] + parts[1]) + (parts[2] + parts[3])
    eights = [[4 * i + k for i in range(2 * count // 4)] for k in range(4)]
    gathered = lax.all_to_all(
        jnp.broadcast_to(part, (2 * count // 4, 8, LANES)), ("rows", "chan"), 0, 0, axis_index_groups=eights
    )
    return final(gathered, ridge)


def jacobian_block(grad_rows, input_rows):
    example_count = input_rows.shape[0]
    side_len = input_rows.shape[1]
    channel_count = input_rows.shape[3]
    grad_count = grad_rows.shape[1]
    grid_grads = grad_rows.reshape(example_count, grad_count, side_len, side_len)
    padded_grads = jnp.pad(grid_grads, ((0, 0), (0, 0), (1, 1), (1, 1)))
    shifted = []
    for row_shift in range(3):
        for col_shift in range(3):
            window = padded_grads[
                :,
                :,
                2 - row_shift : 2 - row_shift + side_len,
                2 - col_shift : 2 - col_shift + side_len,
            ]
            shifted.append(window.reshape(example_count, grad_count, side_len * side_len))
    stacked_grads = jnp.stack(shifted, axis=2).reshape(
        example_count, grad_count * 9, side_len * side_len
    )
    flat_inputs = input_rows.reshape(example_count, side_len * side_len, channel_count)
    product = jnp.einsum(
        "nkp,npq->nkq", stacked_grads, flat_inputs, preferred_element_type=jnp.float32
    )
    return product.astype(jnp.bfloat16).reshape(example_count, -1)


def gram_block(left_rows, right_rows):
    return lax.dot_general(
        left_rows, right_rows, (((1,), (1,)), ((), ())), preferred_element_type=jnp.float32
    )


def local(activations, cotangents, ordering, ridge):
    local_order = ordering[0]
    own_inputs = jnp.take(activations, local_order, axis=0)
    own_grads = jnp.take(cotangents, local_order, axis=0)
    pivot_count = PIV_DEV
    pivot_inputs, pivot_grads = (
        lax.all_gather(own_inputs[:pivot_count], "rows", axis=0, tiled=True),
        lax.all_gather(own_grads[:pivot_count], "rows", axis=0, tiled=True),
    )
    full_own, full_pivot = (
        lax.all_gather(own_inputs, "chan", axis=3, tiled=True),
        lax.all_gather(pivot_inputs, "chan", axis=3, tiled=True),
    )
    own_jac = jacobian_block(own_grads, full_own)
    pivot_jac = jacobian_block(pivot_grads, full_pivot)
    partial_panel = gram_block(own_jac, pivot_jac)
    gram_panel = lax.psum(partial_panel, "chan")
    diag_block = lax.all_gather(gram_panel[:pivot_count], "rows", axis=0, tiled=True)
    system = 0.5 * (diag_block + diag_block.T) + jnp.diag(ridge)
    lower = jnp.linalg.cholesky(system)
    factor_panel = jax.scipy.linalg.solve_triangular(lower, gram_panel.T, lower=True).T
    return (gram_panel, factor_panel)


def solution(mesh):
    row_groups, count = mesh.shape["rows"], mesh.shape["chan"]
    packed = row_groups == 2 and count == 16
    return jax.shard_map(
        functools.partial(local_packed, count) if packed else local,
        mesh=mesh,
        in_specs=(P("rows", None, None, "chan"), P("rows", "chan", None), P("rows", None), P()),
        out_specs=(P("rows", None), P("rows", None)),
        check_vma=False,
    )
```

```python
import functools

import jax
import jax.numpy as jnp
from jax import lax
from jax.experimental import pallas as pl
from jax.experimental.pallas import tpu as pltpu
from jax.sharding import PartitionSpec as P

PIV_DEV = 16

SIDE = 7
PITCH = 8
GROUPS4 = 14
CH = 32
EX = 32
LANES = 128
F32 = jnp.float32
BF16 = jnp.bfloat16


def fetch(sources, targets, sems):
    copies = [pltpu.make_async_copy(a, b, sems.at[i]) for i, (a, b) in enumerate(zip(sources, targets))]
    for copy in copies:
        copy.start()
    return copies


def prep_kernel(order_hbm, x_hbm, g_hbm, xo_ref, go_ref, order_ref, x_ref, g_ref, sems, gs, gt, gout):
    for copy in fetch((order_hbm, x_hbm, g_hbm), (order_ref, x_ref, g_ref), sems):
        copy.wait()
    row_id = lax.broadcasted_iota(jnp.int32, (EX, EX), 0)
    col_id = lax.broadcasted_iota(jnp.int32, (EX, EX), 1)
    onehot = jnp.zeros((EX, EX), F32)
    for k in range(EX):
        example = order_ref[0, k]
        onehot = jnp.where((row_id == k) & (col_id == example), 1.0, onehot)
        gs[k * CH:(k + 1) * CH, 0:SIDE * SIDE] = g_ref[example].astype(F32)
    onehot = onehot.astype(BF16)
    zero_block = jnp.zeros((EX, CH), BF16)
    for group in range(GROUPS4):
        pieces = []
        for j in range(4):
            py, px = group // 2, (group % 2) * 4 + j
            pieces.append(x_ref[py * SIDE + px] if px < SIDE else zero_block)
        packed = jnp.concatenate(pieces, axis=1)
        xo_ref[group] = jnp.dot(onehot, packed, preferred_element_type=F32).astype(BF16)
    block_id = lax.broadcasted_iota(jnp.int32, (GROUPS4, LANES), 1) // CH
    for quad in range(EX // 4):
        flipped = jnp.transpose(gs[quad * LANES:(quad + 1) * LANES, :])
        for py in range(SIDE):
            gt[py * PITCH:py * PITCH + SIDE, :] = flipped[py * SIDE:(py + 1) * SIDE, :]
            gt[py * PITCH + SIDE:(py + 1) * PITCH, :] = jnp.zeros((1, LANES), F32)
        parts = [gt[pl.ds(j, GROUPS4, stride=4), :] for j in range(4)]
        for e in range(4):
            merged = jnp.zeros((GROUPS4, LANES), F32)
            for j in range(4):
                shift = (CH * (j - e)) % LANES
                moved = pltpu.roll(parts[j], shift, 1) if shift else parts[j]
                merged = jnp.where(block_id == j, moved, merged)
            gout[pl.ds(quad * 4 + e, GROUPS4, stride=EX), :] = merged
    for group in range(GROUPS4):
        go_ref[group] = gout[group * EX:(group + 1) * EX, :].astype(BF16)


def prep(order, x, g):
    full = jax.ShapeDtypeStruct((GROUPS4, EX, LANES), BF16)
    vmem = pl.BlockSpec(memory_space=pltpu.VMEM)
    return pl.pallas_call(
        prep_kernel,
        out_shape=(full, full),
        in_specs=[pl.BlockSpec(memory_space=pl.ANY)] * 3,
        out_specs=(vmem,) * 2,
        scratch_shapes=[
            pltpu.SMEM(order.shape, order.dtype),
            pltpu.VMEM(x.shape, x.dtype),
            pltpu.VMEM(g.shape, g.dtype),
            pltpu.SemaphoreType.DMA((3,)),
            pltpu.VMEM((EX * CH, LANES), F32),
            pltpu.VMEM((SIDE * PITCH, LANES), F32),
            pltpu.VMEM((GROUPS4 * EX, LANES), F32),
        ],
        compiler_params=pltpu.CompilerParams(vmem_limit_bytes=56 << 20),
        name="prep",
    )(order, x, g)


SPOTS = SIDE * SIDE
ROWB = SIDE * EX
COLB = PITCH * PIV_DEV


def cost(flops, moved):
    return pl.CostEstimate(flops=flops, bytes_accessed=moved, transcendentals=0)


def unpack_kernel(*refs):
    packed, all_ref, piv_ref = refs[:4], refs[4], refs[5]
    row = lax.broadcasted_iota(jnp.int32, (4 * LANES, 4 * LANES), 0)
    col = lax.broadcasted_iota(jnp.int32, (4 * LANES, 4 * LANES), 1)
    target = (row // CH) % 4 * LANES + row // LANES * CH + row % CH
    move = jnp.where(col == target, 1.0, 0.0).astype(BF16)
    flat = jnp.concatenate([packed[i][...].reshape(GROUPS4 * EX, LANES) for i in range(4)], axis=1)
    moved = jnp.dot(flat, move, preferred_element_type=F32).astype(BF16)
    for group in range(GROUPS4):
        for j in range(4):
            py, px = group // 2, (group % 2) * 4 + j
            if px == SIDE:
                continue
            spot = moved[group * EX:(group + 1) * EX, j * LANES:(j + 1) * LANES]
            all_ref[py * SIDE + px] = spot
            piv_ref[py * SIDE + px] = spot[:PIV_DEV]


def unpack(arrays, name):
    vmem = pl.BlockSpec(memory_space=pltpu.VMEM)
    return pl.pallas_call(
        unpack_kernel,
        out_shape=(
            jax.ShapeDtypeStruct((SPOTS, EX, LANES), BF16),
            jax.ShapeDtypeStruct((SPOTS, PIV_DEV, LANES), BF16),
        ),
        in_specs=[vmem] * len(arrays),
        out_specs=(vmem,) * 2,
        compiler_params=pltpu.CompilerParams(vmem_limit_bytes=8 << 20),
        cost_estimate=cost(0, 1 << 20),
        name=name,
    )(*arrays)


def panel_terms(x, g, xp, gp, lx, rx, rg, t):
    for py in range(SIDE):
        for px in range(PITCH):
            row, col = (py * SIDE + px) * EX, (py * PITCH + px) * PIV_DEV
            for d in range(3):
                from_x = px + d - 1
                inside = 0 <= from_x < SIDE and px < SIDE
                lanes = slice(d * LANES, (d + 1) * LANES)
                spot = py * SIDE + from_x
                rx[col:col + PIV_DEV, lanes] = xp[spot] if inside else jnp.zeros((PIV_DEV, LANES), BF16)
                if px < SIDE:
                    lx[row:row + EX, lanes] = x[spot] if inside else jnp.zeros((EX, LANES), BF16)
            rg[col:col + PIV_DEV, :] = gp[py * SIDE + px] if px < SIDE else jnp.zeros((PIV_DEV, LANES), BF16)

    contract = (((1,), (1,)), ((), ()))
    spans = [(qy, min(qy + 2, SIDE)) for qy in range(0, SIDE, 2)]
    for start, stop in spans:
        right = rx[start * COLB:stop * COLB, :]
        for py in range(SIDE):
            left = lx[py * ROWB:(py + 1) * ROWB, :]
            t[py, :, start * COLB:stop * COLB] = lax.dot_general(left, right, contract, preferred_element_type=F32)
    acc = jnp.zeros((EX, COLB), F32)
    for start, stop in spans:
        right = rg[start * COLB:stop * COLB, :]
        for py in range(SIDE):
            left = g[py * SIDE:(py + 1) * SIDE].reshape(ROWB, LANES)
            gg = lax.dot_general(left, right, contract, preferred_element_type=F32)
            for qy in range(start, stop):
                for px in range(SIDE):
                    rows = slice(px * EX, (px + 1) * EX)
                    total = t[py, rows, qy * COLB:(qy + 1) * COLB]
                    if py > 0 and qy > 0:
                        total = total + t[py - 1, rows, (qy - 1) * COLB:qy * COLB]
                    if py < SIDE - 1 and qy < SIDE - 1:
                        total = total + t[py + 1, rows, (qy + 1) * COLB:(qy + 2) * COLB]
                    acc = acc + gg[rows, (qy - start) * COLB:(qy - start + 1) * COLB] * total
    acc = acc + pltpu.roll(acc, 64, 1)
    acc = acc + pltpu.roll(acc, 32, 1)
    return acc + pltpu.roll(acc, 16, 1)


def own_kernel(x, g, xp, gp, out_ref, *work):
    out_ref[...] = panel_terms(x, g, xp, gp, *work)


def cross_kernel(x, g, xp, gp, own_ref, out_ref, *work):
    across = panel_terms(x, g, xp, gp, *work)
    lane = lax.broadcasted_iota(jnp.int32, (8, LANES), 1)
    is_own = (lane // PIV_DEV) % 2 == lax.axis_index("rows")
    packed = jnp.zeros((8, LANES), F32)
    for j in range(4):
        rows = slice(8 * j, 8 * j + 8)
        packed = jnp.where(lane // EX == j, jnp.where(is_own, own_ref[rows, :], across[rows]), packed)
    out_ref[...] = packed


def terms(kernel, arrays, shape, name):
    vmem = pl.BlockSpec(memory_space=pltpu.VMEM)
    rows, cols = SIDE * ROWB, SIDE * COLB
    return pl.pallas_call(
        kernel,
        out_shape=jax.ShapeDtypeStruct(shape, F32),
        in_specs=[vmem] * len(arrays),
        out_specs=vmem,
        scratch_shapes=[
            pltpu.VMEM((rows, 3 * LANES), BF16),
            pltpu.VMEM((cols, 3 * LANES), BF16),
            pltpu.VMEM((cols, LANES), BF16),
            pltpu.VMEM((SIDE, ROWB, cols), F32),
        ],
        compiler_params=pltpu.CompilerParams(vmem_limit_bytes=24 << 20),
        cost_estimate=cost(2 * rows * cols * 4 * LANES, 8 << 20),
        name=name,
    )(*arrays)


def rows_of(packed, count):
    return jnp.concatenate(
        [packed[:, EX * j:EX * (j + 1)] for j in range(count)], axis=0
    )


def final_kernel(own_ref, other_ref, ridge_ref, gram_ref, factor_ref):
    first = lax.axis_index("rows") == 0
    panel = rows_of(own_ref[...], 4)
    gram_ref[...] = panel
    mine, cross = panel[:PIV_DEV], rows_of(other_ref[...], 2)
    diag = jnp.concatenate([jnp.where(first, mine, cross), jnp.where(first, cross, mine)], axis=0)
    row_id = lax.broadcasted_iota(jnp.int32, (EX, EX), 0)
    col_id = lax.broadcasted_iota(jnp.int32, (EX, EX), 1)
    ridge = jnp.where(row_id == col_id, jnp.broadcast_to(ridge_ref[...], (EX, EX)), 0.0)
    system = 0.5 * (diag + jnp.transpose(diag)) + ridge
    factor = jnp.zeros((EX, EX), F32)
    step = 4
    for j in range(0, EX, step):
        sys_cols = [jnp.broadcast_to(system[:, j + k:j + k + 1], (EX, EX)) for k in range(step)]
        pan_cols = [jnp.broadcast_to(panel[:, j + k:j + k + 1], (EX, EX)) for k in range(step)]
        sys_rows = [system[j + k:j + k + 1, :] for k in range(step)]
        for k in range(step):
            scale = lax.rsqrt(sys_cols[k][j + k:j + k + 1, :])
            sys_cols[k], pan_cols[k], sys_rows[k] = sys_cols[k] * scale, pan_cols[k] * scale, sys_rows[k] * scale
            factor = jnp.where(col_id == j + k, pan_cols[k], factor)
            for m in range(k + 1, step):
                entry = sys_cols[k][j + m:j + m + 1, :]
                sys_cols[m] = sys_cols[m] - sys_cols[k] * entry
                pan_cols[m] = pan_cols[m] - pan_cols[k] * entry
                sys_rows[m] = sys_rows[m] - sys_rows[k] * entry
        if j + step < EX:
            for k in range(step):
                system = system - sys_cols[k] * sys_rows[k]
                panel = panel - pan_cols[k] * sys_rows[k]
    factor_ref[...] = factor


def final(own, other, ridge):
    vmem = pl.BlockSpec(memory_space=pltpu.VMEM)
    out = jax.ShapeDtypeStruct((EX, EX), F32)
    return pl.pallas_call(
        final_kernel,
        out_shape=(out, out),
        in_specs=[vmem] * 3,
        out_specs=(vmem, vmem),
        compiler_params=pltpu.CompilerParams(vmem_limit_bytes=8 << 20),
        name="solve",
    )(own, other, ridge.reshape(1, EX))


def exchange(value, count, flip):
    return lax.ppermute(value, "chan", [(i, i ^ flip) for i in range(count)])


def exchange_across(value, count):
    pairs = [(g * count + i, (1 - g) * count + i) for g in range(2) for i in range(count)]
    return lax.ppermute(value, ("rows", "chan"), pairs)


def local_packed(count, activations, cotangents, ordering, ridge):
    near, far = (1, 2, 3), (4, 8, 12)
    x = jnp.transpose(activations, (1, 2, 0, 3)).reshape(SIDE * SIDE, EX, CH)
    xo, go = prep(ordering, x, cotangents)
    own_g = [go] + [exchange(go, count, f) for f in near]
    own_x = [xo] + [exchange(xo, count, f) for f in far]
    x_all, x_piv = unpack(own_x, "unpack_x")
    x_cross = exchange_across(x_piv, count)
    g_all, g_piv = unpack(own_g, "unpack_g")
    g_cross = exchange_across(g_piv, count)
    own_term = terms(own_kernel, (x_all, g_all, x_piv, g_piv), (EX, LANES), "terms_own")
    term = terms(cross_kernel, (x_all, g_all, x_cross, g_cross, own_term), (8, LANES), "terms_cross")
    for flip in (1, 2, 4, 8):
        term = term + exchange(term, count, flip)
    return final(term, exchange_across(term, count), ridge)


def jacobian_block(grad_rows, input_rows):
    example_count = input_rows.shape[0]
    side_len = input_rows.shape[1]
    channel_count = input_rows.shape[3]
    grad_count = grad_rows.shape[1]
    grid_grads = grad_rows.reshape(example_count, grad_count, side_len, side_len)
    padded_grads = jnp.pad(grid_grads, ((0, 0), (0, 0), (1, 1), (1, 1)))
    shifted = []
    for row_shift in range(3):
        for col_shift in range(3):
            window = padded_grads[
                :,
                :,
                2 - row_shift : 2 - row_shift + side_len,
                2 - col_shift : 2 - col_shift + side_len,
            ]
            shifted.append(window.reshape(example_count, grad_count, side_len * side_len))
    stacked_grads = jnp.stack(shifted, axis=2).reshape(
        example_count, grad_count * 9, side_len * side_len
    )
    flat_inputs = input_rows.reshape(example_count, side_len * side_len, channel_count)
    product = jnp.einsum(
        "nkp,npq->nkq", stacked_grads, flat_inputs, preferred_element_type=jnp.float32
    )
    return product.astype(jnp.bfloat16).reshape(example_count, -1)


def gram_block(left_rows, right_rows):
    return lax.dot_general(
        left_rows, right_rows, (((1,), (1,)), ((), ())), preferred_element_type=jnp.float32
    )


def local(activations, cotangents, ordering, ridge):
    local_order = ordering[0]
    own_inputs = jnp.take(activations, local_order, axis=0)
    own_grads = jnp.take(cotangents, local_order, axis=0)
    pivot_count = PIV_DEV
    pivot_inputs, pivot_grads = (
        lax.all_gather(own_inputs[:pivot_count], "rows", axis=0, tiled=True),
        lax.all_gather(own_grads[:pivot_count], "rows", axis=0, tiled=True),
    )
    full_own, full_pivot = (
        lax.all_gather(own_inputs, "chan", axis=3, tiled=True),
        lax.all_gather(pivot_inputs, "chan", axis=3, tiled=True),
    )
    own_jac = jacobian_block(own_grads, full_own)
    pivot_jac = jacobian_block(pivot_grads, full_pivot)
    partial_panel = gram_block(own_jac, pivot_jac)
    gram_panel = lax.psum(partial_panel, "chan")
    diag_block = lax.all_gather(gram_panel[:pivot_count], "rows", axis=0, tiled=True)
    system = 0.5 * (diag_block + diag_block.T) + jnp.diag(ridge)
    lower = jnp.linalg.cholesky(system)
    factor_panel = jax.scipy.linalg.solve_triangular(lower, gram_panel.T, lower=True).T
    return (gram_panel, factor_panel)


def solution(mesh):
    row_groups, count = mesh.shape["rows"], mesh.shape["chan"]
    packed = row_groups == 2 and count == 16
    return jax.shard_map(
        functools.partial(local_packed, count) if packed else local,
        mesh=mesh,
        in_specs=(P("rows", None, None, "chan"), P("rows", "chan", None), P("rows", None), P()),
        out_specs=(P("rows", None), P("rows", None)),
        check_vma=False,
    )
```

```python
import functools

import jax
import jax.numpy as jnp
from jax import lax
from jax.experimental import pallas as pl
from jax.experimental.pallas import tpu as pltpu
from jax.sharding import PartitionSpec as P

PIV_DEV = 16

SIDE = 7
PITCH = 8
GROUPS4 = 14
CH = 32
EX = 32
LANES = 128
F32 = jnp.float32
BF16 = jnp.bfloat16


def fetch(sources, targets, sems):
    copies = [pltpu.make_async_copy(a, b, sems.at[i]) for i, (a, b) in enumerate(zip(sources, targets))]
    for copy in copies:
        copy.start()
    return copies


def prep_kernel(order_hbm, x_hbm, g_hbm, xo_ref, go_ref, gp_ref, order_ref, x_ref, g_ref, sems, gs, gt, gout):
    for copy in fetch((order_hbm, x_hbm, g_hbm), (order_ref, x_ref, g_ref), sems):
        copy.wait()
    row_id = lax.broadcasted_iota(jnp.int32, (EX, EX), 0)
    col_id = lax.broadcasted_iota(jnp.int32, (EX, EX), 1)
    onehot = jnp.zeros((EX, EX), F32)
    for k in range(EX):
        example = order_ref[0, k]
        onehot = jnp.where((row_id == k) & (col_id == example), 1.0, onehot)
        gs[k * CH:(k + 1) * CH, 0:SIDE * SIDE] = g_ref[example].astype(F32)
    onehot = onehot.astype(BF16)
    zero_block = jnp.zeros((EX, CH), BF16)
    for group in range(GROUPS4):
        pieces = []
        for j in range(4):
            py, px = group // 2, (group % 2) * 4 + j
            pieces.append(x_ref[py * SIDE + px] if px < SIDE else zero_block)
        packed = jnp.concatenate(pieces, axis=1)
        xo_ref[group] = jnp.dot(onehot, packed, preferred_element_type=F32).astype(BF16)
    block_id = lax.broadcasted_iota(jnp.int32, (GROUPS4, LANES), 1) // CH
    for quad in range(EX // 4):
        flipped = jnp.transpose(gs[quad * LANES:(quad + 1) * LANES, :])
        for py in range(SIDE):
            gt[py * PITCH:py * PITCH + SIDE, :] = flipped[py * SIDE:(py + 1) * SIDE, :]
            gt[py * PITCH + SIDE:(py + 1) * PITCH, :] = jnp.zeros((1, LANES), F32)
        parts = [gt[pl.ds(j, GROUPS4, stride=4), :] for j in range(4)]
        for e in range(4):
            merged = jnp.zeros((GROUPS4, LANES), F32)
            for j in range(4):
                shift = (CH * (j - e)) % LANES
                moved = pltpu.roll(parts[j], shift, 1) if shift else parts[j]
                merged = jnp.where(block_id == j, moved, merged)
            gout[pl.ds(quad * 4 + e, GROUPS4, stride=EX), :] = merged
    for group in range(GROUPS4):
        ordered = gout[group * EX:(group + 1) * EX, :].astype(BF16)
        go_ref[group] = ordered
        gp_ref[group] = ordered[:PIV_DEV]


def prep(order, x, g):
    full = jax.ShapeDtypeStruct((GROUPS4, EX, LANES), BF16)
    vmem = pl.BlockSpec(memory_space=pltpu.VMEM)
    return pl.pallas_call(
        prep_kernel,
        out_shape=(full, full, jax.ShapeDtypeStruct((GROUPS4, PIV_DEV, LANES), BF16)),
        in_specs=[pl.BlockSpec(memory_space=pl.ANY)] * 3,
        out_specs=(vmem,) * 3,
        scratch_shapes=[
            pltpu.SMEM(order.shape, order.dtype),
            pltpu.VMEM(x.shape, x.dtype),
            pltpu.VMEM(g.shape, g.dtype),
            pltpu.SemaphoreType.DMA((3,)),
            pltpu.VMEM((EX * CH, LANES), F32),
            pltpu.VMEM((SIDE * PITCH, LANES), F32),
            pltpu.VMEM((GROUPS4 * EX, LANES), F32),
        ],
        compiler_params=pltpu.CompilerParams(vmem_limit_bytes=56 << 20),
        name="prep",
    )(order, x, g)


SPOTS = SIDE * SIDE
ROWB = SIDE * EX
COLB = PITCH * PIV_DEV


def cost(flops, moved):
    return pl.CostEstimate(flops=flops, bytes_accessed=moved, transcendentals=0)


def merge_kernel(own_ref, cross_ref, out_ref):
    out_ref[:, :EX, :] = own_ref[...]
    out_ref[:, EX:, :] = cross_ref[...]


def merge(own, cross):
    vmem = pl.BlockSpec(memory_space=pltpu.VMEM)
    return pl.pallas_call(
        merge_kernel,
        out_shape=jax.ShapeDtypeStruct((GROUPS4, EX + PIV_DEV, LANES), BF16),
        in_specs=[vmem] * 2,
        out_specs=vmem,
        compiler_params=pltpu.CompilerParams(vmem_limit_bytes=8 << 20),
        cost_estimate=cost(0, 1 << 18),
        name="merge",
    )(own, cross)


def unpack_kernel(*refs):
    packed, all_ref, piv_refs = refs[:4], refs[4], refs[5:]
    examples = packed[0].shape[1]
    row = lax.broadcasted_iota(jnp.int32, (4 * LANES, 4 * LANES), 0)
    col = lax.broadcasted_iota(jnp.int32, (4 * LANES, 4 * LANES), 1)
    target = (row // CH) % 4 * LANES + row // LANES * CH + row % CH
    move = jnp.where(col == target, 1.0, 0.0).astype(BF16)
    flat = jnp.concatenate([ref[...].reshape(GROUPS4 * examples, LANES) for ref in packed], axis=1)
    moved = jnp.dot(flat, move, preferred_element_type=F32).astype(BF16)
    for group in range(GROUPS4):
        for j in range(4):
            py, px = group // 2, (group % 2) * 4 + j
            if px == SIDE:
                continue
            spot = moved[group * examples:(group + 1) * examples, j * LANES:(j + 1) * LANES]
            all_ref[py * SIDE + px] = spot[:EX]
            piv_refs[0][py * SIDE + px] = spot[:PIV_DEV]
            if examples > EX:
                piv_refs[1][py * SIDE + px] = spot[EX:]


def unpack(arrays, name):
    vmem = pl.BlockSpec(memory_space=pltpu.VMEM)
    pivots = jax.ShapeDtypeStruct((SPOTS, PIV_DEV, LANES), BF16)
    pivot_sets = arrays[0].shape[1] // PIV_DEV - 1
    return pl.pallas_call(
        unpack_kernel,
        out_shape=(jax.ShapeDtypeStruct((SPOTS, EX, LANES), BF16),) + (pivots,) * pivot_sets,
        in_specs=[vmem] * 4,
        out_specs=(vmem,) * (1 + pivot_sets),
        compiler_params=pltpu.CompilerParams(vmem_limit_bytes=12 << 20),
        cost_estimate=cost(0, 1 << 20),
        name=name,
    )(*arrays)


def panel_terms(x, g, xp, gp, lx, rx, rg, t):
    for py in range(SIDE):
        for px in range(PITCH):
            row, col = (py * SIDE + px) * EX, (py * PITCH + px) * PIV_DEV
            for d in range(3):
                from_x = px + d - 1
                inside = 0 <= from_x < SIDE and px < SIDE
                lanes = slice(d * LANES, (d + 1) * LANES)
                spot = py * SIDE + from_x
                rx[col:col + PIV_DEV, lanes] = xp[spot] if inside else jnp.zeros((PIV_DEV, LANES), BF16)
                if px < SIDE:
                    lx[row:row + EX, lanes] = x[spot] if inside else jnp.zeros((EX, LANES), BF16)
            rg[col:col + PIV_DEV, :] = gp[py * SIDE + px] if px < SIDE else jnp.zeros((PIV_DEV, LANES), BF16)

    contract = (((1,), (1,)), ((), ()))
    spans = [(qy, min(qy + 2, SIDE)) for qy in range(0, SIDE, 2)]
    for start, stop in spans:
        right = rx[start * COLB:stop * COLB, :]
        for py in range(SIDE):
            left = lx[py * ROWB:(py + 1) * ROWB, :]
            t[py, :, start * COLB:stop * COLB] = lax.dot_general(left, right, contract, preferred_element_type=F32)
    acc = jnp.zeros((EX, COLB), F32)
    for start, stop in spans:
        right = rg[start * COLB:stop * COLB, :]
        for py in range(SIDE):
            left = g[py * SIDE:(py + 1) * SIDE].reshape(ROWB, LANES)
            gg = lax.dot_general(left, right, contract, preferred_element_type=F32)
            for qy in range(start, stop):
                for px in range(SIDE):
                    rows = slice(px * EX, (px + 1) * EX)
                    total = t[py, rows, qy * COLB:(qy + 1) * COLB]
                    if py > 0 and qy > 0:
                        total = total + t[py - 1, rows, (qy - 1) * COLB:qy * COLB]
                    if py < SIDE - 1 and qy < SIDE - 1:
                        total = total + t[py + 1, rows, (qy + 1) * COLB:(qy + 2) * COLB]
                    acc = acc + gg[rows, (qy - start) * COLB:(qy - start + 1) * COLB] * total
    acc = acc + pltpu.roll(acc, 64, 1)
    acc = acc + pltpu.roll(acc, 32, 1)
    return acc + pltpu.roll(acc, 16, 1)


def own_kernel(x, g, xp, gp, out_ref, block_ref, *work):
    folded = panel_terms(x, g, xp, gp, *work)
    out_ref[...] = folded
    lane = lax.broadcasted_iota(jnp.int32, (8, LANES), 1)
    block_ref[...] = jnp.where(lane // PIV_DEV == 0, folded[:8], folded[8:PIV_DEV])


def cross_kernel(x, g, xp, gp, own_ref, block_ref, out_ref, *work):
    across = panel_terms(x, g, xp, gp, *work)
    lane = lax.broadcasted_iota(jnp.int32, (8, LANES), 1)
    is_own = (lane // PIV_DEV) % 2 == lax.axis_index("rows")
    packed = jnp.zeros((8, LANES), F32)
    for j in range(4):
        rows = slice(8 * j, 8 * j + 8)
        packed = jnp.where(lane // EX == j, jnp.where(is_own, own_ref[rows, :], across[rows]), packed)
    out_ref[0:8, :] = packed
    out_ref[8:16, :] = block_ref[...]


def terms(kernel, arrays, shapes, name):
    vmem = pl.BlockSpec(memory_space=pltpu.VMEM)
    rows, cols = SIDE * ROWB, SIDE * COLB
    return pl.pallas_call(
        kernel,
        out_shape=tuple(jax.ShapeDtypeStruct(shape, F32) for shape in shapes),
        in_specs=[vmem] * len(arrays),
        out_specs=(vmem,) * len(shapes),
        scratch_shapes=[
            pltpu.VMEM((rows, 3 * LANES), BF16),
            pltpu.VMEM((cols, 3 * LANES), BF16),
            pltpu.VMEM((cols, LANES), BF16),
            pltpu.VMEM((SIDE, ROWB, cols), F32),
        ],
        compiler_params=pltpu.CompilerParams(vmem_limit_bytes=24 << 20),
        cost_estimate=cost(2 * rows * cols * 4 * LANES, 8 << 20),
        name=name,
    )(*arrays)


def rows_of(packed, count):
    return jnp.concatenate(
        [packed[:, EX * j:EX * (j + 1)] for j in range(count)], axis=0
    )


def final_kernel(*refs):
    total_refs, (ridge_ref, gram_ref, factor_ref) = refs[:4], refs[4:]
    total = (total_refs[0][...] + total_refs[1][...]) + (total_refs[2][...] + total_refs[3][...])
    panel = rows_of(total[:8], 4)
    gram_ref[...] = panel
    group = lax.axis_index("rows")
    mine, zero = panel[:PIV_DEV], jnp.zeros((PIV_DEV, EX), F32)
    upper = jnp.concatenate([jnp.where(group == 0, mine, zero), jnp.where(group == 0, zero, mine)], axis=0)
    block = jnp.concatenate([total[8:, :PIV_DEV], total[8:, PIV_DEV:2 * PIV_DEV]], axis=0)
    block = jnp.concatenate([block, block], axis=1)
    block = jnp.concatenate([block, block], axis=0)
    row_id = lax.broadcasted_iota(jnp.int32, (EX, EX), 0)
    col_id = lax.broadcasted_iota(jnp.int32, (EX, EX), 1)
    diag = jnp.where(col_id // PIV_DEV == group, jnp.transpose(upper), block)
    diag = jnp.where(row_id // PIV_DEV == group, upper, diag)
    ridge = jnp.where(row_id == col_id, jnp.broadcast_to(ridge_ref[...], (EX, EX)), 0.0)
    system = 0.5 * (diag + jnp.transpose(diag)) + ridge
    factor = jnp.zeros((EX, EX), F32)
    step = 4
    for j in range(0, EX, step):
        sys_cols = [jnp.broadcast_to(system[:, j + k:j + k + 1], (EX, EX)) for k in range(step)]
        pan_cols = [jnp.broadcast_to(panel[:, j + k:j + k + 1], (EX, EX)) for k in range(step)]
        sys_rows = [system[j + k:j + k + 1, :] for k in range(step)]
        for k in range(step):
            scale = lax.rsqrt(sys_cols[k][j + k:j + k + 1, :])
            sys_cols[k], pan_cols[k], sys_rows[k] = sys_cols[k] * scale, pan_cols[k] * scale, sys_rows[k] * scale
            factor = jnp.where(col_id == j + k, pan_cols[k], factor)
            for m in range(k + 1, step):
                entry = sys_cols[k][j + m:j + m + 1, :]
                sys_cols[m] = sys_cols[m] - sys_cols[k] * entry
                pan_cols[m] = pan_cols[m] - pan_cols[k] * entry
                sys_rows[m] = sys_rows[m] - sys_rows[k] * entry
        if j + step < EX:
            for k in range(step):
                system = system - sys_cols[k] * sys_rows[k]
                panel = panel - pan_cols[k] * sys_rows[k]
    factor_ref[...] = factor


def final(totals, ridge):
    vmem = pl.BlockSpec(memory_space=pltpu.VMEM)
    out = jax.ShapeDtypeStruct((EX, EX), F32)
    return pl.pallas_call(
        final_kernel,
        out_shape=(out, out),
        in_specs=[vmem] * 5,
        out_specs=(vmem, vmem),
        compiler_params=pltpu.CompilerParams(vmem_limit_bytes=8 << 20),
        name="solve",
    )(*totals, ridge.reshape(1, EX))


def exchange(value, count, flip):
    return lax.ppermute(value, "chan", [(i, i ^ flip) for i in range(count)])


def exchange_across(value, count):
    pairs = [(g * count + i, (1 - g) * count + i) for g in range(2) for i in range(count)]
    return lax.ppermute(value, ("rows", "chan"), pairs)


def local_packed(count, activations, cotangents, ordering, ridge):
    near, far = (1, 2, 3), (4, 8, 12)
    x = jnp.transpose(activations, (1, 2, 0, 3)).reshape(SIDE * SIDE, EX, CH)
    xo, go, gp = prep(ordering, x, cotangents)
    gm = merge(go, exchange_across(gp, count))
    own_g = [gm] + [exchange(gm, count, f) for f in near]
    own_x = [xo] + [exchange(xo, count, f) for f in far]
    x_all, x_piv = unpack(own_x, "unpack_x")
    x_cross = exchange_across(x_piv, count)
    g_all, g_piv, g_cross = unpack(own_g, "unpack_g")
    own_term, block = terms(own_kernel, (x_all, g_all, x_piv, g_piv), ((EX, LANES), (8, LANES)), "terms_own")
    block = exchange_across(block, count)
    term, = terms(cross_kernel, (x_all, g_all, x_cross, g_cross, own_term, block), ((16, LANES),), "terms_cross")
    terms_near = [term] + [exchange(term, count, f) for f in near]
    part = (terms_near[0] + terms_near[1]) + (terms_near[2] + terms_near[3])
    return final([part] + [exchange(part, count, f) for f in far], ridge)


def jacobian_block(grad_rows, input_rows):
    example_count = input_rows.shape[0]
    side_len = input_rows.shape[1]
    channel_count = input_rows.shape[3]
    grad_count = grad_rows.shape[1]
    grid_grads = grad_rows.reshape(example_count, grad_count, side_len, side_len)
    padded_grads = jnp.pad(grid_grads, ((0, 0), (0, 0), (1, 1), (1, 1)))
    shifted = []
    for row_shift in range(3):
        for col_shift in range(3):
            window = padded_grads[
                :,
                :,
                2 - row_shift : 2 - row_shift + side_len,
                2 - col_shift : 2 - col_shift + side_len,
            ]
            shifted.append(window.reshape(example_count, grad_count, side_len * side_len))
    stacked_grads = jnp.stack(shifted, axis=2).reshape(
        example_count, grad_count * 9, side_len * side_len
    )
    flat_inputs = input_rows.reshape(example_count, side_len * side_len, channel_count)
    product = jnp.einsum(
        "nkp,npq->nkq", stacked_grads, flat_inputs, preferred_element_type=jnp.float32
    )
    return product.astype(jnp.bfloat16).reshape(example_count, -1)


def gram_block(left_rows, right_rows):
    return lax.dot_general(
        left_rows, right_rows, (((1,), (1,)), ((), ())), preferred_element_type=jnp.float32
    )


def local(activations, cotangents, ordering, ridge):
    local_order = ordering[0]
    own_inputs = jnp.take(activations, local_order, axis=0)
    own_grads = jnp.take(cotangents, local_order, axis=0)
    pivot_count = PIV_DEV
    pivot_inputs, pivot_grads = (
        lax.all_gather(own_inputs[:pivot_count], "rows", axis=0, tiled=True),
        lax.all_gather(own_grads[:pivot_count], "rows", axis=0, tiled=True),
    )
    full_own, full_pivot = (
        lax.all_gather(own_inputs, "chan", axis=3, tiled=True),
        lax.all_gather(pivot_inputs, "chan", axis=3, tiled=True),
    )
    own_jac = jacobian_block(own_grads, full_own)
    pivot_jac = jacobian_block(pivot_grads, full_pivot)
    partial_panel = gram_block(own_jac, pivot_jac)
    gram_panel = lax.psum(partial_panel, "chan")
    diag_block = lax.all_gather(gram_panel[:pivot_count], "rows", axis=0, tiled=True)
    system = 0.5 * (diag_block + diag_block.T) + jnp.diag(ridge)
    lower = jnp.linalg.cholesky(system)
    factor_panel = jax.scipy.linalg.solve_triangular(lower, gram_panel.T, lower=True).T
    return (gram_panel, factor_panel)


def solution(mesh):
    row_groups, count = mesh.shape["rows"], mesh.shape["chan"]
    packed = row_groups == 2 and count == 16
    return jax.shard_map(
        functools.partial(local_packed, count) if packed else local,
        mesh=mesh,
        in_specs=(P("rows", None, None, "chan"), P("rows", "chan", None), P("rows", None), P()),
        out_specs=(P("rows", None), P("rows", None)),
        check_vma=False,
    )
```

```python
import functools

import jax
import jax.numpy as jnp
from jax import lax
from jax.experimental import pallas as pl
from jax.experimental.pallas import tpu as pltpu
from jax.sharding import PartitionSpec as P

PIV_DEV = 16

SIDE = 7
PITCH = 8
GROUPS4 = 14
CH = 32
EX = 32
LANES = 128
F32 = jnp.float32
BF16 = jnp.bfloat16


def fetch(sources, targets, sems):
    copies = [pltpu.make_async_copy(a, b, sems.at[i]) for i, (a, b) in enumerate(zip(sources, targets))]
    for copy in copies:
        copy.start()
    return copies


def prep_kernel(order_hbm, x_hbm, g_hbm, xo_ref, go_ref, gp_ref, order_ref, x_ref, g_ref, sems, gs, gt, gout):
    for copy in fetch((order_hbm, x_hbm, g_hbm), (order_ref, x_ref, g_ref), sems):
        copy.wait()
    row_id = lax.broadcasted_iota(jnp.int32, (EX, EX), 0)
    col_id = lax.broadcasted_iota(jnp.int32, (EX, EX), 1)
    onehot = jnp.zeros((EX, EX), F32)
    for k in range(EX):
        example = order_ref[0, k]
        onehot = jnp.where((row_id == k) & (col_id == example), 1.0, onehot)
        gs[k * CH:(k + 1) * CH, 0:SIDE * SIDE] = g_ref[example].astype(F32)
    onehot = onehot.astype(BF16)
    zero_block = jnp.zeros((EX, CH), BF16)
    for group in range(GROUPS4):
        pieces = []
        for j in range(4):
            py, px = group // 2, (group % 2) * 4 + j
            pieces.append(x_ref[py * SIDE + px] if px < SIDE else zero_block)
        packed = jnp.concatenate(pieces, axis=1)
        xo_ref[group] = jnp.dot(onehot, packed, preferred_element_type=F32).astype(BF16)
    block_id = lax.broadcasted_iota(jnp.int32, (GROUPS4, LANES), 1) // CH
    for quad in range(EX // 4):
        flipped = jnp.transpose(gs[quad * LANES:(quad + 1) * LANES, :])
        for py in range(SIDE):
            gt[py * PITCH:py * PITCH + SIDE, :] = flipped[py * SIDE:(py + 1) * SIDE, :]
            gt[py * PITCH + SIDE:(py + 1) * PITCH, :] = jnp.zeros((1, LANES), F32)
        parts = [gt[pl.ds(j, GROUPS4, stride=4), :] for j in range(4)]
        for e in range(4):
            merged = jnp.zeros((GROUPS4, LANES), F32)
            for j in range(4):
                shift = (CH * (j - e)) % LANES
                moved = pltpu.roll(parts[j], shift, 1) if shift else parts[j]
                merged = jnp.where(block_id == j, moved, merged)
            gout[pl.ds(quad * 4 + e, GROUPS4, stride=EX), :] = merged
    for group in range(GROUPS4):
        ordered = gout[group * EX:(group + 1) * EX, :].astype(BF16)
        go_ref[group] = ordered
        gp_ref[group] = ordered[:PIV_DEV]


def prep(order, x, g):
    full = jax.ShapeDtypeStruct((GROUPS4, EX, LANES), BF16)
    vmem = pl.BlockSpec(memory_space=pltpu.VMEM)
    return pl.pallas_call(
        prep_kernel,
        out_shape=(full, full, jax.ShapeDtypeStruct((GROUPS4, PIV_DEV, LANES), BF16)),
        in_specs=[pl.BlockSpec(memory_space=pl.ANY)] * 3,
        out_specs=(vmem,) * 3,
        scratch_shapes=[
            pltpu.SMEM(order.shape, order.dtype),
            pltpu.VMEM(x.shape, x.dtype),
            pltpu.VMEM(g.shape, g.dtype),
            pltpu.SemaphoreType.DMA((3,)),
            pltpu.VMEM((EX * CH, LANES), F32),
            pltpu.VMEM((SIDE * PITCH, LANES), F32),
            pltpu.VMEM((GROUPS4 * EX, LANES), F32),
        ],
        compiler_params=pltpu.CompilerParams(vmem_limit_bytes=56 << 20),
        name="prep",
    )(order, x, g)


SPOTS = SIDE * SIDE
COLB = PITCH * PIV_DEV


def cost(flops, moved):
    return pl.CostEstimate(flops=flops, bytes_accessed=moved, transcendentals=0)


def merge_kernel(own_ref, cross_ref, out_ref):
    out_ref[:, :EX, :] = own_ref[...]
    out_ref[:, EX:, :] = cross_ref[...]


def merge(own, cross):
    vmem = pl.BlockSpec(memory_space=pltpu.VMEM)
    return pl.pallas_call(
        merge_kernel,
        out_shape=jax.ShapeDtypeStruct((GROUPS4, EX + PIV_DEV, LANES), BF16),
        in_specs=[vmem] * 2,
        out_specs=vmem,
        compiler_params=pltpu.CompilerParams(vmem_limit_bytes=8 << 20),
        cost_estimate=cost(0, 1 << 18),
        name="merge",
    )(own, cross)


def unpack_body(packed, all_ref, piv_refs):
    examples = packed[0].shape[1]
    row = lax.broadcasted_iota(jnp.int32, (4 * LANES, 4 * LANES), 0)
    col = lax.broadcasted_iota(jnp.int32, (4 * LANES, 4 * LANES), 1)
    target = (row // CH) % 4 * LANES + row // LANES * CH + row % CH
    move = jnp.where(col == target, 1.0, 0.0).astype(BF16)
    flat = jnp.concatenate([ref[...].reshape(GROUPS4 * examples, LANES) for ref in packed], axis=1)
    moved = jnp.dot(flat, move, preferred_element_type=F32).astype(BF16)
    for group in range(GROUPS4):
        for j in range(4):
            py, px = group // 2, (group % 2) * 4 + j
            if px == SIDE:
                continue
            spot = moved[group * examples:(group + 1) * examples, j * LANES:(j + 1) * LANES]
            all_ref[py * SIDE + px] = spot[:EX]
            piv_refs[0][py * SIDE + px] = spot[:PIV_DEV]
            if examples > EX:
                piv_refs[1][py * SIDE + px] = spot[EX:]


def unpack_kernel(*refs):
    unpack_body(refs[:4], refs[4], refs[5:])


def unpack_gathered_kernel(gathered, all_ref, piv_ref):
    unpack_body([gathered.at[i] for i in range(4)], all_ref, (piv_ref,))


def unpack(arrays, name):
    vmem = pl.BlockSpec(memory_space=pltpu.VMEM)
    pivots = jax.ShapeDtypeStruct((SPOTS, PIV_DEV, LANES), BF16)
    pivot_sets = arrays[0].shape[-2] // PIV_DEV - 1
    gathered = len(arrays) == 1
    return pl.pallas_call(
        unpack_gathered_kernel if gathered else unpack_kernel,
        out_shape=(jax.ShapeDtypeStruct((SPOTS, EX, LANES), BF16),) + (pivots,) * pivot_sets,
        in_specs=[vmem] * len(arrays),
        out_specs=(vmem,) * (1 + pivot_sets),
        compiler_params=pltpu.CompilerParams(vmem_limit_bytes=12 << 20),
        cost_estimate=cost(0, 1 << 20),
        name=name,
    )(*arrays)


def panel_terms(rows_x, rows_g, xp, gp, lx, lg, rx, rg, t):
    heights = [ref.shape[1] for ref in rows_x]
    height = sum(heights)
    block = SIDE * height
    for py in range(SIDE):
        for px in range(PITCH):
            row, col = (py * SIDE + px) * height, (py * PITCH + px) * PIV_DEV
            for d in range(3):
                from_x = px + d - 1
                inside = 0 <= from_x < SIDE and px < SIDE
                lanes = slice(d * LANES, (d + 1) * LANES)
                spot = py * SIDE + from_x
                rx[col:col + PIV_DEV, lanes] = xp[spot] if inside else jnp.zeros((PIV_DEV, LANES), BF16)
                if px < SIDE:
                    first = row
                    for ref, count in zip(rows_x, heights):
                        lx[first:first + count, lanes] = ref[spot] if inside else jnp.zeros((count, LANES), BF16)
                        first += count
            rg[col:col + PIV_DEV, :] = gp[py * SIDE + px] if px < SIDE else jnp.zeros((PIV_DEV, LANES), BF16)
            if px < SIDE:
                first = row
                for ref, count in zip(rows_g, heights):
                    lg[first:first + count, :] = ref[py * SIDE + px]
                    first += count

    contract = (((1,), (1,)), ((), ()))
    spans = [(qy, min(qy + 2, SIDE)) for qy in range(0, SIDE, 2)]
    for start, stop in spans:
        right = rx[start * COLB:stop * COLB, :]
        for py in range(SIDE):
            left = lx[py * block:(py + 1) * block, :]
            t[py, :, start * COLB:stop * COLB] = lax.dot_general(left, right, contract, preferred_element_type=F32)
    acc = jnp.zeros((height, COLB), F32)
    for start, stop in spans:
        right = rg[start * COLB:stop * COLB, :]
        for py in range(SIDE):
            left = lg[py * block:(py + 1) * block, :]
            gg = lax.dot_general(left, right, contract, preferred_element_type=F32)
            for qy in range(start, stop):
                for px in range(SIDE):
                    rows = slice(px * height, (px + 1) * height)
                    total = t[py, rows, qy * COLB:(qy + 1) * COLB]
                    if py > 0 and qy > 0:
                        total = total + t[py - 1, rows, (qy - 1) * COLB:qy * COLB]
                    if py < SIDE - 1 and qy < SIDE - 1:
                        total = total + t[py + 1, rows, (qy + 1) * COLB:(qy + 2) * COLB]
                    acc = acc + gg[rows, (qy - start) * COLB:(qy - start + 1) * COLB] * total
    acc = acc + pltpu.roll(acc, 64, 1)
    acc = acc + pltpu.roll(acc, 32, 1)
    return acc + pltpu.roll(acc, 16, 1)


def own_kernel(x, g, xp, gp, out_ref, *work):
    out_ref[...] = panel_terms([x], [g], xp, gp, *work)


def cross_kernel(x, g, xp, gp, own_ref, out_ref, *work):
    across = panel_terms([x, xp], [g, gp], xp, gp, *work)
    lane = lax.broadcasted_iota(jnp.int32, (8, LANES), 1)
    is_own = (lane // PIV_DEV) % 2 == lax.axis_index("rows")
    packed = jnp.zeros((8, LANES), F32)
    for j in range(4):
        rows = slice(8 * j, 8 * j + 8)
        packed = jnp.where(lane // EX == j, jnp.where(is_own, own_ref[rows, :], across[rows]), packed)
    out_ref[0:8, :] = packed
    out_ref[8:16, :] = jnp.where(lane // PIV_DEV == 0, across[EX:EX + 8], across[EX + 8:EX + PIV_DEV])


def terms(kernel, arrays, height, shape, name):
    vmem = pl.BlockSpec(memory_space=pltpu.VMEM)
    rows, cols = SPOTS * height, SIDE * COLB
    return pl.pallas_call(
        kernel,
        out_shape=jax.ShapeDtypeStruct(shape, F32),
        in_specs=[vmem] * len(arrays),
        out_specs=vmem,
        scratch_shapes=[
            pltpu.VMEM((rows, 3 * LANES), BF16),
            pltpu.VMEM((rows, LANES), BF16),
            pltpu.VMEM((cols, 3 * LANES), BF16),
            pltpu.VMEM((cols, LANES), BF16),
            pltpu.VMEM((SIDE, SIDE * height, cols), F32),
        ],
        compiler_params=pltpu.CompilerParams(vmem_limit_bytes=28 << 20),
        cost_estimate=cost(2 * rows * cols * 4 * LANES, 8 << 20),
        name=name,
    )(*arrays)


def rows_of(packed, count):
    return jnp.concatenate(
        [packed[:, EX * j:EX * (j + 1)] for j in range(count)], axis=0
    )


def final_kernel(*refs):
    total_refs, (ridge_ref, gram_ref, factor_ref) = refs[:4], refs[4:]
    total = (total_refs[0][...] + total_refs[1][...]) + (total_refs[2][...] + total_refs[3][...])
    panel = rows_of(total[:8], 4)
    gram_ref[...] = panel
    group = lax.axis_index("rows")
    mine, zero = panel[:PIV_DEV], jnp.zeros((PIV_DEV, EX), F32)
    upper = jnp.concatenate([jnp.where(group == 0, mine, zero), jnp.where(group == 0, zero, mine)], axis=0)
    block = jnp.concatenate([total[8:, :PIV_DEV], total[8:, PIV_DEV:2 * PIV_DEV]], axis=0)
    block = jnp.concatenate([block, block], axis=1)
    block = jnp.concatenate([block, block], axis=0)
    row_id = lax.broadcasted_iota(jnp.int32, (EX, EX), 0)
    col_id = lax.broadcasted_iota(jnp.int32, (EX, EX), 1)
    diag = jnp.where(col_id // PIV_DEV == group, jnp.transpose(upper), block)
    diag = jnp.where(row_id // PIV_DEV == group, upper, diag)
    ridge = jnp.where(row_id == col_id, jnp.broadcast_to(ridge_ref[...], (EX, EX)), 0.0)
    system = 0.5 * (diag + jnp.transpose(diag)) + ridge
    factor = jnp.zeros((EX, EX), F32)
    step = 4
    for j in range(0, EX, step):
        sys_cols = [jnp.broadcast_to(system[:, j + k:j + k + 1], (EX, EX)) for k in range(step)]
        pan_cols = [jnp.broadcast_to(panel[:, j + k:j + k + 1], (EX, EX)) for k in range(step)]
        sys_rows = [system[j + k:j + k + 1, :] for k in range(step)]
        for k in range(step):
            scale = lax.rsqrt(sys_cols[k][j + k:j + k + 1, :])
            sys_cols[k], pan_cols[k], sys_rows[k] = sys_cols[k] * scale, pan_cols[k] * scale, sys_rows[k] * scale
            factor = jnp.where(col_id == j + k, pan_cols[k], factor)
            for m in range(k + 1, step):
                entry = sys_cols[k][j + m:j + m + 1, :]
                sys_cols[m] = sys_cols[m] - sys_cols[k] * entry
                pan_cols[m] = pan_cols[m] - pan_cols[k] * entry
                sys_rows[m] = sys_rows[m] - sys_rows[k] * entry
        if j + step < EX:
            for k in range(step):
                system = system - sys_cols[k] * sys_rows[k]
                panel = panel - pan_cols[k] * sys_rows[k]
    factor_ref[...] = factor


def final(totals, ridge):
    vmem = pl.BlockSpec(memory_space=pltpu.VMEM)
    out = jax.ShapeDtypeStruct((EX, EX), F32)
    return pl.pallas_call(
        final_kernel,
        out_shape=(out, out),
        in_specs=[vmem] * 5,
        out_specs=(vmem, vmem),
        compiler_params=pltpu.CompilerParams(vmem_limit_bytes=8 << 20),
        name="solve",
    )(*totals, ridge.reshape(1, EX))


def exchange(value, count, flip):
    return lax.ppermute(value, "chan", [(i, i ^ flip) for i in range(count)])


def exchange_across(value, count):
    pairs = [(g * count + i, (1 - g) * count + i) for g in range(2) for i in range(count)]
    return lax.ppermute(value, ("rows", "chan"), pairs)


def local_packed(count, activations, cotangents, ordering, ridge):
    near, far = (1, 2, 3), (4, 8, 12)
    x = jnp.transpose(activations, (1, 2, 0, 3)).reshape(SIDE * SIDE, EX, CH)
    xo, go, gp = prep(ordering, x, cotangents)
    gm = merge(go, exchange_across(gp, count))
    own_g = [gm] + [exchange(gm, count, f) for f in near]
    lines = [[4 * i + k for i in range(count // 4)] for k in range(4)]
    x_all, x_piv = unpack([lax.all_gather(xo, "chan", axis_index_groups=lines)], "unpack_x")
    x_cross = exchange_across(x_piv, count)
    g_all, g_piv, g_cross = unpack(own_g, "unpack_g")
    own_term = terms(own_kernel, (x_all, g_all, x_piv, g_piv), EX, (EX, LANES), "terms_own")
    arrays = (x_all, g_all, x_cross, g_cross, own_term)
    term = terms(cross_kernel, arrays, EX + PIV_DEV, (16, LANES), "terms_cross")
    terms_near = [term] + [exchange(term, count, f) for f in near]
    part = (terms_near[0] + terms_near[1]) + (terms_near[2] + terms_near[3])
    return final([part] + [exchange(part, count, f) for f in far], ridge)


def jacobian_block(grad_rows, input_rows):
    example_count = input_rows.shape[0]
    side_len = input_rows.shape[1]
    channel_count = input_rows.shape[3]
    grad_count = grad_rows.shape[1]
    grid_grads = grad_rows.reshape(example_count, grad_count, side_len, side_len)
    padded_grads = jnp.pad(grid_grads, ((0, 0), (0, 0), (1, 1), (1, 1)))
    shifted = []
    for row_shift in range(3):
        for col_shift in range(3):
            window = padded_grads[
                :,
                :,
                2 - row_shift : 2 - row_shift + side_len,
                2 - col_shift : 2 - col_shift + side_len,
            ]
            shifted.append(window.reshape(example_count, grad_count, side_len * side_len))
    stacked_grads = jnp.stack(shifted, axis=2).reshape(
        example_count, grad_count * 9, side_len * side_len
    )
    flat_inputs = input_rows.reshape(example_count, side_len * side_len, channel_count)
    product = jnp.einsum(
        "nkp,npq->nkq", stacked_grads, flat_inputs, preferred_element_type=jnp.float32
    )
    return product.astype(jnp.bfloat16).reshape(example_count, -1)


def gram_block(left_rows, right_rows):
    return lax.dot_general(
        left_rows, right_rows, (((1,), (1,)), ((), ())), preferred_element_type=jnp.float32
    )


def local(activations, cotangents, ordering, ridge):
    local_order = ordering[0]
    own_inputs = jnp.take(activations, local_order, axis=0)
    own_grads = jnp.take(cotangents, local_order, axis=0)
    pivot_count = PIV_DEV
    pivot_inputs, pivot_grads = (
        lax.all_gather(own_inputs[:pivot_count], "rows", axis=0, tiled=True),
        lax.all_gather(own_grads[:pivot_count], "rows", axis=0, tiled=True),
    )
    full_own, full_pivot = (
        lax.all_gather(own_inputs, "chan", axis=3, tiled=True),
        lax.all_gather(pivot_inputs, "chan", axis=3, tiled=True),
    )
    own_jac = jacobian_block(own_grads, full_own)
    pivot_jac = jacobian_block(pivot_grads, full_pivot)
    partial_panel = gram_block(own_jac, pivot_jac)
    gram_panel = lax.psum(partial_panel, "chan")
    diag_block = lax.all_gather(gram_panel[:pivot_count], "rows", axis=0, tiled=True)
    system = 0.5 * (diag_block + diag_block.T) + jnp.diag(ridge)
    lower = jnp.linalg.cholesky(system)
    factor_panel = jax.scipy.linalg.solve_triangular(lower, gram_panel.T, lower=True).T
    return (gram_panel, factor_panel)


def solution(mesh):
    row_groups, count = mesh.shape["rows"], mesh.shape["chan"]
    packed = row_groups == 2 and count == 16
    return jax.shard_map(
        functools.partial(local_packed, count) if packed else local,
        mesh=mesh,
        in_specs=(P("rows", None, None, "chan"), P("rows", "chan", None), P("rows", None), P()),
        out_specs=(P("rows", None), P("rows", None)),
        check_vma=False,
    )
```

```python
import functools

import jax
import jax.numpy as jnp
from jax import lax
from jax.experimental import pallas as pl
from jax.experimental.pallas import tpu as pltpu
from jax.sharding import PartitionSpec as P

PIV_DEV = 16

SIDE = 7
PITCH = 8
GROUPS4 = 14
CH = 32
EX = 32
LANES = 128
F32 = jnp.float32
BF16 = jnp.bfloat16


def fetch(sources, targets, sems):
    copies = [pltpu.make_async_copy(a, b, sems.at[i]) for i, (a, b) in enumerate(zip(sources, targets))]
    for copy in copies:
        copy.start()
    return copies


def prep_kernel(order_hbm, x_hbm, g_hbm, xo_ref, go_ref, gp_ref, order_ref, x_ref, g_ref, sems, gs, gt, gout):
    copies = fetch((order_hbm, g_hbm, x_hbm), (order_ref, g_ref, x_ref), sems)
    copies[0].wait()
    copies[1].wait()
    row_id = lax.broadcasted_iota(jnp.int32, (EX, EX), 0)
    col_id = lax.broadcasted_iota(jnp.int32, (EX, EX), 1)
    onehot = jnp.zeros((EX, EX), F32)
    for k in range(EX):
        example = order_ref[0, k]
        onehot = jnp.where((row_id == k) & (col_id == example), 1.0, onehot)
        gs[k * CH:(k + 1) * CH, 0:SIDE * SIDE] = g_ref[example].astype(F32)
    block_id = lax.broadcasted_iota(jnp.int32, (GROUPS4, LANES), 1) // CH
    for quad in range(EX // 4):
        flipped = jnp.transpose(gs[quad * LANES:(quad + 1) * LANES, :])
        for py in range(SIDE):
            gt[py * PITCH:py * PITCH + SIDE, :] = flipped[py * SIDE:(py + 1) * SIDE, :]
            gt[py * PITCH + SIDE:(py + 1) * PITCH, :] = jnp.zeros((1, LANES), F32)
        parts = [gt[pl.ds(j, GROUPS4, stride=4), :] for j in range(4)]
        for e in range(4):
            merged = jnp.zeros((GROUPS4, LANES), F32)
            for j in range(4):
                shift = (CH * (j - e)) % LANES
                moved = pltpu.roll(parts[j], shift, 1) if shift else parts[j]
                merged = jnp.where(block_id == j, moved, merged)
            gout[pl.ds(quad * 4 + e, GROUPS4, stride=EX), :] = merged
    for group in range(GROUPS4):
        ordered = gout[group * EX:(group + 1) * EX, :].astype(BF16)
        go_ref[group] = ordered
        gp_ref[group] = ordered[:PIV_DEV]
    copies[2].wait()
    onehot = onehot.astype(BF16)
    zero_block = jnp.zeros((EX, CH), BF16)
    for group in range(GROUPS4):
        pieces = []
        for j in range(4):
            py, px = group // 2, (group % 2) * 4 + j
            pieces.append(x_ref[py * SIDE + px] if px < SIDE else zero_block)
        packed = jnp.concatenate(pieces, axis=1)
        xo_ref[group] = jnp.dot(onehot, packed, preferred_element_type=F32).astype(BF16)


def prep(order, x, g):
    full = jax.ShapeDtypeStruct((GROUPS4, EX, LANES), BF16)
    vmem = pl.BlockSpec(memory_space=pltpu.VMEM)
    return pl.pallas_call(
        prep_kernel,
        out_shape=(full, full, jax.ShapeDtypeStruct((GROUPS4, PIV_DEV, LANES), BF16)),
        in_specs=[pl.BlockSpec(memory_space=pltpu.HBM)] * 3,
        out_specs=(vmem,) * 3,
        scratch_shapes=[
            pltpu.SMEM(order.shape, order.dtype),
            pltpu.VMEM(x.shape, x.dtype),
            pltpu.VMEM(g.shape, g.dtype),
            pltpu.SemaphoreType.DMA((3,)),
            pltpu.VMEM((EX * CH, LANES), F32),
            pltpu.VMEM((SIDE * PITCH, LANES), F32),
            pltpu.VMEM((GROUPS4 * EX, LANES), F32),
        ],
        compiler_params=pltpu.CompilerParams(vmem_limit_bytes=54848 << 10),
        name="prep",
    )(order, x, g)


SPOTS = SIDE * SIDE
COLB = PITCH * PIV_DEV


def cost(flops, moved):
    return pl.CostEstimate(flops=flops, bytes_accessed=moved, transcendentals=0)


def merge_kernel(own_ref, cross_ref, out_ref):
    out_ref[:, :EX, :] = own_ref[...]
    out_ref[:, EX:, :] = cross_ref[...]


def merge(own, cross):
    vmem = pl.BlockSpec(memory_space=pltpu.VMEM)
    return pl.pallas_call(
        merge_kernel,
        out_shape=jax.ShapeDtypeStruct((GROUPS4, EX + PIV_DEV, LANES), BF16),
        in_specs=[vmem] * 2,
        out_specs=vmem,
        compiler_params=pltpu.CompilerParams(vmem_limit_bytes=8 << 20),
        cost_estimate=cost(0, 1 << 18),
        name="merge",
    )(own, cross)


def unpack_kernel(*refs):
    packed, all_ref, piv_refs = refs[:4], refs[4], refs[5:]
    examples = packed[0].shape[1]
    row = lax.broadcasted_iota(jnp.int32, (4 * LANES, 4 * LANES), 0)
    col = lax.broadcasted_iota(jnp.int32, (4 * LANES, 4 * LANES), 1)
    target = (row // CH) % 4 * LANES + row // LANES * CH + row % CH
    move = jnp.where(col == target, 1.0, 0.0).astype(BF16)
    flat = jnp.concatenate([ref[...].reshape(GROUPS4 * examples, LANES) for ref in packed], axis=1)
    moved = jnp.dot(flat, move, preferred_element_type=F32).astype(BF16)
    for group in range(GROUPS4):
        for j in range(4):
            py, px = group // 2, (group % 2) * 4 + j
            if px == SIDE:
                continue
            spot = moved[group * examples:(group + 1) * examples, j * LANES:(j + 1) * LANES]
            all_ref[py * SIDE + px] = spot[:EX]
            piv_refs[0][py * SIDE + px] = spot[:PIV_DEV]
            if examples > EX:
                piv_refs[1][py * SIDE + px] = spot[EX:]


def unpack(arrays, name):
    vmem = pl.BlockSpec(memory_space=pltpu.VMEM)
    pivots = jax.ShapeDtypeStruct((SPOTS, PIV_DEV, LANES), BF16)
    pivot_sets = arrays[0].shape[1] // PIV_DEV - 1
    return pl.pallas_call(
        unpack_kernel,
        out_shape=(jax.ShapeDtypeStruct((SPOTS, EX, LANES), BF16),) + (pivots,) * pivot_sets,
        in_specs=[vmem] * 4,
        out_specs=(vmem,) * (1 + pivot_sets),
        compiler_params=pltpu.CompilerParams(vmem_limit_bytes=12 << 20),
        cost_estimate=cost(0, 1 << 20),
        name=name,
    )(*arrays)


def panel_terms(rows_x, rows_g, xp, gp, lx, lg, rx, rg, t):
    heights = [ref.shape[1] for ref in rows_x]
    height = sum(heights)
    block = SIDE * height
    for py in range(SIDE):
        for px in range(PITCH):
            row, col = (py * SIDE + px) * height, (py * PITCH + px) * PIV_DEV
            for d in range(3):
                from_x = px + d - 1
                inside = 0 <= from_x < SIDE and px < SIDE
                lanes = slice(d * LANES, (d + 1) * LANES)
                spot = py * SIDE + from_x
                rx[col:col + PIV_DEV, lanes] = xp[spot] if inside else jnp.zeros((PIV_DEV, LANES), BF16)
                if px < SIDE:
                    first = row
                    for ref, count in zip(rows_x, heights):
                        lx[first:first + count, lanes] = ref[spot] if inside else jnp.zeros((count, LANES), BF16)
                        first += count
            rg[col:col + PIV_DEV, :] = gp[py * SIDE + px] if px < SIDE else jnp.zeros((PIV_DEV, LANES), BF16)
            if px < SIDE:
                first = row
                for ref, count in zip(rows_g, heights):
                    lg[first:first + count, :] = ref[py * SIDE + px]
                    first += count

    contract = (((1,), (1,)), ((), ()))
    spans = [(qy, min(qy + 2, SIDE)) for qy in range(0, SIDE, 2)]
    for start, stop in spans:
        right = rx[start * COLB:stop * COLB, :]
        for py in range(SIDE):
            left = lx[py * block:(py + 1) * block, :]
            t[py, :, start * COLB:stop * COLB] = lax.dot_general(left, right, contract, preferred_element_type=F32)
    acc = jnp.zeros((height, COLB), F32)
    for start, stop in spans:
        right = rg[start * COLB:stop * COLB, :]
        for py in range(SIDE):
            left = lg[py * block:(py + 1) * block, :]
            gg = lax.dot_general(left, right, contract, preferred_element_type=F32)
            for qy in range(start, stop):
                for px in range(SIDE):
                    rows = slice(px * height, (px + 1) * height)
                    total = t[py, rows, qy * COLB:(qy + 1) * COLB]
                    if py > 0 and qy > 0:
                        total = total + t[py - 1, rows, (qy - 1) * COLB:qy * COLB]
                    if py < SIDE - 1 and qy < SIDE - 1:
                        total = total + t[py + 1, rows, (qy + 1) * COLB:(qy + 2) * COLB]
                    acc = acc + gg[rows, (qy - start) * COLB:(qy - start + 1) * COLB] * total
    acc = acc + pltpu.roll(acc, 64, 1)
    acc = acc + pltpu.roll(acc, 32, 1)
    return acc + pltpu.roll(acc, 16, 1)


def own_kernel(x, g, xp, gp, out_ref, *work):
    out_ref[...] = panel_terms([x], [g], xp, gp, *work)


def cross_kernel(x, g, xp, gp, own_ref, out_ref, *work):
    across = panel_terms([x], [g], xp, gp, *work)
    lane = lax.broadcasted_iota(jnp.int32, (8, LANES), 1)
    is_own = (lane // PIV_DEV) % 2 == lax.axis_index("rows")
    packed = jnp.zeros((8, LANES), F32)
    for j in range(4):
        rows = slice(8 * j, 8 * j + 8)
        packed = jnp.where(lane // EX == j, jnp.where(is_own, own_ref[rows, :], across[rows]), packed)
    out_ref[...] = packed


def terms(kernel, arrays, height, shape, name):
    vmem = pl.BlockSpec(memory_space=pltpu.VMEM)
    rows, cols = SPOTS * height, SIDE * COLB
    return pl.pallas_call(
        kernel,
        out_shape=jax.ShapeDtypeStruct(shape, F32),
        in_specs=[vmem] * len(arrays),
        out_specs=vmem,
        scratch_shapes=[
            pltpu.VMEM((rows, 3 * LANES), BF16),
            pltpu.VMEM((rows, LANES), BF16),
            pltpu.VMEM((cols, 3 * LANES), BF16),
            pltpu.VMEM((cols, LANES), BF16),
            pltpu.VMEM((SIDE, SIDE * height, cols), F32),
        ],
        compiler_params=pltpu.CompilerParams(vmem_limit_bytes=28 << 20),
        cost_estimate=cost(2 * rows * cols * 4 * LANES, 8 << 20),
        name=name,
    )(*arrays)


def rows_of(packed, count):
    return jnp.concatenate(
        [packed[:, EX * j:EX * (j + 1)] for j in range(count)], axis=0
    )


def tree_sum(values):
    while len(values) > 1:
        values = [a + b for a, b in zip(values[0::2], values[1::2])]
    return values[0]


def final_kernel(terms_ref, ridge_ref, gram_ref, factor_ref):
    count = terms_ref.shape[0] // 2
    sums = [tree_sum([terms_ref[g * count + i] for i in range(count)]) for g in range(2)]
    panel = rows_of(jnp.where(lax.axis_index("rows") == 0, sums[0], sums[1]), 4)
    gram_ref[...] = panel
    diag = jnp.concatenate([rows_of(total, 2) for total in sums], axis=0)
    row_id = lax.broadcasted_iota(jnp.int32, (EX, EX), 0)
    col_id = lax.broadcasted_iota(jnp.int32, (EX, EX), 1)
    ridge = jnp.where(row_id == col_id, jnp.broadcast_to(ridge_ref[...], (EX, EX)), 0.0)
    system = 0.5 * (diag + jnp.transpose(diag)) + ridge
    factor = jnp.zeros((EX, EX), F32)
    step = 4
    for j in range(0, EX, step):
        sys_cols = [jnp.broadcast_to(system[:, j + k:j + k + 1], (EX, EX)) for k in range(step)]
        pan_cols = [jnp.broadcast_to(panel[:, j + k:j + k + 1], (EX, EX)) for k in range(step)]
        sys_rows = [system[j + k:j + k + 1, :] for k in range(step)]
        for k in range(step):
            scale = lax.rsqrt(sys_cols[k][j + k:j + k + 1, :])
            sys_cols[k], pan_cols[k], sys_rows[k] = sys_cols[k] * scale, pan_cols[k] * scale, sys_rows[k] * scale
            factor = jnp.where(col_id == j + k, pan_cols[k], factor)
            for m in range(k + 1, step):
                entry = sys_cols[k][j + m:j + m + 1, :]
                sys_cols[m] = sys_cols[m] - sys_cols[k] * entry
                pan_cols[m] = pan_cols[m] - pan_cols[k] * entry
                sys_rows[m] = sys_rows[m] - sys_rows[k] * entry
        if j + step < EX:
            for k in range(step):
                system = system - sys_cols[k] * sys_rows[k]
                panel = panel - pan_cols[k] * sys_rows[k]
    factor_ref[...] = factor


def final(terms_of_all, ridge):
    vmem = pl.BlockSpec(memory_space=pltpu.VMEM)
    out = jax.ShapeDtypeStruct((EX, EX), F32)
    return pl.pallas_call(
        final_kernel,
        out_shape=(out, out),
        in_specs=[vmem] * 2,
        out_specs=(vmem, vmem),
        compiler_params=pltpu.CompilerParams(vmem_limit_bytes=8 << 20),
        name="solve",
    )(terms_of_all, ridge.reshape(1, EX))


def exchange(value, count, flip):
    return lax.ppermute(value, "chan", [(i, i ^ flip) for i in range(count)])


def gather(value, count, first, second):
    received = exchange(value, count, first)
    return [value, exchange(value, count, second), received, exchange(received, count, second)]


def exchange_across(value, count):
    pairs = [(g * count + i, (1 - g) * count + i) for g in range(2) for i in range(count)]
    return lax.ppermute(value, ("rows", "chan"), pairs)


def local_packed(count, activations, cotangents, ordering, ridge):
    x = jnp.transpose(activations, (1, 2, 0, 3)).reshape(SIDE * SIDE, EX, CH)
    xo, go, gp = prep(ordering, x, cotangents)
    gm = merge(go, exchange_across(gp, count))
    x_all, x_piv = unpack(gather(xo, count, 8, 4), "unpack_x")
    x_cross = exchange_across(x_piv, count)
    g_all, g_piv, g_cross = unpack([gm] + [exchange(gm, count, f) for f in (1, 2, 3)], "unpack_g")
    own_term = terms(own_kernel, (x_all, g_all, x_piv, g_piv), EX, (EX, LANES), "terms_own")
    term = terms(cross_kernel, (x_all, g_all, x_cross, g_cross, own_term), EX, (8, LANES), "terms_cross")
    copies = jnp.broadcast_to(term, (2 * count, 8, LANES))
    return final(lax.all_to_all(copies, ("rows", "chan"), 0, 0), ridge)


def jacobian_block(grad_rows, input_rows):
    example_count = input_rows.shape[0]
    side_len = input_rows.shape[1]
    channel_count = input_rows.shape[3]
    grad_count = grad_rows.shape[1]
    grid_grads = grad_rows.reshape(example_count, grad_count, side_len, side_len)
    padded_grads = jnp.pad(grid_grads, ((0, 0), (0, 0), (1, 1), (1, 1)))
    shifted = []
    for row_shift in range(3):
        for col_shift in range(3):
            window = padded_grads[
                :,
                :,
                2 - row_shift : 2 - row_shift + side_len,
                2 - col_shift : 2 - col_shift + side_len,
            ]
            shifted.append(window.reshape(example_count, grad_count, side_len * side_len))
    stacked_grads = jnp.stack(shifted, axis=2).reshape(
        example_count, grad_count * 9, side_len * side_len
    )
    flat_inputs = input_rows.reshape(example_count, side_len * side_len, channel_count)
    product = jnp.einsum(
        "nkp,npq->nkq", stacked_grads, flat_inputs, preferred_element_type=jnp.float32
    )
    return product.astype(jnp.bfloat16).reshape(example_count, -1)


def gram_block(left_rows, right_rows):
    return lax.dot_general(
        left_rows, right_rows, (((1,), (1,)), ((), ())), preferred_element_type=jnp.float32
    )


def local(activations, cotangents, ordering, ridge):
    local_order = ordering[0]
    own_inputs = jnp.take(activations, local_order, axis=0)
    own_grads = jnp.take(cotangents, local_order, axis=0)
    pivot_count = PIV_DEV
    pivot_inputs, pivot_grads = (
        lax.all_gather(own_inputs[:pivot_count], "rows", axis=0, tiled=True),
        lax.all_gather(own_grads[:pivot_count], "rows", axis=0, tiled=True),
    )
    full_own, full_pivot = (
        lax.all_gather(own_inputs, "chan", axis=3, tiled=True),
        lax.all_gather(pivot_inputs, "chan", axis=3, tiled=True),
    )
    own_jac = jacobian_block(own_grads, full_own)
    pivot_jac = jacobian_block(pivot_grads, full_pivot)
    partial_panel = gram_block(own_jac, pivot_jac)
    gram_panel = lax.psum(partial_panel, "chan")
    diag_block = lax.all_gather(gram_panel[:pivot_count], "rows", axis=0, tiled=True)
    system = 0.5 * (diag_block + diag_block.T) + jnp.diag(ridge)
    lower = jnp.linalg.cholesky(system)
    factor_panel = jax.scipy.linalg.solve_triangular(lower, gram_panel.T, lower=True).T
    return (gram_panel, factor_panel)


def solution(mesh):
    row_groups, count = mesh.shape["rows"], mesh.shape["chan"]
    packed = row_groups == 2 and count == 16
    return jax.shard_map(
        functools.partial(local_packed, count) if packed else local,
        mesh=mesh,
        in_specs=(P("rows", None, None, "chan"), P("rows", "chan", None), P("rows", None), P()),
        out_specs=(P("rows", None), P("rows", None)),
        check_vma=False,
    )
```

```python
import functools

import jax
import jax.numpy as jnp
from jax import lax
from jax.experimental import pallas as pl
from jax.experimental.pallas import tpu as pltpu
from jax.sharding import PartitionSpec as P

PIV_DEV = 16

SIDE = 7
PITCH = 8
GROUPS4 = 14
CH = 32
EX = 32
LANES = 128
F32 = jnp.float32
BF16 = jnp.bfloat16


def fetch(sources, targets, sems):
    copies = [pltpu.make_async_copy(a, b, sems.at[i]) for i, (a, b) in enumerate(zip(sources, targets))]
    for copy in copies:
        copy.start()
    return copies


def prep_kernel(order_hbm, x_hbm, g_hbm, xo_ref, go_ref, order_ref, x_ref, g_ref, sems, gs, gt, gout):
    copies = fetch((order_hbm, g_hbm, x_hbm), (order_ref, g_ref, x_ref), sems)
    copies[0].wait()
    copies[1].wait()
    row_id = lax.broadcasted_iota(jnp.int32, (EX, EX), 0)
    col_id = lax.broadcasted_iota(jnp.int32, (EX, EX), 1)
    onehot = jnp.zeros((EX, EX), F32)
    for k in range(EX):
        example = order_ref[0, k]
        onehot = jnp.where((row_id == k) & (col_id == example), 1.0, onehot)
        gs[k * CH:(k + 1) * CH, 0:SIDE * SIDE] = g_ref[example].astype(F32)
    block_id = lax.broadcasted_iota(jnp.int32, (GROUPS4, LANES), 1) // CH
    for quad in range(EX // 4):
        flipped = jnp.transpose(gs[quad * LANES:(quad + 1) * LANES, :])
        for py in range(SIDE):
            gt[py * PITCH:py * PITCH + SIDE, :] = flipped[py * SIDE:(py + 1) * SIDE, :]
            gt[py * PITCH + SIDE:(py + 1) * PITCH, :] = jnp.zeros((1, LANES), F32)
        parts = [gt[pl.ds(j, GROUPS4, stride=4), :] for j in range(4)]
        for e in range(4):
            merged = jnp.zeros((GROUPS4, LANES), F32)
            for j in range(4):
                shift = (CH * (j - e)) % LANES
                moved = pltpu.roll(parts[j], shift, 1) if shift else parts[j]
                merged = jnp.where(block_id == j, moved, merged)
            gout[pl.ds(quad * 4 + e, GROUPS4, stride=EX), :] = merged
    for group in range(GROUPS4):
        go_ref[group] = gout[group * EX:(group + 1) * EX, :].astype(BF16)
    copies[2].wait()
    onehot = onehot.astype(BF16)
    zero_block = jnp.zeros((EX, CH), BF16)
    for group in range(GROUPS4):
        pieces = []
        for j in range(4):
            py, px = group // 2, (group % 2) * 4 + j
            pieces.append(x_ref[py * SIDE + px] if px < SIDE else zero_block)
        packed = jnp.concatenate(pieces, axis=1)
        xo_ref[group] = jnp.dot(onehot, packed, preferred_element_type=F32).astype(BF16)


def prep(order, x, g):
    full = jax.ShapeDtypeStruct((GROUPS4, EX, LANES), BF16)
    vmem = pl.BlockSpec(memory_space=pltpu.VMEM)
    return pl.pallas_call(
        prep_kernel,
        out_shape=(full, full),
        in_specs=[pl.BlockSpec(memory_space=pltpu.HBM)] * 3,
        out_specs=(vmem,) * 2,
        scratch_shapes=[
            pltpu.SMEM(order.shape, order.dtype),
            pltpu.VMEM(x.shape, x.dtype),
            pltpu.VMEM(g.shape, g.dtype),
            pltpu.SemaphoreType.DMA((3,)),
            pltpu.VMEM((EX * CH, LANES), F32),
            pltpu.VMEM((SIDE * PITCH, LANES), F32),
            pltpu.VMEM((GROUPS4 * EX, LANES), F32),
        ],
        compiler_params=pltpu.CompilerParams(vmem_limit_bytes=54848 << 10),
        name="prep",
    )(order, x, g)


SPOTS = SIDE * SIDE
COLB = PITCH * PIV_DEV


def cost(flops, moved):
    return pl.CostEstimate(flops=flops, bytes_accessed=moved, transcendentals=0)


def unpack_kernel(*refs):
    packed, all_ref, piv_ref = refs[:4], refs[4], refs[5]
    row = lax.broadcasted_iota(jnp.int32, (4 * LANES, 4 * LANES), 0)
    col = lax.broadcasted_iota(jnp.int32, (4 * LANES, 4 * LANES), 1)
    target = (row // CH) % 4 * LANES + row // LANES * CH + row % CH
    move = jnp.where(col == target, 1.0, 0.0).astype(BF16)
    flat = jnp.concatenate([ref[...].reshape(GROUPS4 * EX, LANES) for ref in packed], axis=1)
    moved = jnp.dot(flat, move, preferred_element_type=F32).astype(BF16)
    for group in range(GROUPS4):
        for j in range(4):
            py, px = group // 2, (group % 2) * 4 + j
            if px == SIDE:
                continue
            spot = moved[group * EX:(group + 1) * EX, j * LANES:(j + 1) * LANES]
            all_ref[py * SIDE + px] = spot
            piv_ref[py * SIDE + px] = spot[:PIV_DEV]


def unpack(arrays, name):
    vmem = pl.BlockSpec(memory_space=pltpu.VMEM)
    pivots = jax.ShapeDtypeStruct((SPOTS, PIV_DEV, LANES), BF16)
    return pl.pallas_call(
        unpack_kernel,
        out_shape=(jax.ShapeDtypeStruct((SPOTS, EX, LANES), BF16), pivots),
        in_specs=[vmem] * 4,
        out_specs=(vmem,) * 2,
        compiler_params=pltpu.CompilerParams(vmem_limit_bytes=12 << 20),
        cost_estimate=cost(0, 1 << 20),
        name=name,
    )(*arrays)


def panel_terms(rows_x, rows_g, xp, gp, lx, lg, rx, rg, t):
    heights = [ref.shape[1] for ref in rows_x]
    height = sum(heights)
    block = SIDE * height
    for py in range(SIDE):
        for px in range(PITCH):
            row, col = (py * SIDE + px) * height, (py * PITCH + px) * PIV_DEV
            for d in range(3):
                from_x = px + d - 1
                inside = 0 <= from_x < SIDE and px < SIDE
                lanes = slice(d * LANES, (d + 1) * LANES)
                spot = py * SIDE + from_x
                rx[col:col + PIV_DEV, lanes] = xp[spot] if inside else jnp.zeros((PIV_DEV, LANES), BF16)
                if px < SIDE:
                    first = row
                    for ref, count in zip(rows_x, heights):
                        lx[first:first + count, lanes] = ref[spot] if inside else jnp.zeros((count, LANES), BF16)
                        first += count
            rg[col:col + PIV_DEV, :] = gp[py * SIDE + px] if px < SIDE else jnp.zeros((PIV_DEV, LANES), BF16)
            if px < SIDE:
                first = row
                for ref, count in zip(rows_g, heights):
                    lg[first:first + count, :] = ref[py * SIDE + px]
                    first += count

    contract = (((1,), (1,)), ((), ()))
    spans = [(qy, min(qy + 2, SIDE)) for qy in range(0, SIDE, 2)]
    for start, stop in spans:
        right = rx[start * COLB:stop * COLB, :]
        for py in range(SIDE):
            left = lx[py * block:(py + 1) * block, :]
            t[py, :, start * COLB:stop * COLB] = lax.dot_general(left, right, contract, preferred_element_type=F32)
    acc = jnp.zeros((height, COLB), F32)
    for start, stop in spans:
        right = rg[start * COLB:stop * COLB, :]
        for py in range(SIDE):
            left = lg[py * block:(py + 1) * block, :]
            gg = lax.dot_general(left, right, contract, preferred_element_type=F32)
            for qy in range(start, stop):
                for px in range(SIDE):
                    rows = slice(px * height, (px + 1) * height)
                    total = t[py, rows, qy * COLB:(qy + 1) * COLB]
                    if py > 0 and qy > 0:
                        total = total + t[py - 1, rows, (qy - 1) * COLB:qy * COLB]
                    if py < SIDE - 1 and qy < SIDE - 1:
                        total = total + t[py + 1, rows, (qy + 1) * COLB:(qy + 2) * COLB]
                    acc = acc + gg[rows, (qy - start) * COLB:(qy - start + 1) * COLB] * total
    acc = acc + pltpu.roll(acc, 64, 1)
    acc = acc + pltpu.roll(acc, 32, 1)
    return acc + pltpu.roll(acc, 16, 1)


def own_kernel(x, g, xp, gp, out_ref, *work):
    out_ref[...] = panel_terms([x], [g], xp, gp, *work)


def cross_kernel(x, g, xp, gp, own_ref, out_ref, *work):
    across = panel_terms([x], [g], xp, gp, *work)
    lane = lax.broadcasted_iota(jnp.int32, (8, LANES), 1)
    is_own = (lane // PIV_DEV) % 2 == lax.axis_index("rows")
    packed = jnp.zeros((8, LANES), F32)
    for j in range(4):
        rows = slice(8 * j, 8 * j + 8)
        packed = jnp.where(lane // EX == j, jnp.where(is_own, own_ref[rows, :], across[rows]), packed)
    out_ref[...] = packed


def terms(kernel, arrays, height, shape, name):
    vmem = pl.BlockSpec(memory_space=pltpu.VMEM)
    rows, cols = SPOTS * height, SIDE * COLB
    return pl.pallas_call(
        kernel,
        out_shape=jax.ShapeDtypeStruct(shape, F32),
        in_specs=[vmem] * len(arrays),
        out_specs=vmem,
        scratch_shapes=[
            pltpu.VMEM((rows, 3 * LANES), BF16),
            pltpu.VMEM((rows, LANES), BF16),
            pltpu.VMEM((cols, 3 * LANES), BF16),
            pltpu.VMEM((cols, LANES), BF16),
            pltpu.VMEM((SIDE, SIDE * height, cols), F32),
        ],
        compiler_params=pltpu.CompilerParams(vmem_limit_bytes=28 << 20),
        cost_estimate=cost(2 * rows * cols * 4 * LANES, 8 << 20),
        name=name,
    )(*arrays)


def rows_of(packed, count):
    return jnp.concatenate(
        [packed[:, EX * j:EX * (j + 1)] for j in range(count)], axis=0
    )


def tree_sum(values):
    while len(values) > 1:
        values = [a + b for a, b in zip(values[0::2], values[1::2])]
    return values[0]


def final_kernel(terms_ref, ridge_ref, gram_ref, factor_ref):
    count = terms_ref.shape[0] // 2
    sums = [tree_sum([terms_ref[g * count + i] for i in range(count)]) for g in range(2)]
    panel = rows_of(jnp.where(lax.axis_index("rows") == 0, sums[0], sums[1]), 4)
    gram_ref[...] = panel
    diag = jnp.concatenate([rows_of(total, 2) for total in sums], axis=0)
    row_id = lax.broadcasted_iota(jnp.int32, (EX, EX), 0)
    col_id = lax.broadcasted_iota(jnp.int32, (EX, EX), 1)
    ridge = jnp.where(row_id == col_id, jnp.broadcast_to(ridge_ref[...], (EX, EX)), 0.0)
    system = 0.5 * (diag + jnp.transpose(diag)) + ridge
    factor = jnp.zeros((EX, EX), F32)
    step = 4
    for j in range(0, EX, step):
        sys_cols = [jnp.broadcast_to(system[:, j + k:j + k + 1], (EX, EX)) for k in range(step)]
        pan_cols = [jnp.broadcast_to(panel[:, j + k:j + k + 1], (EX, EX)) for k in range(step)]
        sys_rows = [system[j + k:j + k + 1, :] for k in range(step)]
        for k in range(step):
            scale = lax.rsqrt(sys_cols[k][j + k:j + k + 1, :])
            sys_cols[k], pan_cols[k], sys_rows[k] = sys_cols[k] * scale, pan_cols[k] * scale, sys_rows[k] * scale
            factor = jnp.where(col_id == j + k, pan_cols[k], factor)
            for m in range(k + 1, step):
                entry = sys_cols[k][j + m:j + m + 1, :]
                sys_cols[m] = sys_cols[m] - sys_cols[k] * entry
                pan_cols[m] = pan_cols[m] - pan_cols[k] * entry
                sys_rows[m] = sys_rows[m] - sys_rows[k] * entry
        if j + step < EX:
            for k in range(step):
                system = system - sys_cols[k] * sys_rows[k]
                panel = panel - pan_cols[k] * sys_rows[k]
    factor_ref[...] = factor


def final(terms_of_all, ridge):
    vmem = pl.BlockSpec(memory_space=pltpu.VMEM)
    out = jax.ShapeDtypeStruct((EX, EX), F32)
    return pl.pallas_call(
        final_kernel,
        out_shape=(out, out),
        in_specs=[vmem] * 2,
        out_specs=(vmem, vmem),
        compiler_params=pltpu.CompilerParams(vmem_limit_bytes=8 << 20),
        name="solve",
    )(terms_of_all, ridge.reshape(1, EX))


def exchange(value, count, flip):
    return lax.ppermute(value, "chan", [(i, i ^ flip) for i in range(count)])


def gather(value, count, first, second):
    received = exchange(value, count, first)
    return [value, exchange(value, count, second), received, exchange(received, count, second)]


def exchange_across(value, count):
    pairs = [(g * count + i, (1 - g) * count + i) for g in range(2) for i in range(count)]
    return lax.ppermute(value, ("rows", "chan"), pairs)


def local_packed(count, activations, cotangents, ordering, ridge):
    x = jnp.transpose(activations, (1, 2, 0, 3)).reshape(SIDE * SIDE, EX, CH)
    xo, go = prep(ordering, x, cotangents)
    x_all, x_piv = unpack(gather(xo, count, 2, 1), "unpack_x")
    x_cross = exchange_across(x_piv, count)
    g_all, g_piv = unpack(gather(go, count, 8, 4), "unpack_g")
    g_cross = exchange_across(g_piv, count)
    own_term = terms(own_kernel, (x_all, g_all, x_piv, g_piv), EX, (EX, LANES), "terms_own")
    term = terms(cross_kernel, (x_all, g_all, x_cross, g_cross, own_term), EX, (8, LANES), "terms_cross")
    copies = jnp.broadcast_to(term, (2 * count, 8, LANES))
    return final(lax.all_to_all(copies, ("rows", "chan"), 0, 0), ridge)


def jacobian_block(grad_rows, input_rows):
    example_count = input_rows.shape[0]
    side_len = input_rows.shape[1]
    channel_count = input_rows.shape[3]
    grad_count = grad_rows.shape[1]
    grid_grads = grad_rows.reshape(example_count, grad_count, side_len, side_len)
    padded_grads = jnp.pad(grid_grads, ((0, 0), (0, 0), (1, 1), (1, 1)))
    shifted = []
    for row_shift in range(3):
        for col_shift in range(3):
            window = padded_grads[
                :,
                :,
                2 - row_shift : 2 - row_shift + side_len,
                2 - col_shift : 2 - col_shift + side_len,
            ]
            shifted.append(window.reshape(example_count, grad_count, side_len * side_len))
    stacked_grads = jnp.stack(shifted, axis=2).reshape(
        example_count, grad_count * 9, side_len * side_len
    )
    flat_inputs = input_rows.reshape(example_count, side_len * side_len, channel_count)
    product = jnp.einsum(
        "nkp,npq->nkq", stacked_grads, flat_inputs, preferred_element_type=jnp.float32
    )
    return product.astype(jnp.bfloat16).reshape(example_count, -1)


def gram_block(left_rows, right_rows):
    return lax.dot_general(
        left_rows, right_rows, (((1,), (1,)), ((), ())), preferred_element_type=jnp.float32
    )


def local(activations, cotangents, ordering, ridge):
    local_order = ordering[0]
    own_inputs = jnp.take(activations, local_order, axis=0)
    own_grads = jnp.take(cotangents, local_order, axis=0)
    pivot_count = PIV_DEV
    pivot_inputs, pivot_grads = (
        lax.all_gather(own_inputs[:pivot_count], "rows", axis=0, tiled=True),
        lax.all_gather(own_grads[:pivot_count], "rows", axis=0, tiled=True),
    )
    full_own, full_pivot = (
        lax.all_gather(own_inputs, "chan", axis=3, tiled=True),
        lax.all_gather(pivot_inputs, "chan", axis=3, tiled=True),
    )
    own_jac = jacobian_block(own_grads, full_own)
    pivot_jac = jacobian_block(pivot_grads, full_pivot)
    partial_panel = gram_block(own_jac, pivot_jac)
    gram_panel = lax.psum(partial_panel, "chan")
    diag_block = lax.all_gather(gram_panel[:pivot_count], "rows", axis=0, tiled=True)
    system = 0.5 * (diag_block + diag_block.T) + jnp.diag(ridge)
    lower = jnp.linalg.cholesky(system)
    factor_panel = jax.scipy.linalg.solve_triangular(lower, gram_panel.T, lower=True).T
    return (gram_panel, factor_panel)


def solution(mesh):
    row_groups, count = mesh.shape["rows"], mesh.shape["chan"]
    packed = row_groups == 2 and count == 16
    return jax.shard_map(
        functools.partial(local_packed, count) if packed else local,
        mesh=mesh,
        in_specs=(P("rows", None, None, "chan"), P("rows", "chan", None), P("rows", None), P()),
        out_specs=(P("rows", None), P("rows", None)),
        check_vma=False,
    )
```

```python
import functools

import jax
import jax.numpy as jnp
from jax import lax
from jax.experimental import pallas as pl
from jax.experimental.pallas import tpu as pltpu
from jax.sharding import PartitionSpec as P

PIV_DEV = 16

SIDE = 7
PITCH = 8
GROUPS4 = 14
CH = 32
EX = 32
LANES = 128
F32 = jnp.float32
BF16 = jnp.bfloat16


def fetch(sources, targets, sems):
    copies = [pltpu.make_async_copy(a, b, sems.at[i]) for i, (a, b) in enumerate(zip(sources, targets))]
    for copy in copies:
        copy.start()
    return copies


def prep_kernel(order_hbm, x_hbm, g_hbm, xo_ref, go_ref, order_ref, x_ref, g_ref, sems, gs, gt, gout):
    copies = fetch((order_hbm, g_hbm, x_hbm), (order_ref, g_ref, x_ref), sems)
    copies[0].wait()
    copies[1].wait()
    row_id = lax.broadcasted_iota(jnp.int32, (EX, EX), 0)
    col_id = lax.broadcasted_iota(jnp.int32, (EX, EX), 1)
    onehot = jnp.zeros((EX, EX), F32)
    for k in range(EX):
        example = order_ref[0, k]
        onehot = jnp.where((row_id == k) & (col_id == example), 1.0, onehot)
        gs[k * CH:(k + 1) * CH, 0:SIDE * SIDE] = g_ref[example].astype(F32)
    block_id = lax.broadcasted_iota(jnp.int32, (GROUPS4, LANES), 1) // CH
    for quad in range(EX // 4):
        flipped = jnp.transpose(gs[quad * LANES:(quad + 1) * LANES, :])
        for py in range(SIDE):
            gt[py * PITCH:py * PITCH + SIDE, :] = flipped[py * SIDE:(py + 1) * SIDE, :]
            gt[py * PITCH + SIDE:(py + 1) * PITCH, :] = jnp.zeros((1, LANES), F32)
        parts = [gt[pl.ds(j, GROUPS4, stride=4), :] for j in range(4)]
        for e in range(4):
            merged = jnp.zeros((GROUPS4, LANES), F32)
            for j in range(4):
                shift = (CH * (j - e)) % LANES
                moved = pltpu.roll(parts[j], shift, 1) if shift else parts[j]
                merged = jnp.where(block_id == j, moved, merged)
            gout[pl.ds(quad * 4 + e, GROUPS4, stride=EX), :] = merged
    for group in range(GROUPS4):
        go_ref[group] = gout[group * EX:(group + 1) * EX, :].astype(BF16)
    copies[2].wait()
    onehot = onehot.astype(BF16)
    zero_block = jnp.zeros((EX, CH), BF16)
    for group in range(GROUPS4):
        pieces = []
        for j in range(4):
            py, px = group // 2, (group % 2) * 4 + j
            pieces.append(x_ref[py * SIDE + px] if px < SIDE else zero_block)
        packed = jnp.concatenate(pieces, axis=1)
        xo_ref[group] = jnp.dot(onehot, packed, preferred_element_type=F32).astype(BF16)


def prep(order, x, g):
    full = jax.ShapeDtypeStruct((GROUPS4, EX, LANES), BF16)
    vmem = pl.BlockSpec(memory_space=pltpu.VMEM)
    return pl.pallas_call(
        prep_kernel,
        out_shape=(full, full),
        in_specs=[pl.BlockSpec(memory_space=pltpu.HBM)] * 3,
        out_specs=(vmem,) * 2,
        scratch_shapes=[
            pltpu.SMEM(order.shape, order.dtype),
            pltpu.VMEM(x.shape, x.dtype),
            pltpu.VMEM(g.shape, g.dtype),
            pltpu.SemaphoreType.DMA((3,)),
            pltpu.VMEM((EX * CH, LANES), F32),
            pltpu.VMEM((SIDE * PITCH, LANES), F32),
            pltpu.VMEM((GROUPS4 * EX, LANES), F32),
        ],
        compiler_params=pltpu.CompilerParams(vmem_limit_bytes=54848 << 10),
        name="prep",
    )(order, x, g)


SPOTS = SIDE * SIDE
COLB = PITCH * PIV_DEV


def cost(flops, moved):
    return pl.CostEstimate(flops=flops, bytes_accessed=moved, transcendentals=0)


def unpack_kernel(*refs):
    packed, all_ref, piv_ref = refs[:4], refs[4], refs[5]
    row = lax.broadcasted_iota(jnp.int32, (4 * LANES, 4 * LANES), 0)
    col = lax.broadcasted_iota(jnp.int32, (4 * LANES, 4 * LANES), 1)
    target = (row // CH) % 4 * LANES + row // LANES * CH + row % CH
    move = jnp.where(col == target, 1.0, 0.0).astype(BF16)
    flat = jnp.concatenate([ref[...].reshape(GROUPS4 * EX, LANES) for ref in packed], axis=1)
    moved = jnp.dot(flat, move, preferred_element_type=F32).astype(BF16)
    for group in range(GROUPS4):
        for j in range(4):
            py, px = group // 2, (group % 2) * 4 + j
            if px == SIDE:
                continue
            spot = moved[group * EX:(group + 1) * EX, j * LANES:(j + 1) * LANES]
            all_ref[py * SIDE + px] = spot
            piv_ref[py * SIDE + px] = spot[:PIV_DEV]


def unpack(arrays, name):
    vmem = pl.BlockSpec(memory_space=pltpu.VMEM)
    pivots = jax.ShapeDtypeStruct((SPOTS, PIV_DEV, LANES), BF16)
    return pl.pallas_call(
        unpack_kernel,
        out_shape=(jax.ShapeDtypeStruct((SPOTS, EX, LANES), BF16), pivots),
        in_specs=[vmem] * 4,
        out_specs=(vmem,) * 2,
        compiler_params=pltpu.CompilerParams(vmem_limit_bytes=12 << 20),
        cost_estimate=cost(0, 1 << 20),
        name=name,
    )(*arrays)


CONTRACT = (((1,), (1,)), ((), ()))
SPANS = [(qy, min(qy + 2, SIDE)) for qy in range(0, SIDE, 2)]


def input_products(rows_x, xp, lx, rx, t):
    heights = [ref.shape[1] for ref in rows_x]
    height = sum(heights)
    for py in range(SIDE):
        for px in range(PITCH):
            row, col = (py * SIDE + px) * height, (py * PITCH + px) * PIV_DEV
            for d in range(3):
                from_x = px + d - 1
                inside = 0 <= from_x < SIDE and px < SIDE
                lanes = slice(d * LANES, (d + 1) * LANES)
                spot = py * SIDE + from_x
                rx[col:col + PIV_DEV, lanes] = xp[spot] if inside else jnp.zeros((PIV_DEV, LANES), BF16)
                if px < SIDE:
                    first = row
                    for ref, count in zip(rows_x, heights):
                        lx[first:first + count, lanes] = ref[spot] if inside else jnp.zeros((count, LANES), BF16)
                        first += count
    block = SIDE * height
    for start, stop in SPANS:
        right = rx[start * COLB:stop * COLB, :]
        for py in range(SIDE):
            left = lx[py * block:(py + 1) * block, :]
            t[py, :, start * COLB:stop * COLB] = lax.dot_general(left, right, CONTRACT, preferred_element_type=F32)


def panel_terms(rows_g, gp, lg, rg, t):
    heights = [ref.shape[1] for ref in rows_g]
    height = sum(heights)
    for py in range(SIDE):
        for px in range(PITCH):
            row, col = (py * SIDE + px) * height, (py * PITCH + px) * PIV_DEV
            rg[col:col + PIV_DEV, :] = gp[py * SIDE + px] if px < SIDE else jnp.zeros((PIV_DEV, LANES), BF16)
            if px < SIDE:
                first = row
                for ref, count in zip(rows_g, heights):
                    lg[first:first + count, :] = ref[py * SIDE + px]
                    first += count
    block = SIDE * height
    acc = jnp.zeros((height, COLB), F32)
    for start, stop in SPANS:
        right = rg[start * COLB:stop * COLB, :]
        for py in range(SIDE):
            left = lg[py * block:(py + 1) * block, :]
            gg = lax.dot_general(left, right, CONTRACT, preferred_element_type=F32)
            for qy in range(start, stop):
                for px in range(SIDE):
                    rows = slice(px * height, (px + 1) * height)
                    total = t[py, rows, qy * COLB:(qy + 1) * COLB]
                    if py > 0 and qy > 0:
                        total = total + t[py - 1, rows, (qy - 1) * COLB:qy * COLB]
                    if py < SIDE - 1 and qy < SIDE - 1:
                        total = total + t[py + 1, rows, (qy + 1) * COLB:(qy + 2) * COLB]
                    acc = acc + gg[rows, (qy - start) * COLB:(qy - start + 1) * COLB] * total
    acc = acc + pltpu.roll(acc, 64, 1)
    acc = acc + pltpu.roll(acc, 32, 1)
    return acc + pltpu.roll(acc, 16, 1)


def own_kernel(x, g, xp, gp, ridge, out_ref, ridge_out, lx, rx, lg, rg, t):
    ridge_out[...] = ridge[...]
    input_products([x], xp, lx, rx, t)
    out_ref[...] = panel_terms([g], gp, lg, rg, t)


def cross_inputs_kernel(x, xp, t_out, lx, rx):
    input_products([x, xp], xp, lx, rx, t_out)


def cross_kernel(t, g, gp, own_ref, out_ref, lg, rg):
    across = panel_terms([g, gp], gp, lg, rg, t)
    lane = lax.broadcasted_iota(jnp.int32, (8, LANES), 1)
    is_own = (lane // PIV_DEV) % 2 == lax.axis_index("rows")
    packed = jnp.zeros((8, LANES), F32)
    for j in range(4):
        rows = slice(8 * j, 8 * j + 8)
        packed = jnp.where(lane // EX == j, jnp.where(is_own, own_ref[rows, :], across[rows]), packed)
    out_ref[0:8, :] = packed
    out_ref[8:16, :] = jnp.where(lane // PIV_DEV == 0, across[EX:EX + 8], across[EX + 8:EX + PIV_DEV])


def product_shape(height):
    return (SIDE, SIDE * height, SIDE * COLB)


def scratch_of(height, width):
    return [pltpu.VMEM((SPOTS * height, width), BF16), pltpu.VMEM((SIDE * COLB, width), BF16)]


def terms(kernel, arrays, shapes, scratch, flops, name):
    vmem = pl.BlockSpec(memory_space=pltpu.VMEM)
    return pl.pallas_call(
        kernel,
        out_shape=tuple(jax.ShapeDtypeStruct(shape, F32) for shape in shapes),
        in_specs=[vmem] * len(arrays),
        out_specs=(vmem,) * len(shapes),
        scratch_shapes=scratch,
        compiler_params=pltpu.CompilerParams(vmem_limit_bytes=20 << 20),
        cost_estimate=cost(flops, 4 << 20),
        name=name,
    )(*arrays)


def rows_of(packed, count):
    return jnp.concatenate(
        [packed[:, EX * j:EX * (j + 1)] for j in range(count)], axis=0
    )


def final_kernel(total_ref, ridge_ref, gram_ref, factor_ref):
    total = (total_ref[0] + total_ref[1]) + (total_ref[2] + total_ref[3])
    panel = rows_of(total[:8], 4)
    gram_ref[...] = panel
    group = lax.axis_index("rows")
    mine, zero = panel[:PIV_DEV], jnp.zeros((PIV_DEV, EX), F32)
    upper = jnp.concatenate([jnp.where(group == 0, mine, zero), jnp.where(group == 0, zero, mine)], axis=0)
    block = jnp.concatenate([total[8:, :PIV_DEV], total[8:, PIV_DEV:2 * PIV_DEV]], axis=0)
    block = jnp.concatenate([block, block], axis=1)
    block = jnp.concatenate([block, block], axis=0)
    row_id = lax.broadcasted_iota(jnp.int32, (EX, EX), 0)
    col_id = lax.broadcasted_iota(jnp.int32, (EX, EX), 1)
    diag = jnp.where(col_id // PIV_DEV == group, jnp.transpose(upper), block)
    diag = jnp.where(row_id // PIV_DEV == group, upper, diag)
    ridge = jnp.where(row_id == col_id, jnp.broadcast_to(ridge_ref[...], (EX, EX)), 0.0)
    system = 0.5 * (diag + jnp.transpose(diag)) + ridge
    factor = jnp.zeros((EX, EX), F32)
    step = 4
    for j in range(0, EX, step):
        sys_cols = [jnp.broadcast_to(system[:, j + k:j + k + 1], (EX, EX)) for k in range(step)]
        pan_cols = [jnp.broadcast_to(panel[:, j + k:j + k + 1], (EX, EX)) for k in range(step)]
        sys_rows = [system[j + k:j + k + 1, :] for k in range(step)]
        for k in range(step):
            scale = lax.rsqrt(sys_cols[k][j + k:j + k + 1, :])
            sys_cols[k], pan_cols[k], sys_rows[k] = sys_cols[k] * scale, pan_cols[k] * scale, sys_rows[k] * scale
            factor = jnp.where(col_id == j + k, pan_cols[k], factor)
            for m in range(k + 1, step):
                entry = sys_cols[k][j + m:j + m + 1, :]
                sys_cols[m] = sys_cols[m] - sys_cols[k] * entry
                pan_cols[m] = pan_cols[m] - pan_cols[k] * entry
                sys_rows[m] = sys_rows[m] - sys_rows[k] * entry
        if j + step < EX:
            for k in range(step):
                system = system - sys_cols[k] * sys_rows[k]
                panel = panel - pan_cols[k] * sys_rows[k]
    factor_ref[...] = factor


def final(totals, ridge):
    vmem = pl.BlockSpec(memory_space=pltpu.VMEM)
    out = jax.ShapeDtypeStruct((EX, EX), F32)
    return pl.pallas_call(
        final_kernel,
        out_shape=(out, out),
        in_specs=[vmem] * 2,
        out_specs=(vmem, vmem),
        compiler_params=pltpu.CompilerParams(vmem_limit_bytes=8 << 20),
        name="solve",
    )(totals, ridge)


def exchange(value, count, flip):
    return lax.ppermute(value, "chan", [(i, i ^ flip) for i in range(count)])


def gather(value, count, first, second):
    received = exchange(value, count, first)
    return [value, exchange(value, count, second), received, exchange(received, count, second)]


def exchange_across(value, count):
    pairs = [(g * count + i, (1 - g) * count + i) for g in range(2) for i in range(count)]
    return lax.ppermute(value, ("rows", "chan"), pairs)


def local_packed(count, activations, cotangents, ordering, ridge):
    x = jnp.transpose(activations, (1, 2, 0, 3)).reshape(SIDE * SIDE, EX, CH)
    xo, go = prep(ordering, x, cotangents)
    x_all, x_piv = unpack(gather(xo, count, 2, 1), "unpack_x")
    x_cross = exchange_across(x_piv, count)
    g_all, g_piv = unpack(gather(go, count, 8, 4), "unpack_g")
    g_cross = exchange_across(g_piv, count)
    height = EX + PIV_DEV
    own_term, ridge = terms(
        own_kernel,
        (x_all, g_all, x_piv, g_piv, ridge.reshape(1, EX)),
        ((EX, LANES), (1, EX)),
        scratch_of(EX, 3 * LANES) + scratch_of(EX, LANES) + [pltpu.VMEM(product_shape(EX), F32)],
        11 * 10**9,
        "terms_own",
    )
    products, = terms(
        cross_inputs_kernel, (x_all, x_cross), (product_shape(height),), scratch_of(height, 3 * LANES), 8 * 10**9, "cross_inputs"
    )
    term, = terms(
        cross_kernel, (products, g_all, g_cross, own_term), ((16, LANES),), scratch_of(height, LANES), 8 * 10**9, "terms_cross"
    )
    quads = [[4 * i + k for k in range(4)] for i in range(count // 4)]
    lines = [[4 * i + k for i in range(count // 4)] for k in range(4)]
    parts = lax.all_gather(term, "chan", axis_index_groups=quads)
    part = (parts[0] + parts[1]) + (parts[2] + parts[3])
    return final(lax.all_gather(part, "chan", axis_index_groups=lines), ridge)


def jacobian_block(grad_rows, input_rows):
    example_count = input_rows.shape[0]
    side_len = input_rows.shape[1]
    channel_count = input_rows.shape[3]
    grad_count = grad_rows.shape[1]
    grid_grads = grad_rows.reshape(example_count, grad_count, side_len, side_len)
    padded_grads = jnp.pad(grid_grads, ((0, 0), (0, 0), (1, 1), (1, 1)))
    shifted = []
    for row_shift in range(3):
        for col_shift in range(3):
            window = padded_grads[
                :,
                :,
                2 - row_shift : 2 - row_shift + side_len,
                2 - col_shift : 2 - col_shift + side_len,
            ]
            shifted.append(window.reshape(example_count, grad_count, side_len * side_len))
    stacked_grads = jnp.stack(shifted, axis=2).reshape(
        example_count, grad_count * 9, side_len * side_len
    )
    flat_inputs = input_rows.reshape(example_count, side_len * side_len, channel_count)
    product = jnp.einsum(
        "nkp,npq->nkq", stacked_grads, flat_inputs, preferred_element_type=jnp.float32
    )
    return product.astype(jnp.bfloat16).reshape(example_count, -1)


def gram_block(left_rows, right_rows):
    return lax.dot_general(
        left_rows, right_rows, (((1,), (1,)), ((), ())), preferred_element_type=jnp.float32
    )


def local(activations, cotangents, ordering, ridge):
    local_order = ordering[0]
    own_inputs = jnp.take(activations, local_order, axis=0)
    own_grads = jnp.take(cotangents, local_order, axis=0)
    pivot_count = PIV_DEV
    pivot_inputs, pivot_grads = (
        lax.all_gather(own_inputs[:pivot_count], "rows", axis=0, tiled=True),
        lax.all_gather(own_grads[:pivot_count], "rows", axis=0, tiled=True),
    )
    full_own, full_pivot = (
        lax.all_gather(own_inputs, "chan", axis=3, tiled=True),
        lax.all_gather(pivot_inputs, "chan", axis=3, tiled=True),
    )
    own_jac = jacobian_block(own_grads, full_own)
    pivot_jac = jacobian_block(pivot_grads, full_pivot)
    partial_panel = gram_block(own_jac, pivot_jac)
    gram_panel = lax.psum(partial_panel, "chan")
    diag_block = lax.all_gather(gram_panel[:pivot_count], "rows", axis=0, tiled=True)
    system = 0.5 * (diag_block + diag_block.T) + jnp.diag(ridge)
    lower = jnp.linalg.cholesky(system)
    factor_panel = jax.scipy.linalg.solve_triangular(lower, gram_panel.T, lower=True).T
    return (gram_panel, factor_panel)


def solution(mesh):
    row_groups, count = mesh.shape["rows"], mesh.shape["chan"]
    packed = row_groups == 2 and count == 16
    return jax.shard_map(
        functools.partial(local_packed, count) if packed else local,
        mesh=mesh,
        in_specs=(P("rows", None, None, "chan"), P("rows", "chan", None), P("rows", None), P()),
        out_specs=(P("rows", None), P("rows", None)),
        check_vma=False,
    )
```

```python
import functools

import jax
import jax.numpy as jnp
from jax import lax
from jax.experimental import pallas as pl
from jax.experimental.pallas import tpu as pltpu
from jax.sharding import PartitionSpec as P

PIV_DEV = 16

SIDE = 7
PITCH = 8
GROUPS4 = 14
CH = 32
EX = 32
LANES = 128
F32 = jnp.float32
BF16 = jnp.bfloat16


def fetch(sources, targets, sems):
    copies = [pltpu.make_async_copy(a, b, sems.at[i]) for i, (a, b) in enumerate(zip(sources, targets))]
    for copy in copies:
        copy.start()
    return copies


def prep_kernel(order_hbm, x_hbm, g_hbm, xo_ref, go_ref, order_ref, x_ref, g_ref, sems, gs, gt, gout):
    copies = fetch((order_hbm, g_hbm, x_hbm), (order_ref, g_ref, x_ref), sems)
    copies[0].wait()
    copies[1].wait()
    row_id = lax.broadcasted_iota(jnp.int32, (EX, EX), 0)
    col_id = lax.broadcasted_iota(jnp.int32, (EX, EX), 1)
    onehot = jnp.zeros((EX, EX), F32)
    for k in range(EX):
        example = order_ref[0, k]
        onehot = jnp.where((row_id == k) & (col_id == example), 1.0, onehot)
        gs[k * CH:(k + 1) * CH, 0:SIDE * SIDE] = g_ref[example].astype(F32)
    block_id = lax.broadcasted_iota(jnp.int32, (GROUPS4, LANES), 1) // CH
    for quad in range(EX // 4):
        flipped = jnp.transpose(gs[quad * LANES:(quad + 1) * LANES, :])
        for py in range(SIDE):
            gt[py * PITCH:py * PITCH + SIDE, :] = flipped[py * SIDE:(py + 1) * SIDE, :]
            gt[py * PITCH + SIDE:(py + 1) * PITCH, :] = jnp.zeros((1, LANES), F32)
        parts = [gt[pl.ds(j, GROUPS4, stride=4), :] for j in range(4)]
        for e in range(4):
            merged = jnp.zeros((GROUPS4, LANES), F32)
            for j in range(4):
                shift = (CH * (j - e)) % LANES
                moved = pltpu.roll(parts[j], shift, 1) if shift else parts[j]
                merged = jnp.where(block_id == j, moved, merged)
            gout[pl.ds(quad * 4 + e, GROUPS4, stride=EX), :] = merged
    for group in range(GROUPS4):
        go_ref[group] = gout[group * EX:(group + 1) * EX, :].astype(BF16)
    copies[2].wait()
    onehot = onehot.astype(BF16)
    zero_block = jnp.zeros((EX, CH), BF16)
    for group in range(GROUPS4):
        pieces = []
        for j in range(4):
            py, px = group // 2, (group % 2) * 4 + j
            pieces.append(x_ref[py * SIDE + px] if px < SIDE else zero_block)
        packed = jnp.concatenate(pieces, axis=1)
        xo_ref[group] = jnp.dot(onehot, packed, preferred_element_type=F32).astype(BF16)


def prep(order, x, g):
    full = jax.ShapeDtypeStruct((GROUPS4, EX, LANES), BF16)
    vmem = pl.BlockSpec(memory_space=pltpu.VMEM)
    return pl.pallas_call(
        prep_kernel,
        out_shape=(full, full),
        in_specs=[pl.BlockSpec(memory_space=pltpu.HBM)] * 3,
        out_specs=(vmem,) * 2,
        scratch_shapes=[
            pltpu.SMEM(order.shape, order.dtype),
            pltpu.VMEM(x.shape, x.dtype),
            pltpu.VMEM(g.shape, g.dtype),
            pltpu.SemaphoreType.DMA((3,)),
            pltpu.VMEM((EX * CH, LANES), F32),
            pltpu.VMEM((SIDE * PITCH, LANES), F32),
            pltpu.VMEM((GROUPS4 * EX, LANES), F32),
        ],
        compiler_params=pltpu.CompilerParams(vmem_limit_bytes=54848 << 10),
        name="prep",
    )(order, x, g)


SPOTS = SIDE * SIDE
COLB = PITCH * PIV_DEV


def cost(flops, moved):
    return pl.CostEstimate(flops=flops, bytes_accessed=moved, transcendentals=0)


def unpack_kernel(*refs):
    packed, all_ref, piv_ref = refs[:4], refs[4], refs[5]
    row = lax.broadcasted_iota(jnp.int32, (4 * LANES, 4 * LANES), 0)
    col = lax.broadcasted_iota(jnp.int32, (4 * LANES, 4 * LANES), 1)
    target = (row // CH) % 4 * LANES + row // LANES * CH + row % CH
    move = jnp.where(col == target, 1.0, 0.0).astype(BF16)
    flat = jnp.concatenate([ref[...].reshape(GROUPS4 * EX, LANES) for ref in packed], axis=1)
    moved = jnp.dot(flat, move, preferred_element_type=F32).astype(BF16)
    for group in range(GROUPS4):
        for j in range(4):
            py, px = group // 2, (group % 2) * 4 + j
            if px == SIDE:
                continue
            spot = moved[group * EX:(group + 1) * EX, j * LANES:(j + 1) * LANES]
            all_ref[py * SIDE + px] = spot
            piv_ref[py * SIDE + px] = spot[:PIV_DEV]


def unpack(arrays, name):
    vmem = pl.BlockSpec(memory_space=pltpu.VMEM)
    pivots = jax.ShapeDtypeStruct((SPOTS, PIV_DEV, LANES), BF16)
    return pl.pallas_call(
        unpack_kernel,
        out_shape=(jax.ShapeDtypeStruct((SPOTS, EX, LANES), BF16), pivots),
        in_specs=[vmem] * 4,
        out_specs=(vmem,) * 2,
        compiler_params=pltpu.CompilerParams(vmem_limit_bytes=12 << 20),
        cost_estimate=cost(0, 1 << 20),
        name=name,
    )(*arrays)


CONTRACT = (((1,), (1,)), ((), ()))
SPANS = [(qy, min(qy + 2, SIDE)) for qy in range(0, SIDE, 2)]


def input_products(rows_x, xp, lx, rx, t):
    heights = [ref.shape[1] for ref in rows_x]
    height = sum(heights)
    for py in range(SIDE):
        for px in range(PITCH):
            row, col = (py * SIDE + px) * height, (py * PITCH + px) * PIV_DEV
            for d in range(3):
                from_x = px + d - 1
                inside = 0 <= from_x < SIDE and px < SIDE
                lanes = slice(d * LANES, (d + 1) * LANES)
                spot = py * SIDE + from_x
                rx[col:col + PIV_DEV, lanes] = xp[spot] if inside else jnp.zeros((PIV_DEV, LANES), BF16)
                if px < SIDE:
                    first = row
                    for ref, count in zip(rows_x, heights):
                        lx[first:first + count, lanes] = ref[spot] if inside else jnp.zeros((count, LANES), BF16)
                        first += count
    block = SIDE * height
    for start, stop in SPANS:
        right = rx[start * COLB:stop * COLB, :]
        for py in range(SIDE):
            left = lx[py * block:(py + 1) * block, :]
            t[py, :, start * COLB:stop * COLB] = lax.dot_general(left, right, CONTRACT, preferred_element_type=F32)


def panel_terms(rows_g, gp, lg, rg, t):
    heights = [ref.shape[1] for ref in rows_g]
    height = sum(heights)
    for py in range(SIDE):
        for px in range(PITCH):
            row, col = (py * SIDE + px) * height, (py * PITCH + px) * PIV_DEV
            rg[col:col + PIV_DEV, :] = gp[py * SIDE + px] if px < SIDE else jnp.zeros((PIV_DEV, LANES), BF16)
            if px < SIDE:
                first = row
                for ref, count in zip(rows_g, heights):
                    lg[first:first + count, :] = ref[py * SIDE + px]
                    first += count
    block = SIDE * height
    acc = jnp.zeros((height, COLB), F32)
    for start, stop in SPANS:
        right = rg[start * COLB:stop * COLB, :]
        for py in range(SIDE):
            left = lg[py * block:(py + 1) * block, :]
            gg = lax.dot_general(left, right, CONTRACT, preferred_element_type=F32)
            for qy in range(start, stop):
                for px in range(SIDE):
                    rows = slice(px * height, (px + 1) * height)
                    total = t[py, rows, qy * COLB:(qy + 1) * COLB]
                    if py > 0 and qy > 0:
                        total = total + t[py - 1, rows, (qy - 1) * COLB:qy * COLB]
                    if py < SIDE - 1 and qy < SIDE - 1:
                        total = total + t[py + 1, rows, (qy + 1) * COLB:(qy + 2) * COLB]
                    acc = acc + gg[rows, (qy - start) * COLB:(qy - start + 1) * COLB] * total
    acc = acc + pltpu.roll(acc, 64, 1)
    acc = acc + pltpu.roll(acc, 32, 1)
    return acc + pltpu.roll(acc, 16, 1)


def own_kernel(x, g, xp, gp, out_ref, lx, rx, lg, rg, t):
    input_products([x], xp, lx, rx, t)
    out_ref[...] = panel_terms([g], gp, lg, rg, t)


def cross_inputs_kernel(x, xp, t_out, lx, rx):
    input_products([x], xp, lx, rx, t_out)


def cross_kernel(t, g, gp, own_ref, ridge, out_ref, ridge_out, lg, rg):
    ridge_out[...] = ridge[...]
    across = panel_terms([g], gp, lg, rg, t)
    lane = lax.broadcasted_iota(jnp.int32, (8, LANES), 1)
    is_own = (lane // PIV_DEV) % 2 == lax.axis_index("rows")
    packed = jnp.zeros((8, LANES), F32)
    for j in range(4):
        rows = slice(8 * j, 8 * j + 8)
        packed = jnp.where(lane // EX == j, jnp.where(is_own, own_ref[rows, :], across[rows]), packed)
    out_ref[...] = packed


def product_shape(height):
    return (SIDE, SIDE * height, SIDE * COLB)


def scratch_of(height, width):
    return [pltpu.VMEM((SPOTS * height, width), BF16), pltpu.VMEM((SIDE * COLB, width), BF16)]


def terms(kernel, arrays, shapes, scratch, flops, name):
    vmem = pl.BlockSpec(memory_space=pltpu.VMEM)
    return pl.pallas_call(
        kernel,
        out_shape=tuple(jax.ShapeDtypeStruct(shape, F32) for shape in shapes),
        in_specs=[vmem] * len(arrays),
        out_specs=(vmem,) * len(shapes),
        scratch_shapes=scratch,
        compiler_params=pltpu.CompilerParams(vmem_limit_bytes=20 << 20),
        cost_estimate=cost(flops, 4 << 20),
        name=name,
    )(*arrays)


def rows_of(packed, count):
    return jnp.concatenate(
        [packed[:, EX * j:EX * (j + 1)] for j in range(count)], axis=0
    )


def tree_sum(values):
    while len(values) > 1:
        values = [a + b for a, b in zip(values[0::2], values[1::2])]
    return values[0]


def final_kernel(terms_ref, ridge_ref, gram_ref, factor_ref):
    count = terms_ref.shape[0] // 2
    sums = [tree_sum([terms_ref[g * count + i] for i in range(count)]) for g in range(2)]
    panel = rows_of(jnp.where(lax.axis_index("rows") == 0, sums[0], sums[1]), 4)
    gram_ref[...] = panel
    diag = jnp.concatenate([rows_of(total, 2) for total in sums], axis=0)
    row_id = lax.broadcasted_iota(jnp.int32, (EX, EX), 0)
    col_id = lax.broadcasted_iota(jnp.int32, (EX, EX), 1)
    ridge = jnp.where(row_id == col_id, jnp.broadcast_to(ridge_ref[...], (EX, EX)), 0.0)
    system = 0.5 * (diag + jnp.transpose(diag)) + ridge
    factor = jnp.zeros((EX, EX), F32)
    step = 4
    for j in range(0, EX, step):
        sys_cols = [jnp.broadcast_to(system[:, j + k:j + k + 1], (EX, EX)) for k in range(step)]
        pan_cols = [jnp.broadcast_to(panel[:, j + k:j + k + 1], (EX, EX)) for k in range(step)]
        sys_rows = [system[j + k:j + k + 1, :] for k in range(step)]
        for k in range(step):
            scale = lax.rsqrt(sys_cols[k][j + k:j + k + 1, :])
            sys_cols[k], pan_cols[k], sys_rows[k] = sys_cols[k] * scale, pan_cols[k] * scale, sys_rows[k] * scale
            factor = jnp.where(col_id == j + k, pan_cols[k], factor)
            for m in range(k + 1, step):
                entry = sys_cols[k][j + m:j + m + 1, :]
                sys_cols[m] = sys_cols[m] - sys_cols[k] * entry
                pan_cols[m] = pan_cols[m] - pan_cols[k] * entry
                sys_rows[m] = sys_rows[m] - sys_rows[k] * entry
        if j + step < EX:
            for k in range(step):
                system = system - sys_cols[k] * sys_rows[k]
                panel = panel - pan_cols[k] * sys_rows[k]
    factor_ref[...] = factor


def final(terms_of_all, ridge):
    vmem = pl.BlockSpec(memory_space=pltpu.VMEM)
    out = jax.ShapeDtypeStruct((EX, EX), F32)
    return pl.pallas_call(
        final_kernel,
        out_shape=(out, out),
        in_specs=[vmem] * 2,
        out_specs=(vmem, vmem),
        compiler_params=pltpu.CompilerParams(vmem_limit_bytes=8 << 20),
        name="solve",
    )(terms_of_all, ridge)


def exchange(value, count, flip):
    return lax.ppermute(value, "chan", [(i, i ^ flip) for i in range(count)])


def gather(value, count, first, second):
    received = exchange(value, count, first)
    return [value, exchange(value, count, second), received, exchange(received, count, second)]


def exchange_across(value, count):
    pairs = [(g * count + i, (1 - g) * count + i) for g in range(2) for i in range(count)]
    return lax.ppermute(value, ("rows", "chan"), pairs)


def local_packed(count, activations, cotangents, ordering, ridge):
    x = jnp.transpose(activations, (1, 2, 0, 3)).reshape(SIDE * SIDE, EX, CH)
    xo, go = prep(ordering, x, cotangents)
    x_all, x_piv = unpack(gather(xo, count, 2, 1), "unpack_x")
    x_cross = exchange_across(x_piv, count)
    g_all, g_piv = unpack(gather(go, count, 8, 4), "unpack_g")
    g_cross = exchange_across(g_piv, count)
    wide, narrow = scratch_of(EX, 3 * LANES), scratch_of(EX, LANES)
    shape, flops = product_shape(EX), 6 * 10**9
    arrays = (x_all, g_all, x_piv, g_piv)
    own_term, = terms(own_kernel, arrays, ((EX, LANES),), wide + narrow + [pltpu.VMEM(shape, F32)], 2 * flops, "terms_own")
    products, = terms(cross_inputs_kernel, (x_all, x_cross), (shape,), wide, flops, "cross_inputs")
    arrays = (products, g_all, g_cross, own_term, ridge.reshape(1, EX))
    term, ridge = terms(cross_kernel, arrays, ((8, LANES), (1, EX)), narrow, flops, "terms_cross")
    copies = jnp.broadcast_to(term, (2 * count, 8, LANES))
    return final(lax.all_to_all(copies, ("rows", "chan"), 0, 0), ridge)


def jacobian_block(grad_rows, input_rows):
    example_count = input_rows.shape[0]
    side_len = input_rows.shape[1]
    channel_count = input_rows.shape[3]
    grad_count = grad_rows.shape[1]
    grid_grads = grad_rows.reshape(example_count, grad_count, side_len, side_len)
    padded_grads = jnp.pad(grid_grads, ((0, 0), (0, 0), (1, 1), (1, 1)))
    shifted = []
    for row_shift in range(3):
        for col_shift in range(3):
            window = padded_grads[
                :,
                :,
                2 - row_shift : 2 - row_shift + side_len,
                2 - col_shift : 2 - col_shift + side_len,
            ]
            shifted.append(window.reshape(example_count, grad_count, side_len * side_len))
    stacked_grads = jnp.stack(shifted, axis=2).reshape(
        example_count, grad_count * 9, side_len * side_len
    )
    flat_inputs = input_rows.reshape(example_count, side_len * side_len, channel_count)
    product = jnp.einsum(
        "nkp,npq->nkq", stacked_grads, flat_inputs, preferred_element_type=jnp.float32
    )
    return product.astype(jnp.bfloat16).reshape(example_count, -1)


def gram_block(left_rows, right_rows):
    return lax.dot_general(
        left_rows, right_rows, (((1,), (1,)), ((), ())), preferred_element_type=jnp.float32
    )


def local(activations, cotangents, ordering, ridge):
    local_order = ordering[0]
    own_inputs = jnp.take(activations, local_order, axis=0)
    own_grads = jnp.take(cotangents, local_order, axis=0)
    pivot_count = PIV_DEV
    pivot_inputs, pivot_grads = (
        lax.all_gather(own_inputs[:pivot_count], "rows", axis=0, tiled=True),
        lax.all_gather(own_grads[:pivot_count], "rows", axis=0, tiled=True),
    )
    full_own, full_pivot = (
        lax.all_gather(own_inputs, "chan", axis=3, tiled=True),
        lax.all_gather(pivot_inputs, "chan", axis=3, tiled=True),
    )
    own_jac = jacobian_block(own_grads, full_own)
    pivot_jac = jacobian_block(pivot_grads, full_pivot)
    partial_panel = gram_block(own_jac, pivot_jac)
    gram_panel = lax.psum(partial_panel, "chan")
    diag_block = lax.all_gather(gram_panel[:pivot_count], "rows", axis=0, tiled=True)
    system = 0.5 * (diag_block + diag_block.T) + jnp.diag(ridge)
    lower = jnp.linalg.cholesky(system)
    factor_panel = jax.scipy.linalg.solve_triangular(lower, gram_panel.T, lower=True).T
    return (gram_panel, factor_panel)


def solution(mesh):
    row_groups, count = mesh.shape["rows"], mesh.shape["chan"]
    packed = row_groups == 2 and count == 16
    return jax.shard_map(
        functools.partial(local_packed, count) if packed else local,
        mesh=mesh,
        in_specs=(P("rows", None, None, "chan"), P("rows", "chan", None), P("rows", None), P()),
        out_specs=(P("rows", None), P("rows", None)),
        check_vma=False,
    )
```

```python
import functools

import jax
import jax.numpy as jnp
from jax import lax
from jax.experimental import pallas as pl
from jax.experimental.pallas import tpu as pltpu
from jax.sharding import PartitionSpec as P

PIV_DEV = 16

SIDE = 7
PITCH = 8
GROUPS4 = 14
CH = 32
EX = 32
LANES = 128
F32 = jnp.float32
BF16 = jnp.bfloat16


def fetch(sources, targets, sems):
    copies = [pltpu.make_async_copy(a, b, sems.at[i]) for i, (a, b) in enumerate(zip(sources, targets))]
    for copy in copies:
        copy.start()
    return copies


def prep_kernel(order_hbm, x_hbm, g_hbm, xo_ref, go_ref, order_ref, x_ref, g_ref, sems, gs, gt, gout):
    copies = fetch((order_hbm, g_hbm, x_hbm), (order_ref, g_ref, x_ref), sems)
    copies[0].wait()
    copies[1].wait()
    row_id = lax.broadcasted_iota(jnp.int32, (EX, EX), 0)
    col_id = lax.broadcasted_iota(jnp.int32, (EX, EX), 1)
    onehot = jnp.zeros((EX, EX), F32)
    for k in range(EX):
        example = order_ref[0, k]
        onehot = jnp.where((row_id == k) & (col_id == example), 1.0, onehot)
        gs[k * CH:(k + 1) * CH, 0:SIDE * SIDE] = g_ref[example].astype(F32)
    block_id = lax.broadcasted_iota(jnp.int32, (GROUPS4, LANES), 1) // CH
    for quad in range(EX // 4):
        flipped = jnp.transpose(gs[quad * LANES:(quad + 1) * LANES, :])
        for py in range(SIDE):
            gt[py * PITCH:py * PITCH + SIDE, :] = flipped[py * SIDE:(py + 1) * SIDE, :]
            gt[py * PITCH + SIDE:(py + 1) * PITCH, :] = jnp.zeros((1, LANES), F32)
        parts = [gt[pl.ds(j, GROUPS4, stride=4), :] for j in range(4)]
        for e in range(4):
            merged = jnp.zeros((GROUPS4, LANES), F32)
            for j in range(4):
                shift = (CH * (j - e)) % LANES
                moved = pltpu.roll(parts[j], shift, 1) if shift else parts[j]
                merged = jnp.where(block_id == j, moved, merged)
            gout[pl.ds(quad * 4 + e, GROUPS4, stride=EX), :] = merged
    for group in range(GROUPS4):
        go_ref[group] = gout[group * EX:(group + 1) * EX, :].astype(BF16)
    copies[2].wait()
    onehot = onehot.astype(BF16)
    zero_block = jnp.zeros((EX, CH), BF16)
    for group in range(GROUPS4):
        pieces = []
        for j in range(4):
            py, px = group // 2, (group % 2) * 4 + j
            pieces.append(x_ref[py * SIDE + px] if px < SIDE else zero_block)
        packed = jnp.concatenate(pieces, axis=1)
        xo_ref[group] = jnp.dot(onehot, packed, preferred_element_type=F32).astype(BF16)


def prep(order, x, g):
    full = jax.ShapeDtypeStruct((GROUPS4, EX, LANES), BF16)
    vmem = pl.BlockSpec(memory_space=pltpu.VMEM)
    return pl.pallas_call(
        prep_kernel,
        out_shape=(full, full),
        in_specs=[pl.BlockSpec(memory_space=pltpu.HBM)] * 3,
        out_specs=(vmem,) * 2,
        scratch_shapes=[
            pltpu.SMEM(order.shape, order.dtype),
            pltpu.VMEM(x.shape, x.dtype),
            pltpu.VMEM(g.shape, g.dtype),
            pltpu.SemaphoreType.DMA((3,)),
            pltpu.VMEM((EX * CH, LANES), F32),
            pltpu.VMEM((SIDE * PITCH, LANES), F32),
            pltpu.VMEM((GROUPS4 * EX, LANES), F32),
        ],
        compiler_params=pltpu.CompilerParams(vmem_limit_bytes=54848 << 10),
        name="prep",
    )(order, x, g)


SPOTS = SIDE * SIDE
COLB = PITCH * PIV_DEV


def cost(flops, moved):
    return pl.CostEstimate(flops=flops, bytes_accessed=moved, transcendentals=0)


def unpack_kernel(*refs):
    packed, all_ref, piv_ref = refs[:4], refs[4], refs[5]
    row = lax.broadcasted_iota(jnp.int32, (4 * LANES, 4 * LANES), 0)
    col = lax.broadcasted_iota(jnp.int32, (4 * LANES, 4 * LANES), 1)
    target = (row // CH) % 4 * LANES + row // LANES * CH + row % CH
    move = jnp.where(col == target, 1.0, 0.0).astype(BF16)
    flat = jnp.concatenate([ref[...].reshape(GROUPS4 * EX, LANES) for ref in packed], axis=1)
    moved = jnp.dot(flat, move, preferred_element_type=F32).astype(BF16)
    for group in range(GROUPS4):
        for j in range(4):
            py, px = group // 2, (group % 2) * 4 + j
            if px == SIDE:
                continue
            spot = moved[group * EX:(group + 1) * EX, j * LANES:(j + 1) * LANES]
            all_ref[py * SIDE + px] = spot
            piv_ref[py * SIDE + px] = spot[:PIV_DEV]


def unpack(arrays, name):
    vmem = pl.BlockSpec(memory_space=pltpu.VMEM)
    pivots = jax.ShapeDtypeStruct((SPOTS, PIV_DEV, LANES), BF16)
    return pl.pallas_call(
        unpack_kernel,
        out_shape=(jax.ShapeDtypeStruct((SPOTS, EX, LANES), BF16), pivots),
        in_specs=[vmem] * 4,
        out_specs=(vmem,) * 2,
        compiler_params=pltpu.CompilerParams(vmem_limit_bytes=12 << 20),
        cost_estimate=cost(0, 1 << 20),
        name=name,
    )(*arrays)


CONTRACT = (((1,), (1,)), ((), ()))
SPANS = [(qy, min(qy + 2, SIDE)) for qy in range(0, SIDE, 2)]


def input_products(rows_x, xp, lx, rx, t):
    heights = [ref.shape[1] for ref in rows_x]
    height = sum(heights)
    for py in range(SIDE):
        for px in range(PITCH):
            row, col = (py * SIDE + px) * height, (py * PITCH + px) * PIV_DEV
            for d in range(3):
                from_x = px + d - 1
                inside = 0 <= from_x < SIDE and px < SIDE
                lanes = slice(d * LANES, (d + 1) * LANES)
                spot = py * SIDE + from_x
                rx[col:col + PIV_DEV, lanes] = xp[spot] if inside else jnp.zeros((PIV_DEV, LANES), BF16)
                if px < SIDE:
                    first = row
                    for ref, count in zip(rows_x, heights):
                        lx[first:first + count, lanes] = ref[spot] if inside else jnp.zeros((count, LANES), BF16)
                        first += count
    block = SIDE * height
    for start, stop in SPANS:
        right = rx[start * COLB:stop * COLB, :]
        for py in range(SIDE):
            left = lx[py * block:(py + 1) * block, :]
            t[py, :, start * COLB:stop * COLB] = lax.dot_general(left, right, CONTRACT, preferred_element_type=F32)


def panel_terms(rows_g, gp, lg, rg, t):
    heights = [ref.shape[1] for ref in rows_g]
    height = sum(heights)
    for py in range(SIDE):
        for px in range(PITCH):
            row, col = (py * SIDE + px) * height, (py * PITCH + px) * PIV_DEV
            rg[col:col + PIV_DEV, :] = gp[py * SIDE + px] if px < SIDE else jnp.zeros((PIV_DEV, LANES), BF16)
            if px < SIDE:
                first = row
                for ref, count in zip(rows_g, heights):
                    lg[first:first + count, :] = ref[py * SIDE + px]
                    first += count
    block = SIDE * height
    acc = jnp.zeros((height, COLB), F32)
    for start, stop in SPANS:
        right = rg[start * COLB:stop * COLB, :]
        for py in range(SIDE):
            left = lg[py * block:(py + 1) * block, :]
            gg = lax.dot_general(left, right, CONTRACT, preferred_element_type=F32)
            for qy in range(start, stop):
                for px in range(SIDE):
                    rows = slice(px * height, (px + 1) * height)
                    total = t[py, rows, qy * COLB:(qy + 1) * COLB]
                    if py > 0 and qy > 0:
                        total = total + t[py - 1, rows, (qy - 1) * COLB:qy * COLB]
                    if py < SIDE - 1 and qy < SIDE - 1:
                        total = total + t[py + 1, rows, (qy + 1) * COLB:(qy + 2) * COLB]
                    acc = acc + gg[rows, (qy - start) * COLB:(qy - start + 1) * COLB] * total
    acc = acc + pltpu.roll(acc, 64, 1)
    acc = acc + pltpu.roll(acc, 32, 1)
    return acc + pltpu.roll(acc, 16, 1)


def products_kernel(x, xp, t_out, lx, rx):
    input_products([x], xp, lx, rx, t_out)


def own_kernel(t, g, gp, out_ref, lg, rg):
    out_ref[...] = panel_terms([g], gp, lg, rg, t)


def cross_kernel(t, g, gp, own_ref, ridge, out_ref, ridge_out, lg, rg):
    ridge_out[...] = ridge[...]
    across = panel_terms([g], gp, lg, rg, t)
    lane = lax.broadcasted_iota(jnp.int32, (8, LANES), 1)
    is_own = (lane // PIV_DEV) % 2 == lax.axis_index("rows")
    packed = jnp.zeros((8, LANES), F32)
    for j in range(4):
        rows = slice(8 * j, 8 * j + 8)
        packed = jnp.where(lane // EX == j, jnp.where(is_own, own_ref[rows, :], across[rows]), packed)
    out_ref[...] = packed


def product_shape(height):
    return (SIDE, SIDE * height, SIDE * COLB)


def scratch_of(height, width):
    return [pltpu.VMEM((SPOTS * height, width), BF16), pltpu.VMEM((SIDE * COLB, width), BF16)]


def terms(kernel, arrays, shapes, scratch, flops, name):
    vmem = pl.BlockSpec(memory_space=pltpu.VMEM)
    return pl.pallas_call(
        kernel,
        out_shape=tuple(jax.ShapeDtypeStruct(shape, F32) for shape in shapes),
        in_specs=[vmem] * len(arrays),
        out_specs=(vmem,) * len(shapes),
        scratch_shapes=scratch,
        compiler_params=pltpu.CompilerParams(vmem_limit_bytes=20 << 20),
        cost_estimate=cost(flops, 4 << 20),
        name=name,
    )(*arrays)


def rows_of(packed, count):
    return jnp.concatenate(
        [packed[:, EX * j:EX * (j + 1)] for j in range(count)], axis=0
    )


def tree_sum(values):
    while len(values) > 1:
        values = [a + b for a, b in zip(values[0::2], values[1::2])]
    return values[0]


def final_kernel(terms_ref, ridge_ref, gram_ref, factor_ref):
    count = terms_ref.shape[0] // 2
    sums = [tree_sum([terms_ref[g * count + i] for i in range(count)]) for g in range(2)]
    panel = rows_of(jnp.where(lax.axis_index("rows") == 0, sums[0], sums[1]), 4)
    gram_ref[...] = panel
    diag = jnp.concatenate([rows_of(total, 2) for total in sums], axis=0)
    row_id = lax.broadcasted_iota(jnp.int32, (EX, EX), 0)
    col_id = lax.broadcasted_iota(jnp.int32, (EX, EX), 1)
    ridge = jnp.where(row_id == col_id, jnp.broadcast_to(ridge_ref[...], (EX, EX)), 0.0)
    system = 0.5 * (diag + jnp.transpose(diag)) + ridge
    factor = jnp.zeros((EX, EX), F32)
    step = 4
    for j in range(0, EX, step):
        sys_cols = [jnp.broadcast_to(system[:, j + k:j + k + 1], (EX, EX)) for k in range(step)]
        pan_cols = [jnp.broadcast_to(panel[:, j + k:j + k + 1], (EX, EX)) for k in range(step)]
        sys_rows = [system[j + k:j + k + 1, :] for k in range(step)]
        for k in range(step):
            scale = lax.rsqrt(sys_cols[k][j + k:j + k + 1, :])
            sys_cols[k], pan_cols[k], sys_rows[k] = sys_cols[k] * scale, pan_cols[k] * scale, sys_rows[k] * scale
            factor = jnp.where(col_id == j + k, pan_cols[k], factor)
            for m in range(k + 1, step):
                entry = sys_cols[k][j + m:j + m + 1, :]
                sys_cols[m] = sys_cols[m] - sys_cols[k] * entry
                pan_cols[m] = pan_cols[m] - pan_cols[k] * entry
                sys_rows[m] = sys_rows[m] - sys_rows[k] * entry
        if j + step < EX:
            for k in range(step):
                system = system - sys_cols[k] * sys_rows[k]
                panel = panel - pan_cols[k] * sys_rows[k]
    factor_ref[...] = factor


def final(terms_of_all, ridge):
    vmem = pl.BlockSpec(memory_space=pltpu.VMEM)
    out = jax.ShapeDtypeStruct((EX, EX), F32)
    return pl.pallas_call(
        final_kernel,
        out_shape=(out, out),
        in_specs=[vmem] * 2,
        out_specs=(vmem, vmem),
        compiler_params=pltpu.CompilerParams(vmem_limit_bytes=8 << 20),
        name="solve",
    )(terms_of_all, ridge)


def exchange(value, count, flip):
    return lax.ppermute(value, "chan", [(i, i ^ flip) for i in range(count)])


def gather(value, count, first, second):
    received = exchange(value, count, first)
    return [value, exchange(value, count, second), received, exchange(received, count, second)]


def exchange_across(value, count):
    pairs = [(g * count + i, (1 - g) * count + i) for g in range(2) for i in range(count)]
    return lax.ppermute(value, ("rows", "chan"), pairs)


def local_packed(count, activations, cotangents, ordering, ridge):
    x = jnp.transpose(activations, (1, 2, 0, 3)).reshape(SIDE * SIDE, EX, CH)
    xo, go = prep(ordering, x, cotangents)
    x_all, x_piv = unpack(gather(xo, count, 2, 1), "unpack_x")
    x_cross = exchange_across(x_piv, count)
    g_all, g_piv = unpack(gather(go, count, 8, 4), "unpack_g")
    g_cross = exchange_across(g_piv, count)
    wide, narrow = scratch_of(EX, 3 * LANES), scratch_of(EX, LANES)
    shape, flops = product_shape(EX), 6 * 10**9
    products, = terms(products_kernel, (x_all, x_piv), (shape,), wide, flops, "own_inputs")
    own_term, = terms(own_kernel, (products, g_all, g_piv), ((EX, LANES),), narrow, flops, "terms_own")
    products, = terms(products_kernel, (x_all, x_cross), (shape,), wide, flops, "cross_inputs")
    arrays = (products, g_all, g_cross, own_term, ridge.reshape(1, EX))
    term, ridge = terms(cross_kernel, arrays, ((8, LANES), (1, EX)), narrow, flops, "terms_cross")
    return final(lax.all_gather(term, ("rows", "chan")), ridge)


def jacobian_block(grad_rows, input_rows):
    example_count = input_rows.shape[0]
    side_len = input_rows.shape[1]
    channel_count = input_rows.shape[3]
    grad_count = grad_rows.shape[1]
    grid_grads = grad_rows.reshape(example_count, grad_count, side_len, side_len)
    padded_grads = jnp.pad(grid_grads, ((0, 0), (0, 0), (1, 1), (1, 1)))
    shifted = []
    for row_shift in range(3):
        for col_shift in range(3):
            window = padded_grads[
                :,
                :,
                2 - row_shift : 2 - row_shift + side_len,
                2 - col_shift : 2 - col_shift + side_len,
            ]
            shifted.append(window.reshape(example_count, grad_count, side_len * side_len))
    stacked_grads = jnp.stack(shifted, axis=2).reshape(
        example_count, grad_count * 9, side_len * side_len
    )
    flat_inputs = input_rows.reshape(example_count, side_len * side_len, channel_count)
    product = jnp.einsum(
        "nkp,npq->nkq", stacked_grads, flat_inputs, preferred_element_type=jnp.float32
    )
    return product.astype(jnp.bfloat16).reshape(example_count, -1)


def gram_block(left_rows, right_rows):
    return lax.dot_general(
        left_rows, right_rows, (((1,), (1,)), ((), ())), preferred_element_type=jnp.float32
    )


def local(activations, cotangents, ordering, ridge):
    local_order = ordering[0]
    own_inputs = jnp.take(activations, local_order, axis=0)
    own_grads = jnp.take(cotangents, local_order, axis=0)
    pivot_count = PIV_DEV
    pivot_inputs, pivot_grads = (
        lax.all_gather(own_inputs[:pivot_count], "rows", axis=0, tiled=True),
        lax.all_gather(own_grads[:pivot_count], "rows", axis=0, tiled=True),
    )
    full_own, full_pivot = (
        lax.all_gather(own_inputs, "chan", axis=3, tiled=True),
        lax.all_gather(pivot_inputs, "chan", axis=3, tiled=True),
    )
    own_jac = jacobian_block(own_grads, full_own)
    pivot_jac = jacobian_block(pivot_grads, full_pivot)
    partial_panel = gram_block(own_jac, pivot_jac)
    gram_panel = lax.psum(partial_panel, "chan")
    diag_block = lax.all_gather(gram_panel[:pivot_count], "rows", axis=0, tiled=True)
    system = 0.5 * (diag_block + diag_block.T) + jnp.diag(ridge)
    lower = jnp.linalg.cholesky(system)
    factor_panel = jax.scipy.linalg.solve_triangular(lower, gram_panel.T, lower=True).T
    return (gram_panel, factor_panel)


def solution(mesh):
    row_groups, count = mesh.shape["rows"], mesh.shape["chan"]
    packed = row_groups == 2 and count == 16
    return jax.shard_map(
        functools.partial(local_packed, count) if packed else local,
        mesh=mesh,
        in_specs=(P("rows", None, None, "chan"), P("rows", "chan", None), P("rows", None), P()),
        out_specs=(P("rows", None), P("rows", None)),
        check_vma=False,
    )
```

```python
import functools

import jax
import jax.numpy as jnp
from jax import lax
from jax.experimental import pallas as pl
from jax.experimental.pallas import tpu as pltpu
from jax.sharding import PartitionSpec as P

PIV_DEV = 16

SIDE = 7
PITCH = 8
GROUPS4 = 14
CH = 32
EX = 32
LANES = 128
F32 = jnp.float32
BF16 = jnp.bfloat16


def fetch(sources, targets, sems):
    copies = [pltpu.make_async_copy(a, b, sems.at[i]) for i, (a, b) in enumerate(zip(sources, targets))]
    for copy in copies:
        copy.start()
    return copies


def prep_kernel(order_hbm, x_hbm, g_hbm, xo_ref, go_ref, order_ref, x_ref, g_ref, sems, gs, gt, gout):
    copies = fetch((order_hbm, g_hbm, x_hbm), (order_ref, g_ref, x_ref), sems)
    copies[0].wait()
    copies[1].wait()
    row_id = lax.broadcasted_iota(jnp.int32, (EX, EX), 0)
    col_id = lax.broadcasted_iota(jnp.int32, (EX, EX), 1)
    onehot = jnp.zeros((EX, EX), F32)
    for k in range(EX):
        example = order_ref[0, k]
        onehot = jnp.where((row_id == k) & (col_id == example), 1.0, onehot)
        gs[k * CH:(k + 1) * CH, 0:SIDE * SIDE] = g_ref[example].astype(F32)
    block_id = lax.broadcasted_iota(jnp.int32, (GROUPS4, LANES), 1) // CH
    for quad in range(EX // 4):
        flipped = jnp.transpose(gs[quad * LANES:(quad + 1) * LANES, :])
        for py in range(SIDE):
            gt[py * PITCH:py * PITCH + SIDE, :] = flipped[py * SIDE:(py + 1) * SIDE, :]
            gt[py * PITCH + SIDE:(py + 1) * PITCH, :] = jnp.zeros((1, LANES), F32)
        parts = [gt[pl.ds(j, GROUPS4, stride=4), :] for j in range(4)]
        for e in range(4):
            merged = jnp.zeros((GROUPS4, LANES), F32)
            for j in range(4):
                shift = (CH * (j - e)) % LANES
                moved = pltpu.roll(parts[j], shift, 1) if shift else parts[j]
                merged = jnp.where(block_id == j, moved, merged)
            gout[pl.ds(quad * 4 + e, GROUPS4, stride=EX), :] = merged
    for group in range(GROUPS4):
        go_ref[group] = gout[group * EX:(group + 1) * EX, :].astype(BF16)
    copies[2].wait()
    onehot = onehot.astype(BF16)
    zero_block = jnp.zeros((EX, CH), BF16)
    for group in range(GROUPS4):
        pieces = []
        for j in range(4):
            py, px = group // 2, (group % 2) * 4 + j
            pieces.append(x_ref[py * SIDE + px] if px < SIDE else zero_block)
        packed = jnp.concatenate(pieces, axis=1)
        xo_ref[group] = jnp.dot(onehot, packed, preferred_element_type=F32).astype(BF16)


def prep(order, x, g):
    full = jax.ShapeDtypeStruct((GROUPS4, EX, LANES), BF16)
    vmem = pl.BlockSpec(memory_space=pltpu.VMEM)
    return pl.pallas_call(
        prep_kernel,
        out_shape=(full, full),
        in_specs=[pl.BlockSpec(memory_space=pltpu.HBM)] * 3,
        out_specs=(vmem,) * 2,
        scratch_shapes=[
            pltpu.SMEM(order.shape, order.dtype),
            pltpu.VMEM(x.shape, x.dtype),
            pltpu.VMEM(g.shape, g.dtype),
            pltpu.SemaphoreType.DMA((3,)),
            pltpu.VMEM((EX * CH, LANES), F32),
            pltpu.VMEM((SIDE * PITCH, LANES), F32),
            pltpu.VMEM((GROUPS4 * EX, LANES), F32),
        ],
        compiler_params=pltpu.CompilerParams(vmem_limit_bytes=54848 << 10),
        name="prep",
    )(order, x, g)


SPOTS = SIDE * SIDE
COLB = PITCH * PIV_DEV


def cost(flops, moved):
    return pl.CostEstimate(flops=flops, bytes_accessed=moved, transcendentals=0)


def unpack_kernel(*refs):
    packed, (all_ref, piv_ref) = refs[:4], refs[-2:]
    row = lax.broadcasted_iota(jnp.int32, (4 * LANES, 4 * LANES), 0)
    col = lax.broadcasted_iota(jnp.int32, (4 * LANES, 4 * LANES), 1)
    target = (row // CH) % 4 * LANES + row // LANES * CH + row % CH
    move = jnp.where(col == target, 1.0, 0.0).astype(BF16)
    flat = jnp.concatenate([ref[...].reshape(GROUPS4 * EX, LANES) for ref in packed], axis=1)
    moved = jnp.dot(flat, move, preferred_element_type=F32).astype(BF16)
    for group in range(GROUPS4):
        for j in range(4):
            py, px = group // 2, (group % 2) * 4 + j
            if px == SIDE:
                continue
            spot = moved[group * EX:(group + 1) * EX, j * LANES:(j + 1) * LANES]
            all_ref[py * SIDE + px] = spot
            piv_ref[py * SIDE + px] = spot[:PIV_DEV]


def unpack(arrays, name, after=()):
    vmem = pl.BlockSpec(memory_space=pltpu.VMEM)
    pivots = jax.ShapeDtypeStruct((SPOTS, PIV_DEV, LANES), BF16)
    return pl.pallas_call(
        unpack_kernel,
        out_shape=(jax.ShapeDtypeStruct((SPOTS, EX, LANES), BF16), pivots),
        in_specs=[vmem] * 4 + [pl.BlockSpec(memory_space=pl.ANY)] * len(after),
        out_specs=(vmem,) * 2,
        compiler_params=pltpu.CompilerParams(vmem_limit_bytes=12 << 20),
        cost_estimate=cost(0, 1 << 20),
        name=name,
    )(*arrays, *after)


CONTRACT = (((1,), (1,)), ((), ()))
SPANS = [(qy, min(qy + 2, SIDE)) for qy in range(0, SIDE, 2)]


def input_products(rows_x, xp, lx, rx, t):
    heights = [ref.shape[1] for ref in rows_x]
    height = sum(heights)
    for py in range(SIDE):
        for px in range(PITCH):
            row, col = (py * SIDE + px) * height, (py * PITCH + px) * PIV_DEV
            for d in range(3):
                from_x = px + d - 1
                inside = 0 <= from_x < SIDE and px < SIDE
                lanes = slice(d * LANES, (d + 1) * LANES)
                spot = py * SIDE + from_x
                rx[col:col + PIV_DEV, lanes] = xp[spot] if inside else jnp.zeros((PIV_DEV, LANES), BF16)
                if px < SIDE:
                    first = row
                    for ref, count in zip(rows_x, heights):
                        lx[first:first + count, lanes] = ref[spot] if inside else jnp.zeros((count, LANES), BF16)
                        first += count
    block = SIDE * height
    for start, stop in SPANS:
        right = rx[start * COLB:stop * COLB, :]
        for py in range(SIDE):
            left = lx[py * block:(py + 1) * block, :]
            t[py, :, start * COLB:stop * COLB] = lax.dot_general(left, right, CONTRACT, preferred_element_type=F32)


def panel_terms(rows_g, gp, lg, rg, t):
    heights = [ref.shape[1] for ref in rows_g]
    height = sum(heights)
    for py in range(SIDE):
        for px in range(PITCH):
            row, col = (py * SIDE + px) * height, (py * PITCH + px) * PIV_DEV
            rg[col:col + PIV_DEV, :] = gp[py * SIDE + px] if px < SIDE else jnp.zeros((PIV_DEV, LANES), BF16)
            if px < SIDE:
                first = row
                for ref, count in zip(rows_g, heights):
                    lg[first:first + count, :] = ref[py * SIDE + px]
                    first += count
    block = SIDE * height
    acc = jnp.zeros((height, COLB), F32)
    for start, stop in SPANS:
        right = rg[start * COLB:stop * COLB, :]
        for py in range(SIDE):
            left = lg[py * block:(py + 1) * block, :]
            gg = lax.dot_general(left, right, CONTRACT, preferred_element_type=F32)
            for qy in range(start, stop):
                for px in range(SIDE):
                    rows = slice(px * height, (px + 1) * height)
                    total = t[py, rows, qy * COLB:(qy + 1) * COLB]
                    if py > 0 and qy > 0:
                        total = total + t[py - 1, rows, (qy - 1) * COLB:qy * COLB]
                    if py < SIDE - 1 and qy < SIDE - 1:
                        total = total + t[py + 1, rows, (qy + 1) * COLB:(qy + 2) * COLB]
                    acc = acc + gg[rows, (qy - start) * COLB:(qy - start + 1) * COLB] * total
    acc = acc + pltpu.roll(acc, 64, 1)
    acc = acc + pltpu.roll(acc, 32, 1)
    return acc + pltpu.roll(acc, 16, 1)


def products_kernel(x, xp, t_out, lx, rx):
    input_products([x], xp, lx, rx, t_out)


def own_kernel(t, g, gp, out_ref, lg, rg):
    out_ref[...] = panel_terms([g], gp, lg, rg, t)


def cross_kernel(t, g, gp, own_ref, ridge, out_ref, ridge_out, lg, rg):
    ridge_out[...] = ridge[...]
    across = panel_terms([g], gp, lg, rg, t)
    lane = lax.broadcasted_iota(jnp.int32, (8, LANES), 1)
    is_own = (lane // PIV_DEV) % 2 == lax.axis_index("rows")
    packed = jnp.zeros((8, LANES), F32)
    for j in range(4):
        rows = slice(8 * j, 8 * j + 8)
        packed = jnp.where(lane // EX == j, jnp.where(is_own, own_ref[rows, :], across[rows]), packed)
    out_ref[...] = packed


def product_shape(height):
    return (SIDE, SIDE * height, SIDE * COLB)


def scratch_of(height, width):
    return [pltpu.VMEM((SPOTS * height, width), BF16), pltpu.VMEM((SIDE * COLB, width), BF16)]


def terms(kernel, arrays, shapes, scratch, flops, name):
    vmem = pl.BlockSpec(memory_space=pltpu.VMEM)
    return pl.pallas_call(
        kernel,
        out_shape=tuple(jax.ShapeDtypeStruct(shape, F32) for shape in shapes),
        in_specs=[vmem] * len(arrays),
        out_specs=(vmem,) * len(shapes),
        scratch_shapes=scratch,
        compiler_params=pltpu.CompilerParams(vmem_limit_bytes=20 << 20),
        cost_estimate=cost(flops, 4 << 20),
        name=name,
    )(*arrays)


def rows_of(packed, count):
    return jnp.concatenate(
        [packed[:, EX * j:EX * (j + 1)] for j in range(count)], axis=0
    )


def tree_sum(values):
    while len(values) > 1:
        values = [a + b for a, b in zip(values[0::2], values[1::2])]
    return values[0]


def final_kernel(terms_ref, ridge_ref, gram_ref, factor_ref):
    count = terms_ref.shape[0] // 2
    sums = [tree_sum([terms_ref[g * count + i] for i in range(count)]) for g in range(2)]
    panel = rows_of(jnp.where(lax.axis_index("rows") == 0, sums[0], sums[1]), 4)
    gram_ref[...] = panel
    diag = jnp.concatenate([rows_of(total, 2) for total in sums], axis=0)
    row_id = lax.broadcasted_iota(jnp.int32, (EX, EX), 0)
    col_id = lax.broadcasted_iota(jnp.int32, (EX, EX), 1)
    ridge = jnp.where(row_id == col_id, jnp.broadcast_to(ridge_ref[...], (EX, EX)), 0.0)
    system = 0.5 * (diag + jnp.transpose(diag)) + ridge
    factor = jnp.zeros((EX, EX), F32)
    step = 4
    for j in range(0, EX, step):
        sys_cols = [jnp.broadcast_to(system[:, j + k:j + k + 1], (EX, EX)) for k in range(step)]
        pan_cols = [jnp.broadcast_to(panel[:, j + k:j + k + 1], (EX, EX)) for k in range(step)]
        sys_rows = [system[j + k:j + k + 1, :] for k in range(step)]
        for k in range(step):
            scale = lax.rsqrt(sys_cols[k][j + k:j + k + 1, :])
            sys_cols[k], pan_cols[k], sys_rows[k] = sys_cols[k] * scale, pan_cols[k] * scale, sys_rows[k] * scale
            factor = jnp.where(col_id == j + k, pan_cols[k], factor)
            for m in range(k + 1, step):
                entry = sys_cols[k][j + m:j + m + 1, :]
                sys_cols[m] = sys_cols[m] - sys_cols[k] * entry
                pan_cols[m] = pan_cols[m] - pan_cols[k] * entry
                sys_rows[m] = sys_rows[m] - sys_rows[k] * entry
        if j + step < EX:
            for k in range(step):
                system = system - sys_cols[k] * sys_rows[k]
                panel = panel - pan_cols[k] * sys_rows[k]
    factor_ref[...] = factor


def final(terms_of_all, ridge):
    vmem = pl.BlockSpec(memory_space=pltpu.VMEM)
    out = jax.ShapeDtypeStruct((EX, EX), F32)
    return pl.pallas_call(
        final_kernel,
        out_shape=(out, out),
        in_specs=[vmem] * 2,
        out_specs=(vmem, vmem),
        compiler_params=pltpu.CompilerParams(vmem_limit_bytes=8 << 20),
        name="solve",
    )(terms_of_all, ridge)


def exchange(value, count, flip):
    return lax.ppermute(value, "chan", [(i, i ^ flip) for i in range(count)])


def gather(value, count, first, second):
    received = exchange(value, count, first)
    return [value, exchange(value, count, second), received, exchange(received, count, second)]


def exchange_across(value, count):
    pairs = [(g * count + i, (1 - g) * count + i) for g in range(2) for i in range(count)]
    return lax.ppermute(value, ("rows", "chan"), pairs)


def local_packed(count, activations, cotangents, ordering, ridge):
    x = jnp.transpose(activations, (1, 2, 0, 3)).reshape(SIDE * SIDE, EX, CH)
    xo, go = prep(ordering, x, cotangents)
    own_g = gather(go, count, 8, 4)
    x_all, x_piv = unpack(gather(xo, count, 2, 1), "unpack_x", (own_g[1],))
    x_cross = exchange_across(x_piv, count)
    g_all, g_piv = unpack(own_g, "unpack_g")
    g_cross = exchange_across(g_piv, count)
    wide, narrow = scratch_of(EX, 3 * LANES), scratch_of(EX, LANES)
    shape, flops = product_shape(EX), 6 * 10**9
    products, = terms(products_kernel, (x_all, x_piv), (shape,), wide, flops, "own_inputs")
    own_term, = terms(own_kernel, (products, g_all, g_piv), ((EX, LANES),), narrow, flops, "terms_own")
    products, = terms(products_kernel, (x_all, x_cross), (shape,), wide, flops, "cross_inputs")
    arrays = (products, g_all, g_cross, own_term, ridge.reshape(1, EX))
    term, ridge = terms(cross_kernel, arrays, ((8, LANES), (1, EX)), narrow, flops, "terms_cross")
    copies = jnp.broadcast_to(term, (2 * count, 8, LANES))
    return final(lax.all_to_all(copies, ("rows", "chan"), 0, 0), ridge)


def jacobian_block(grad_rows, input_rows):
    example_count = input_rows.shape[0]
    side_len = input_rows.shape[1]
    channel_count = input_rows.shape[3]
    grad_count = grad_rows.shape[1]
    grid_grads = grad_rows.reshape(example_count, grad_count, side_len, side_len)
    padded_grads = jnp.pad(grid_grads, ((0, 0), (0, 0), (1, 1), (1, 1)))
    shifted = []
    for row_shift in range(3):
        for col_shift in range(3):
            window = padded_grads[
                :,
                :,
                2 - row_shift : 2 - row_shift + side_len,
                2 - col_shift : 2 - col_shift + side_len,
            ]
            shifted.append(window.reshape(example_count, grad_count, side_len * side_len))
    stacked_grads = jnp.stack(shifted, axis=2).reshape(
        example_count, grad_count * 9, side_len * side_len
    )
    flat_inputs = input_rows.reshape(example_count, side_len * side_len, channel_count)
    product = jnp.einsum(
        "nkp,npq->nkq", stacked_grads, flat_inputs, preferred_element_type=jnp.float32
    )
    return product.astype(jnp.bfloat16).reshape(example_count, -1)


def gram_block(left_rows, right_rows):
    return lax.dot_general(
        left_rows, right_rows, (((1,), (1,)), ((), ())), preferred_element_type=jnp.float32
    )


def local(activations, cotangents, ordering, ridge):
    local_order = ordering[0]
    own_inputs = jnp.take(activations, local_order, axis=0)
    own_grads = jnp.take(cotangents, local_order, axis=0)
    pivot_count = PIV_DEV
    pivot_inputs, pivot_grads = (
        lax.all_gather(own_inputs[:pivot_count], "rows", axis=0, tiled=True),
        lax.all_gather(own_grads[:pivot_count], "rows", axis=0, tiled=True),
    )
    full_own, full_pivot = (
        lax.all_gather(own_inputs, "chan", axis=3, tiled=True),
        lax.all_gather(pivot_inputs, "chan", axis=3, tiled=True),
    )
    own_jac = jacobian_block(own_grads, full_own)
    pivot_jac = jacobian_block(pivot_grads, full_pivot)
    partial_panel = gram_block(own_jac, pivot_jac)
    gram_panel = lax.psum(partial_panel, "chan")
    diag_block = lax.all_gather(gram_panel[:pivot_count], "rows", axis=0, tiled=True)
    system = 0.5 * (diag_block + diag_block.T) + jnp.diag(ridge)
    lower = jnp.linalg.cholesky(system)
    factor_panel = jax.scipy.linalg.solve_triangular(lower, gram_panel.T, lower=True).T
    return (gram_panel, factor_panel)


def solution(mesh):
    row_groups, count = mesh.shape["rows"], mesh.shape["chan"]
    packed = row_groups == 2 and count == 16
    return jax.shard_map(
        functools.partial(local_packed, count) if packed else local,
        mesh=mesh,
        in_specs=(P("rows", None, None, "chan"), P("rows", "chan", None), P("rows", None), P()),
        out_specs=(P("rows", None), P("rows", None)),
        check_vma=False,
    )
```

```python
import functools

import jax
import jax.numpy as jnp
from jax import lax
from jax.experimental import pallas as pl
from jax.experimental.pallas import tpu as pltpu
from jax.sharding import PartitionSpec as P

PIV_DEV = 16

SIDE = 7
SPOTS = SIDE * SIDE
PITCH = 8
GROUPS4 = 13
CH = 32
EX = 32
LANES = 128
F32 = jnp.float32
BF16 = jnp.bfloat16


def fetch(sources, targets, sems):
    copies = [pltpu.make_async_copy(a, b, sems.at[i]) for i, (a, b) in enumerate(zip(sources, targets))]
    for copy in copies:
        copy.start()
    return copies


def prep_kernel(order_hbm, x_hbm, g_hbm, xo_ref, go_ref, order_ref, x_ref, g_ref, sems, gs, gt, gout):
    copies = fetch((order_hbm, g_hbm, x_hbm), (order_ref, g_ref, x_ref), sems)
    copies[0].wait()
    copies[1].wait()
    row_id = lax.broadcasted_iota(jnp.int32, (EX, EX), 0)
    col_id = lax.broadcasted_iota(jnp.int32, (EX, EX), 1)
    onehot = jnp.zeros((EX, EX), F32)
    for k in range(EX):
        example = order_ref[0, k]
        onehot = jnp.where((row_id == k) & (col_id == example), 1.0, onehot)
        gs[k * CH:(k + 1) * CH, 0:SPOTS] = g_ref[example].astype(F32)
    gt[SPOTS:, :] = jnp.zeros((4 * GROUPS4 - SPOTS, LANES), F32)
    block_id = lax.broadcasted_iota(jnp.int32, (GROUPS4, LANES), 1) // CH
    for quad in range(EX // 4):
        gt[0:SPOTS, :] = jnp.transpose(gs[quad * LANES:(quad + 1) * LANES, :])[0:SPOTS, :]
        parts = [gt[pl.ds(j, GROUPS4, stride=4), :] for j in range(4)]
        for e in range(4):
            merged = jnp.zeros((GROUPS4, LANES), F32)
            for j in range(4):
                shift = (CH * (j - e)) % LANES
                moved = pltpu.roll(parts[j], shift, 1) if shift else parts[j]
                merged = jnp.where(block_id == j, moved, merged)
            gout[pl.ds(quad * 4 + e, GROUPS4, stride=EX), :] = merged
    for group in range(GROUPS4):
        go_ref[group] = gout[group * EX:(group + 1) * EX, :].astype(BF16)
    copies[2].wait()
    onehot = onehot.astype(BF16)
    zero_block = jnp.zeros((EX, CH), BF16)
    for group in range(GROUPS4):
        spots = [4 * group + j for j in range(4)]
        packed = jnp.concatenate([x_ref[p] if p < SPOTS else zero_block for p in spots], axis=1)
        xo_ref[group] = jnp.dot(onehot, packed, preferred_element_type=F32).astype(BF16)


def prep(order, x, g):
    full = jax.ShapeDtypeStruct((GROUPS4, EX, LANES), BF16)
    vmem = pl.BlockSpec(memory_space=pltpu.VMEM)
    return pl.pallas_call(
        prep_kernel,
        out_shape=(full, full),
        in_specs=[pl.BlockSpec(memory_space=pltpu.HBM)] * 3,
        out_specs=(vmem,) * 2,
        scratch_shapes=[
            pltpu.SMEM(order.shape, order.dtype),
            pltpu.VMEM(x.shape, x.dtype),
            pltpu.VMEM(g.shape, g.dtype),
            pltpu.SemaphoreType.DMA((3,)),
            pltpu.VMEM((EX * CH, LANES), F32),
            pltpu.VMEM((4 * GROUPS4, LANES), F32),
            pltpu.VMEM((GROUPS4 * EX, LANES), F32),
        ],
        compiler_params=pltpu.CompilerParams(vmem_limit_bytes=54848 << 10),
        name="prep",
    )(order, x, g)


ROWB = SIDE * EX
COLB = PITCH * PIV_DEV


def cost(flops, moved):
    return pl.CostEstimate(flops=flops, bytes_accessed=moved, transcendentals=0)


def unpack_kernel(*refs):
    packed, (all_ref, piv_ref) = refs[:4], refs[-2:]
    row = lax.broadcasted_iota(jnp.int32, (4 * LANES, 4 * LANES), 0)
    col = lax.broadcasted_iota(jnp.int32, (4 * LANES, 4 * LANES), 1)
    target = (row // CH) % 4 * LANES + row // LANES * CH + row % CH
    move = jnp.where(col == target, 1.0, 0.0).astype(BF16)
    flat = jnp.concatenate([ref[...].reshape(GROUPS4 * EX, LANES) for ref in packed], axis=1)
    moved = jnp.dot(flat, move, preferred_element_type=F32).astype(BF16)
    for group in range(GROUPS4):
        for j in range(4):
            if 4 * group + j < SPOTS:
                spot = moved[group * EX:(group + 1) * EX, j * LANES:(j + 1) * LANES]
                all_ref[4 * group + j] = spot
                piv_ref[4 * group + j] = spot[:PIV_DEV]


def unpack(arrays, name, after=()):
    vmem = pl.BlockSpec(memory_space=pltpu.VMEM)
    pivots = jax.ShapeDtypeStruct((SPOTS, PIV_DEV, LANES), BF16)
    return pl.pallas_call(
        unpack_kernel,
        out_shape=(jax.ShapeDtypeStruct((SPOTS, EX, LANES), BF16), pivots),
        in_specs=[vmem] * 4 + [pl.BlockSpec(memory_space=pl.ANY)] * len(after),
        out_specs=(vmem,) * 2,
        compiler_params=pltpu.CompilerParams(vmem_limit_bytes=12 << 20),
        cost_estimate=cost(0, 1 << 20),
        name=name,
    )(*arrays, *after)


CONTRACT = (((1,), (1,)), ((), ()))
SPANS = [(qy, min(qy + 2, SIDE)) for qy in range(0, SIDE, 2)]


def place_windows(values, window, pitch):
    count = values.shape[1]
    zero = jnp.zeros((count, LANES), BF16)
    for py in range(SIDE):
        for px in range(pitch):
            first = (py * pitch + px) * count
            for d in range(3):
                from_x = px + d - 1
                inside = 0 <= from_x < SIDE and px < SIDE
                window[first:first + count, d * LANES:(d + 1) * LANES] = values[py * SIDE + from_x] if inside else zero


def input_products(lx, rx, t):
    for start, stop in SPANS:
        right = rx[start * COLB:stop * COLB, :]
        for py in range(SIDE):
            left = lx[py * ROWB:(py + 1) * ROWB, :]
            t[py, :, start * COLB:stop * COLB] = lax.dot_general(left, right, CONTRACT, preferred_element_type=F32)


def panel_terms(g, gp, rg, t):
    for py in range(SIDE):
        for px in range(PITCH):
            col = (py * PITCH + px) * PIV_DEV
            rg[col:col + PIV_DEV, :] = gp[py * SIDE + px] if px < SIDE else jnp.zeros((PIV_DEV, LANES), BF16)
    acc = jnp.zeros((EX, COLB), F32)
    for start, stop in SPANS:
        right = rg[start * COLB:stop * COLB, :]
        for py in range(SIDE):
            left = g[py * SIDE:(py + 1) * SIDE].reshape(ROWB, LANES)
            gg = lax.dot_general(left, right, CONTRACT, preferred_element_type=F32)
            for qy in range(start, stop):
                for px in range(SIDE):
                    rows = slice(px * EX, (px + 1) * EX)
                    total = t[py, rows, qy * COLB:(qy + 1) * COLB]
                    if py > 0 and qy > 0:
                        total = total + t[py - 1, rows, (qy - 1) * COLB:qy * COLB]
                    if py < SIDE - 1 and qy < SIDE - 1:
                        total = total + t[py + 1, rows, (qy + 1) * COLB:(qy + 2) * COLB]
                    acc = acc + gg[rows, (qy - start) * COLB:(qy - start + 1) * COLB] * total
    acc = acc + pltpu.roll(acc, 64, 1)
    acc = acc + pltpu.roll(acc, 32, 1)
    return acc + pltpu.roll(acc, 16, 1)


def own_inputs_kernel(x, xp, t_out, lx_out, rx):
    place_windows(x, lx_out, SIDE)
    place_windows(xp, rx, PITCH)
    input_products(lx_out, rx, t_out)


def cross_inputs_kernel(lx, xp, t_out, rx):
    place_windows(xp, rx, PITCH)
    input_products(lx, rx, t_out)


def own_kernel(t, g, gp, out_ref, rg):
    out_ref[...] = panel_terms(g, gp, rg, t)


def cross_kernel(t, g, gp, own_ref, ridge, out_ref, ridge_out, rg):
    ridge_out[...] = ridge[...]
    across = panel_terms(g, gp, rg, t)
    lane = lax.broadcasted_iota(jnp.int32, (8, LANES), 1)
    is_own = (lane // PIV_DEV) % 2 == lax.axis_index("rows")
    packed = jnp.zeros((8, LANES), F32)
    for j in range(4):
        rows = slice(8 * j, 8 * j + 8)
        packed = jnp.where(lane // EX == j, jnp.where(is_own, own_ref[rows, :], across[rows]), packed)
    out_ref[...] = packed


def terms(kernel, arrays, outs, width, flops, name):
    vmem = pl.BlockSpec(memory_space=pltpu.VMEM)
    return pl.pallas_call(
        kernel,
        out_shape=tuple(jax.ShapeDtypeStruct(*out) for out in outs),
        in_specs=[vmem] * len(arrays),
        out_specs=(vmem,) * len(outs),
        scratch_shapes=[pltpu.VMEM((SIDE * COLB, width), BF16)],
        compiler_params=pltpu.CompilerParams(vmem_limit_bytes=20 << 20),
        cost_estimate=cost(flops, 4 << 20),
        name=name,
    )(*arrays)


def rows_of(packed, count):
    return jnp.concatenate(
        [packed[:, EX * j:EX * (j + 1)] for j in range(count)], axis=0
    )


def tree_sum(values):
    while len(values) > 1:
        values = [a + b for a, b in zip(values[0::2], values[1::2])]
    return values[0]


def final_kernel(terms_ref, ridge_ref, gram_ref, factor_ref):
    count = terms_ref.shape[0] // 2
    sums = [tree_sum([terms_ref[g * count + i] for i in range(count)]) for g in range(2)]
    panel = rows_of(jnp.where(lax.axis_index("rows") == 0, sums[0], sums[1]), 4)
    gram_ref[...] = panel
    diag = jnp.concatenate([rows_of(total, 2) for total in sums], axis=0)
    row_id = lax.broadcasted_iota(jnp.int32, (EX, EX), 0)
    col_id = lax.broadcasted_iota(jnp.int32, (EX, EX), 1)
    ridge = jnp.where(row_id == col_id, jnp.broadcast_to(ridge_ref[...], (EX, EX)), 0.0)
    system = 0.5 * (diag + jnp.transpose(diag)) + ridge
    factor = jnp.zeros((EX, EX), F32)
    step = 4
    for j in range(0, EX, step):
        sys_cols = [jnp.broadcast_to(system[:, j + k:j + k + 1], (EX, EX)) for k in range(step)]
        pan_cols = [jnp.broadcast_to(panel[:, j + k:j + k + 1], (EX, EX)) for k in range(step)]
        sys_rows = [system[j + k:j + k + 1, :] for k in range(step)]
        for k in range(step):
            scale = lax.rsqrt(sys_cols[k][j + k:j + k + 1, :])
            sys_cols[k], pan_cols[k], sys_rows[k] = sys_cols[k] * scale, pan_cols[k] * scale, sys_rows[k] * scale
            factor = jnp.where(col_id == j + k, pan_cols[k], factor)
            for m in range(k + 1, step):
                entry = sys_cols[k][j + m:j + m + 1, :]
                sys_cols[m] = sys_cols[m] - sys_cols[k] * entry
                pan_cols[m] = pan_cols[m] - pan_cols[k] * entry
                sys_rows[m] = sys_rows[m] - sys_rows[k] * entry
        if j + step < EX:
            for k in range(step):
                system = system - sys_cols[k] * sys_rows[k]
                panel = panel - pan_cols[k] * sys_rows[k]
    factor_ref[...] = factor


def final(terms_of_all, ridge):
    vmem = pl.BlockSpec(memory_space=pltpu.VMEM)
    out = jax.ShapeDtypeStruct((EX, EX), F32)
    return pl.pallas_call(
        final_kernel,
        out_shape=(out, out),
        in_specs=[vmem] * 2,
        out_specs=(vmem, vmem),
        compiler_params=pltpu.CompilerParams(vmem_limit_bytes=8 << 20),
        name="solve",
    )(terms_of_all, ridge)


def exchange(value, count, flip):
    return lax.ppermute(value, "chan", [(i, i ^ flip) for i in range(count)])


def gather(value, count, first, second):
    received = exchange(value, count, first)
    return [value, exchange(value, count, second), received, exchange(received, count, second)]


def exchange_across(value, count):
    pairs = [(g * count + i, (1 - g) * count + i) for g in range(2) for i in range(count)]
    return lax.ppermute(value, ("rows", "chan"), pairs)


def local_packed(count, activations, cotangents, ordering, ridge):
    x = jnp.transpose(activations, (1, 2, 0, 3)).reshape(SPOTS, EX, CH)
    xo, go = prep(ordering, x, cotangents)
    own_g = gather(go, count, 8, 4)
    x_all, x_piv = unpack(gather(xo, count, 2, 1), "unpack_x", (own_g[1],))
    x_cross = exchange_across(x_piv, count)
    g_all, g_piv = unpack(own_g, "unpack_g", (x_piv,))
    g_cross = exchange_across(g_piv, count)
    flops, product = 6 * 10**9, ((SIDE, ROWB, SIDE * COLB), F32)
    windows = ((SPOTS * EX, 3 * LANES), BF16)
    products, lx = terms(own_inputs_kernel, (x_all, x_piv), (product, windows), 3 * LANES, flops, "own_inputs")
    own_term, = terms(own_kernel, (products, g_all, g_piv), (((EX, LANES), F32),), LANES, flops, "terms_own")
    products, = terms(cross_inputs_kernel, (lx, x_cross), (product,), 3 * LANES, flops, "cross_inputs")
    arrays = (products, g_all, g_cross, own_term, ridge.reshape(1, EX))
    term, ridge = terms(cross_kernel, arrays, (((8, LANES), F32), ((1, EX), F32)), LANES, flops, "terms_cross")
    copies = jnp.broadcast_to(term, (2 * count, 8, LANES))
    return final(lax.all_to_all(copies, ("rows", "chan"), 0, 0), ridge)


def jacobian_block(grad_rows, input_rows):
    example_count = input_rows.shape[0]
    side_len = input_rows.shape[1]
    channel_count = input_rows.shape[3]
    grad_count = grad_rows.shape[1]
    grid_grads = grad_rows.reshape(example_count, grad_count, side_len, side_len)
    padded_grads = jnp.pad(grid_grads, ((0, 0), (0, 0), (1, 1), (1, 1)))
    shifted = []
    for row_shift in range(3):
        for col_shift in range(3):
            window = padded_grads[
                :,
                :,
                2 - row_shift : 2 - row_shift + side_len,
                2 - col_shift : 2 - col_shift + side_len,
            ]
            shifted.append(window.reshape(example_count, grad_count, side_len * side_len))
    stacked_grads = jnp.stack(shifted, axis=2).reshape(
        example_count, grad_count * 9, side_len * side_len
    )
    flat_inputs = input_rows.reshape(example_count, side_len * side_len, channel_count)
    product = jnp.einsum(
        "nkp,npq->nkq", stacked_grads, flat_inputs, preferred_element_type=jnp.float32
    )
    return product.astype(jnp.bfloat16).reshape(example_count, -1)


def gram_block(left_rows, right_rows):
    return lax.dot_general(
        left_rows, right_rows, (((1,), (1,)), ((), ())), preferred_element_type=jnp.float32
    )


def local(activations, cotangents, ordering, ridge):
    local_order = ordering[0]
    own_inputs = jnp.take(activations, local_order, axis=0)
    own_grads = jnp.take(cotangents, local_order, axis=0)
    pivot_count = PIV_DEV
    pivot_inputs, pivot_grads = (
        lax.all_gather(own_inputs[:pivot_count], "rows", axis=0, tiled=True),
        lax.all_gather(own_grads[:pivot_count], "rows", axis=0, tiled=True),
    )
    full_own, full_pivot = (
        lax.all_gather(own_inputs, "chan", axis=3, tiled=True),
        lax.all_gather(pivot_inputs, "chan", axis=3, tiled=True),
    )
    own_jac = jacobian_block(own_grads, full_own)
    pivot_jac = jacobian_block(pivot_grads, full_pivot)
    partial_panel = gram_block(own_jac, pivot_jac)
    gram_panel = lax.psum(partial_panel, "chan")
    diag_block = lax.all_gather(gram_panel[:pivot_count], "rows", axis=0, tiled=True)
    system = 0.5 * (diag_block + diag_block.T) + jnp.diag(ridge)
    lower = jnp.linalg.cholesky(system)
    factor_panel = jax.scipy.linalg.solve_triangular(lower, gram_panel.T, lower=True).T
    return (gram_panel, factor_panel)


def solution(mesh):
    row_groups, count = mesh.shape["rows"], mesh.shape["chan"]
    packed = row_groups == 2 and count == 16
    return jax.shard_map(
        functools.partial(local_packed, count) if packed else local,
        mesh=mesh,
        in_specs=(P("rows", None, None, "chan"), P("rows", "chan", None), P("rows", None), P()),
        out_specs=(P("rows", None), P("rows", None)),
        check_vma=False,
    )
```

```python
import functools

import jax
import jax.numpy as jnp
from jax import lax
from jax.experimental import pallas as pl
from jax.experimental.pallas import tpu as pltpu
from jax.sharding import PartitionSpec as P

PIV_DEV = 16

SIDE = 7
SPOTS = SIDE * SIDE
PITCH = 8
GROUPS4 = 13
CH = 32
EX = 32
LANES = 128
F32 = jnp.float32
BF16 = jnp.bfloat16


def fetch(sources, targets, sems):
    copies = [pltpu.make_async_copy(a, b, sems.at[i]) for i, (a, b) in enumerate(zip(sources, targets))]
    for copy in copies:
        copy.start()
    return copies


def prep_kernel(order_hbm, x_hbm, g_hbm, xo_ref, go_ref, order_ref, x_ref, g_ref, sems, gs, gt, gout):
    copies = fetch((order_hbm, g_hbm, x_hbm), (order_ref, g_ref, x_ref), sems)
    copies[0].wait()
    copies[1].wait()
    row_id = lax.broadcasted_iota(jnp.int32, (EX, EX), 0)
    col_id = lax.broadcasted_iota(jnp.int32, (EX, EX), 1)
    onehot = jnp.zeros((EX, EX), F32)
    for k in range(EX):
        example = order_ref[0, k]
        onehot = jnp.where((row_id == k) & (col_id == example), 1.0, onehot)
        gs[k * CH:(k + 1) * CH, 0:SPOTS] = g_ref[example].astype(F32)
    gt[SPOTS:, :] = jnp.zeros((4 * GROUPS4 - SPOTS, LANES), F32)
    block_id = lax.broadcasted_iota(jnp.int32, (GROUPS4, LANES), 1) // CH
    for quad in range(EX // 4):
        gt[0:SPOTS, :] = jnp.transpose(gs[quad * LANES:(quad + 1) * LANES, :])[0:SPOTS, :]
        parts = [gt[pl.ds(j, GROUPS4, stride=4), :] for j in range(4)]
        for e in range(4):
            merged = jnp.zeros((GROUPS4, LANES), F32)
            for j in range(4):
                shift = (CH * (j - e)) % LANES
                moved = pltpu.roll(parts[j], shift, 1) if shift else parts[j]
                merged = jnp.where(block_id == j, moved, merged)
            gout[pl.ds(quad * 4 + e, GROUPS4, stride=EX), :] = merged
    for group in range(GROUPS4):
        go_ref[group] = gout[group * EX:(group + 1) * EX, :].astype(BF16)
    copies[2].wait()
    onehot = onehot.astype(BF16)
    zero_block = jnp.zeros((EX, CH), BF16)
    for group in range(GROUPS4):
        spots = [4 * group + j for j in range(4)]
        packed = jnp.concatenate([x_ref[p] if p < SPOTS else zero_block for p in spots], axis=1)
        xo_ref[group] = jnp.dot(onehot, packed, preferred_element_type=F32).astype(BF16)


def prep(order, x, g):
    full = jax.ShapeDtypeStruct((GROUPS4, EX, LANES), BF16)
    vmem = pl.BlockSpec(memory_space=pltpu.VMEM)
    return pl.pallas_call(
        prep_kernel,
        out_shape=(full, full),
        in_specs=[pl.BlockSpec(memory_space=pltpu.HBM)] * 3,
        out_specs=(vmem,) * 2,
        scratch_shapes=[
            pltpu.SMEM(order.shape, order.dtype),
            pltpu.VMEM(x.shape, x.dtype),
            pltpu.VMEM(g.shape, g.dtype),
            pltpu.SemaphoreType.DMA((3,)),
            pltpu.VMEM((EX * CH, LANES), F32),
            pltpu.VMEM((4 * GROUPS4, LANES), F32),
            pltpu.VMEM((GROUPS4 * EX, LANES), F32),
        ],
        compiler_params=pltpu.CompilerParams(vmem_limit_bytes=54848 << 10),
        name="prep",
    )(order, x, g)


ROWB = SIDE * EX
COLB = PITCH * PIV_DEV


def cost(flops, moved):
    return pl.CostEstimate(flops=flops, bytes_accessed=moved, transcendentals=0)


def unpack_kernel(*refs):
    packed, (all_ref, piv_ref) = refs[:4], refs[-2:]
    row = lax.broadcasted_iota(jnp.int32, (4 * LANES, 4 * LANES), 0)
    col = lax.broadcasted_iota(jnp.int32, (4 * LANES, 4 * LANES), 1)
    target = (row // CH) % 4 * LANES + row // LANES * CH + row % CH
    move = jnp.where(col == target, 1.0, 0.0).astype(BF16)
    flat = jnp.concatenate([ref[...].reshape(GROUPS4 * EX, LANES) for ref in packed], axis=1)
    moved = jnp.dot(flat, move, preferred_element_type=F32).astype(BF16)
    for group in range(GROUPS4):
        for j in range(4):
            if 4 * group + j < SPOTS:
                spot = moved[group * EX:(group + 1) * EX, j * LANES:(j + 1) * LANES]
                all_ref[4 * group + j] = spot
                piv_ref[4 * group + j] = spot[:PIV_DEV]


def unpack(arrays, name, after=()):
    vmem = pl.BlockSpec(memory_space=pltpu.VMEM)
    pivots = jax.ShapeDtypeStruct((SPOTS, PIV_DEV, LANES), BF16)
    return pl.pallas_call(
        unpack_kernel,
        out_shape=(jax.ShapeDtypeStruct((SPOTS, EX, LANES), BF16), pivots),
        in_specs=[vmem] * 4 + [pl.BlockSpec(memory_space=pl.ANY)] * len(after),
        out_specs=(vmem,) * 2,
        compiler_params=pltpu.CompilerParams(vmem_limit_bytes=12 << 20),
        cost_estimate=cost(0, 1 << 20),
        name=name,
    )(*arrays, *after)


CONTRACT = (((1,), (1,)), ((), ()))
SPANS = [(qy, min(qy + 2, SIDE)) for qy in range(0, SIDE, 2)]


def place_windows(values, window, pitch):
    count = values.shape[1]
    zero = jnp.zeros((count, LANES), BF16)
    for py in range(SIDE):
        for px in range(pitch):
            first = (py * pitch + px) * count
            for d in range(3):
                from_x = px + d - 1
                inside = 0 <= from_x < SIDE and px < SIDE
                window[first:first + count, d * LANES:(d + 1) * LANES] = values[py * SIDE + from_x] if inside else zero


def input_products(lx, rx, t):
    for start, stop in SPANS:
        right = rx[start * COLB:stop * COLB, :]
        for py in range(SIDE):
            left = lx[py * ROWB:(py + 1) * ROWB, :]
            t[py, :, start * COLB:stop * COLB] = lax.dot_general(left, right, CONTRACT, preferred_element_type=F32)


def panel_terms(g, gp, rg, t):
    for py in range(SIDE):
        for px in range(PITCH):
            col = (py * PITCH + px) * PIV_DEV
            rg[col:col + PIV_DEV, :] = gp[py * SIDE + px] if px < SIDE else jnp.zeros((PIV_DEV, LANES), BF16)
    acc = jnp.zeros((EX, COLB), F32)
    for start, stop in SPANS:
        right = rg[start * COLB:stop * COLB, :]
        for py in range(SIDE):
            left = g[py * SIDE:(py + 1) * SIDE].reshape(ROWB, LANES)
            gg = lax.dot_general(left, right, CONTRACT, preferred_element_type=F32)
            for qy in range(start, stop):
                for px in range(SIDE):
                    rows = slice(px * EX, (px + 1) * EX)
                    total = t[py, rows, qy * COLB:(qy + 1) * COLB]
                    if py > 0 and qy > 0:
                        total = total + t[py - 1, rows, (qy - 1) * COLB:qy * COLB]
                    if py < SIDE - 1 and qy < SIDE - 1:
                        total = total + t[py + 1, rows, (qy + 1) * COLB:(qy + 2) * COLB]
                    acc = acc + gg[rows, (qy - start) * COLB:(qy - start + 1) * COLB] * total
    acc = acc + pltpu.roll(acc, 64, 1)
    acc = acc + pltpu.roll(acc, 32, 1)
    return acc + pltpu.roll(acc, 16, 1)


def own_inputs_kernel(x, xp, t_out, lx_out, rx):
    place_windows(x, lx_out, SIDE)
    place_windows(xp, rx, PITCH)
    input_products(lx_out, rx, t_out)


def cross_inputs_kernel(lx, xp, t_out, rx):
    place_windows(xp, rx, PITCH)
    input_products(lx, rx, t_out)


def own_kernel(t, g, gp, out_ref, rg):
    out_ref[...] = panel_terms(g, gp, rg, t)


def cross_kernel(t, g, gp, own_ref, ridge, out_ref, ridge_out, rg):
    ridge_out[...] = ridge[...]
    across = panel_terms(g, gp, rg, t)
    lane = lax.broadcasted_iota(jnp.int32, (8, LANES), 1)
    is_own = (lane // PIV_DEV) % 2 == lax.axis_index("rows")
    packed = jnp.zeros((8, LANES), F32)
    for j in range(4):
        rows = slice(8 * j, 8 * j + 8)
        packed = jnp.where(lane // EX == j, jnp.where(is_own, own_ref[rows, :], across[rows]), packed)
    out_ref[...] = packed


def terms(kernel, arrays, outs, width, flops, name):
    vmem = pl.BlockSpec(memory_space=pltpu.VMEM)
    return pl.pallas_call(
        kernel,
        out_shape=tuple(jax.ShapeDtypeStruct(*out) for out in outs),
        in_specs=[vmem] * len(arrays),
        out_specs=(vmem,) * len(outs),
        scratch_shapes=[pltpu.VMEM((SIDE * COLB, width), BF16)],
        compiler_params=pltpu.CompilerParams(vmem_limit_bytes=20 << 20),
        cost_estimate=cost(flops, 4 << 20),
        name=name,
    )(*arrays)


def rows_of(packed, count):
    return jnp.concatenate(
        [packed[:, EX * j:EX * (j + 1)] for j in range(count)], axis=0
    )


def tree_sum(values):
    while len(values) > 1:
        values = [a + b for a, b in zip(values[0::2], values[1::2])]
    return values[0]


def final_kernel(terms_ref, ridge_ref, gram_ref, factor_ref):
    count = terms_ref.shape[0] // 2
    sums = [tree_sum([terms_ref[g * count + i] for i in range(count)]) for g in range(2)]
    panel = rows_of(jnp.where(lax.axis_index("rows") == 0, sums[0], sums[1]), 4)
    gram_ref[...] = panel
    diag = jnp.concatenate([rows_of(total, 2) for total in sums], axis=0)
    row_id = lax.broadcasted_iota(jnp.int32, (EX, EX), 0)
    col_id = lax.broadcasted_iota(jnp.int32, (EX, EX), 1)
    ridge = jnp.where(row_id == col_id, jnp.broadcast_to(ridge_ref[...], (EX, EX)), 0.0)
    system = 0.5 * (diag + jnp.transpose(diag)) + ridge
    factor = jnp.zeros((EX, EX), F32)
    step = 4
    for j in range(0, EX, step):
        sys_cols = [jnp.broadcast_to(system[:, j + k:j + k + 1], (EX, EX)) for k in range(step)]
        pan_cols = [jnp.broadcast_to(panel[:, j + k:j + k + 1], (EX, EX)) for k in range(step)]
        sys_rows = [system[j + k:j + k + 1, :] for k in range(step)]
        for k in range(step):
            scale = lax.rsqrt(sys_cols[k][j + k:j + k + 1, :])
            sys_cols[k], pan_cols[k], sys_rows[k] = sys_cols[k] * scale, pan_cols[k] * scale, sys_rows[k] * scale
            factor = jnp.where(col_id == j + k, pan_cols[k], factor)
            for m in range(k + 1, step):
                entry = sys_cols[k][j + m:j + m + 1, :]
                sys_cols[m] = sys_cols[m] - sys_cols[k] * entry
                pan_cols[m] = pan_cols[m] - pan_cols[k] * entry
                sys_rows[m] = sys_rows[m] - sys_rows[k] * entry
        if j + step < EX:
            for k in range(step):
                system = system - sys_cols[k] * sys_rows[k]
                panel = panel - pan_cols[k] * sys_rows[k]
    factor_ref[...] = factor


def final(terms_of_all, ridge):
    vmem = pl.BlockSpec(memory_space=pltpu.VMEM)
    out = jax.ShapeDtypeStruct((EX, EX), F32)
    return pl.pallas_call(
        final_kernel,
        out_shape=(out, out),
        in_specs=[vmem] * 2,
        out_specs=(vmem, vmem),
        compiler_params=pltpu.CompilerParams(vmem_limit_bytes=8 << 20),
        name="solve",
    )(terms_of_all, ridge)


def exchange(value, count, flip):
    return lax.ppermute(value, "chan", [(i, i ^ flip) for i in range(count)])


def gather(value, count, first, second):
    received = exchange(value, count, first)
    return [value, exchange(value, count, second), received, exchange(received, count, second)]


def exchange_across(value, count):
    pairs = [(g * count + i, (1 - g) * count + i) for g in range(2) for i in range(count)]
    return lax.ppermute(value, ("rows", "chan"), pairs)


def local_packed(count, activations, cotangents, ordering, ridge):
    x = jnp.transpose(activations, (1, 2, 0, 3)).reshape(SPOTS, EX, CH)
    xo, go = prep(ordering, x, cotangents)
    own_g = gather(go, count, 8, 4)
    x_all, x_piv = unpack([xo] + [exchange(xo, count, f) for f in (1, 2, 3)], "unpack_x", (own_g[1], own_g[2]))
    x_cross = exchange_across(x_piv, count)
    g_all, g_piv = unpack(own_g, "unpack_g", (x_piv,))
    g_cross = exchange_across(g_piv, count)
    flops, product = 6 * 10**9, ((SIDE, ROWB, SIDE * COLB), F32)
    windows = ((SPOTS * EX, 3 * LANES), BF16)
    products, lx = terms(own_inputs_kernel, (x_all, x_piv), (product, windows), 3 * LANES, flops, "own_inputs")
    own_term, = terms(own_kernel, (products, g_all, g_piv), (((EX, LANES), F32),), LANES, flops, "terms_own")
    products, = terms(cross_inputs_kernel, (lx, x_cross), (product,), 3 * LANES, flops, "cross_inputs")
    arrays = (products, g_all, g_cross, own_term, ridge.reshape(1, EX))
    term, ridge = terms(cross_kernel, arrays, (((8, LANES), F32), ((1, EX), F32)), LANES, flops, "terms_cross")
    copies = jnp.broadcast_to(term, (2 * count, 8, LANES))
    return final(lax.all_to_all(copies, ("rows", "chan"), 0, 0), ridge)


def jacobian_block(grad_rows, input_rows):
    example_count = input_rows.shape[0]
    side_len = input_rows.shape[1]
    channel_count = input_rows.shape[3]
    grad_count = grad_rows.shape[1]
    grid_grads = grad_rows.reshape(example_count, grad_count, side_len, side_len)
    padded_grads = jnp.pad(grid_grads, ((0, 0), (0, 0), (1, 1), (1, 1)))
    shifted = []
    for row_shift in range(3):
        for col_shift in range(3):
            window = padded_grads[
                :,
                :,
                2 - row_shift : 2 - row_shift + side_len,
                2 - col_shift : 2 - col_shift + side_len,
            ]
            shifted.append(window.reshape(example_count, grad_count, side_len * side_len))
    stacked_grads = jnp.stack(shifted, axis=2).reshape(
        example_count, grad_count * 9, side_len * side_len
    )
    flat_inputs = input_rows.reshape(example_count, side_len * side_len, channel_count)
    product = jnp.einsum(
        "nkp,npq->nkq", stacked_grads, flat_inputs, preferred_element_type=jnp.float32
    )
    return product.astype(jnp.bfloat16).reshape(example_count, -1)


def gram_block(left_rows, right_rows):
    return lax.dot_general(
        left_rows, right_rows, (((1,), (1,)), ((), ())), preferred_element_type=jnp.float32
    )


def local(activations, cotangents, ordering, ridge):
    local_order = ordering[0]
    own_inputs = jnp.take(activations, local_order, axis=0)
    own_grads = jnp.take(cotangents, local_order, axis=0)
    pivot_count = PIV_DEV
    pivot_inputs, pivot_grads = (
        lax.all_gather(own_inputs[:pivot_count], "rows", axis=0, tiled=True),
        lax.all_gather(own_grads[:pivot_count], "rows", axis=0, tiled=True),
    )
    full_own, full_pivot = (
        lax.all_gather(own_inputs, "chan", axis=3, tiled=True),
        lax.all_gather(pivot_inputs, "chan", axis=3, tiled=True),
    )
    own_jac = jacobian_block(own_grads, full_own)
    pivot_jac = jacobian_block(pivot_grads, full_pivot)
    partial_panel = gram_block(own_jac, pivot_jac)
    gram_panel = lax.psum(partial_panel, "chan")
    diag_block = lax.all_gather(gram_panel[:pivot_count], "rows", axis=0, tiled=True)
    system = 0.5 * (diag_block + diag_block.T) + jnp.diag(ridge)
    lower = jnp.linalg.cholesky(system)
    factor_panel = jax.scipy.linalg.solve_triangular(lower, gram_panel.T, lower=True).T
    return (gram_panel, factor_panel)


def solution(mesh):
    row_groups, count = mesh.shape["rows"], mesh.shape["chan"]
    packed = row_groups == 2 and count == 16
    return jax.shard_map(
        functools.partial(local_packed, count) if packed else local,
        mesh=mesh,
        in_specs=(P("rows", None, None, "chan"), P("rows", "chan", None), P("rows", None), P()),
        out_specs=(P("rows", None), P("rows", None)),
        check_vma=False,
    )
```

```python
import functools

import jax
import jax.numpy as jnp
from jax import lax
from jax.experimental import pallas as pl
from jax.experimental.pallas import tpu as pltpu
from jax.sharding import PartitionSpec as P

PIV_DEV = 16

SIDE = 7
SPOTS = SIDE * SIDE
PITCH = 8
GROUPS4 = 13
CH = 32
EX = 32
LANES = 128
F32 = jnp.float32
BF16 = jnp.bfloat16


def fetch(sources, targets, sems):
    copies = [pltpu.make_async_copy(a, b, sems.at[i]) for i, (a, b) in enumerate(zip(sources, targets))]
    for copy in copies:
        copy.start()
    return copies


def prep_kernel(x_hbm, g_hbm, xo_ref, go_ref, x_ref, g_ref, sems, gs, gt, gout):
    copies = fetch((g_hbm, x_hbm), (g_ref, x_ref), sems)
    copies[0].wait()
    for k in range(EX):
        gs[k * CH:(k + 1) * CH, 0:SPOTS] = g_ref[k].astype(F32)
    gt[SPOTS:, :] = jnp.zeros((4 * GROUPS4 - SPOTS, LANES), F32)
    block_id = lax.broadcasted_iota(jnp.int32, (GROUPS4, LANES), 1) // CH
    for quad in range(EX // 4):
        gt[0:SPOTS, :] = jnp.transpose(gs[quad * LANES:(quad + 1) * LANES, :])[0:SPOTS, :]
        parts = [gt[pl.ds(j, GROUPS4, stride=4), :] for j in range(4)]
        for e in range(4):
            merged = jnp.zeros((GROUPS4, LANES), F32)
            for j in range(4):
                shift = (CH * (j - e)) % LANES
                moved = pltpu.roll(parts[j], shift, 1) if shift else parts[j]
                merged = jnp.where(block_id == j, moved, merged)
            gout[pl.ds(quad * 4 + e, GROUPS4, stride=EX), :] = merged
    for group in range(GROUPS4):
        go_ref[group] = gout[group * EX:(group + 1) * EX, :].astype(BF16)
    copies[1].wait()
    zero_block = jnp.zeros((EX, CH), BF16)
    for group in range(GROUPS4):
        spots = [4 * group + j for j in range(4)]
        xo_ref[group] = jnp.concatenate([x_ref[p] if p < SPOTS else zero_block for p in spots], axis=1)


def prep(x, g):
    full = jax.ShapeDtypeStruct((GROUPS4, EX, LANES), BF16)
    vmem = pl.BlockSpec(memory_space=pltpu.VMEM)
    return pl.pallas_call(
        prep_kernel,
        out_shape=(full, full),
        in_specs=[pl.BlockSpec(memory_space=pltpu.HBM)] * 2,
        out_specs=(vmem,) * 2,
        scratch_shapes=[
            pltpu.VMEM(x.shape, x.dtype),
            pltpu.VMEM(g.shape, g.dtype),
            pltpu.SemaphoreType.DMA((2,)),
            pltpu.VMEM((EX * CH, LANES), F32),
            pltpu.VMEM((4 * GROUPS4, LANES), F32),
            pltpu.VMEM((GROUPS4 * EX, LANES), F32),
        ],
        compiler_params=pltpu.CompilerParams(vmem_limit_bytes=54848 << 10),
        name="prep",
    )(x, g)


ROWB = SIDE * EX
COLB = PITCH * PIV_DEV


def cost(flops, moved):
    return pl.CostEstimate(flops=flops, bytes_accessed=moved, transcendentals=0)


def order_matrix(order):
    example = lax.broadcasted_iota(jnp.int32, (EX, EX), 0)
    return jnp.transpose(jnp.where(example == jnp.broadcast_to(order, (EX, EX)), 1.0, 0.0))


def unpack_kernel(*refs):
    packed, order_ref, (all_ref, piv_ref) = refs[:4], refs[4], refs[-2:]
    pick = order_matrix(order_ref[...])[:PIV_DEV].astype(BF16)
    row = lax.broadcasted_iota(jnp.int32, (4 * LANES, 4 * LANES), 0)
    col = lax.broadcasted_iota(jnp.int32, (4 * LANES, 4 * LANES), 1)
    target = (row // CH) % 4 * LANES + row // LANES * CH + row % CH
    move = jnp.where(col == target, 1.0, 0.0).astype(BF16)
    flat = jnp.concatenate([ref[...].reshape(GROUPS4 * EX, LANES) for ref in packed], axis=1)
    moved = jnp.dot(flat, move, preferred_element_type=F32).astype(BF16)
    for group in range(GROUPS4):
        rows = moved[group * EX:(group + 1) * EX]
        pivots = jnp.dot(pick, rows, preferred_element_type=F32).astype(BF16)
        for j in range(4):
            if 4 * group + j < SPOTS:
                all_ref[4 * group + j] = rows[:, j * LANES:(j + 1) * LANES]
                piv_ref[4 * group + j] = pivots[:, j * LANES:(j + 1) * LANES]


def unpack(arrays, order, name, after=()):
    vmem = pl.BlockSpec(memory_space=pltpu.VMEM)
    pivots = jax.ShapeDtypeStruct((SPOTS, PIV_DEV, LANES), BF16)
    return pl.pallas_call(
        unpack_kernel,
        out_shape=(jax.ShapeDtypeStruct((SPOTS, EX, LANES), BF16), pivots),
        in_specs=[vmem] * 5 + [pl.BlockSpec(memory_space=pl.ANY)] * len(after),
        out_specs=(vmem,) * 2,
        compiler_params=pltpu.CompilerParams(vmem_limit_bytes=12 << 20),
        cost_estimate=cost(0, 1 << 20),
        name=name,
    )(*arrays, order, *after)


CONTRACT = (((1,), (1,)), ((), ()))
SPANS = [(qy, min(qy + 2, SIDE)) for qy in range(0, SIDE, 2)]


def place_windows(values, window, pitch):
    count = values.shape[1]
    zero = jnp.zeros((count, LANES), BF16)
    for py in range(SIDE):
        for px in range(pitch):
            first = (py * pitch + px) * count
            for d in range(3):
                from_x = px + d - 1
                inside = 0 <= from_x < SIDE and px < SIDE
                window[first:first + count, d * LANES:(d + 1) * LANES] = values[py * SIDE + from_x] if inside else zero


def input_products(lx, rx, t):
    for start, stop in SPANS:
        right = rx[start * COLB:stop * COLB, :]
        for py in range(SIDE):
            left = lx[py * ROWB:(py + 1) * ROWB, :]
            t[py, :, start * COLB:stop * COLB] = lax.dot_general(left, right, CONTRACT, preferred_element_type=F32)


def panel_terms(g, gp, rg, t):
    for py in range(SIDE):
        for px in range(PITCH):
            col = (py * PITCH + px) * PIV_DEV
            rg[col:col + PIV_DEV, :] = gp[py * SIDE + px] if px < SIDE else jnp.zeros((PIV_DEV, LANES), BF16)
    acc = jnp.zeros((EX, COLB), F32)
    for start, stop in SPANS:
        right = rg[start * COLB:stop * COLB, :]
        for py in range(SIDE):
            left = g[py * SIDE:(py + 1) * SIDE].reshape(ROWB, LANES)
            gg = lax.dot_general(left, right, CONTRACT, preferred_element_type=F32)
            for qy in range(start, stop):
                for px in range(SIDE):
                    rows = slice(px * EX, (px + 1) * EX)
                    total = t[py, rows, qy * COLB:(qy + 1) * COLB]
                    if py > 0 and qy > 0:
                        total = total + t[py - 1, rows, (qy - 1) * COLB:qy * COLB]
                    if py < SIDE - 1 and qy < SIDE - 1:
                        total = total + t[py + 1, rows, (qy + 1) * COLB:(qy + 2) * COLB]
                    acc = acc + gg[rows, (qy - start) * COLB:(qy - start + 1) * COLB] * total
    acc = acc + pltpu.roll(acc, 64, 1)
    acc = acc + pltpu.roll(acc, 32, 1)
    return acc + pltpu.roll(acc, 16, 1)


def own_inputs_kernel(x, xp, t_out, lx_out, rx):
    place_windows(x, lx_out, SIDE)
    place_windows(xp, rx, PITCH)
    input_products(lx_out, rx, t_out)


def cross_inputs_kernel(lx, xp, t_out, rx):
    place_windows(xp, rx, PITCH)
    input_products(lx, rx, t_out)


def own_kernel(t, g, gp, out_ref, rg):
    out_ref[...] = panel_terms(g, gp, rg, t)


def cross_kernel(t, g, gp, own_ref, order_ref, ridge, out_ref, ridge_out, rg):
    ridge_out[...] = ridge[...]
    across = panel_terms(g, gp, rg, t)
    lane = lax.broadcasted_iota(jnp.int32, (EX, LANES), 1)
    both = jnp.where((lane // PIV_DEV) % 2 == lax.axis_index("rows"), own_ref[...], across)
    both = jnp.dot(order_matrix(order_ref[...]), both, precision=lax.Precision.HIGHEST, preferred_element_type=F32)
    packed = both[:8]
    for j in range(1, 4):
        packed = jnp.where(lane[:8] // EX == j, both[8 * j:8 * j + 8], packed)
    out_ref[...] = packed


def terms(kernel, arrays, outs, width, flops, name):
    vmem = pl.BlockSpec(memory_space=pltpu.VMEM)
    return pl.pallas_call(
        kernel,
        out_shape=tuple(jax.ShapeDtypeStruct(*out) for out in outs),
        in_specs=[vmem] * len(arrays),
        out_specs=(vmem,) * len(outs),
        scratch_shapes=[pltpu.VMEM((SIDE * COLB, width), BF16)],
        compiler_params=pltpu.CompilerParams(vmem_limit_bytes=20 << 20),
        cost_estimate=cost(flops, 4 << 20),
        name=name,
    )(*arrays)


def rows_of(packed, count):
    return jnp.concatenate(
        [packed[:, EX * j:EX * (j + 1)] for j in range(count)], axis=0
    )


def tree_sum(values):
    while len(values) > 1:
        values = [a + b for a, b in zip(values[0::2], values[1::2])]
    return values[0]


def final_kernel(terms_ref, ridge_ref, gram_ref, factor_ref):
    count = terms_ref.shape[0] // 2
    sums = [tree_sum([terms_ref[g * count + i] for i in range(count)]) for g in range(2)]
    panel = rows_of(jnp.where(lax.axis_index("rows") == 0, sums[0], sums[1]), 4)
    gram_ref[...] = panel
    diag = jnp.concatenate([rows_of(total, 2) for total in sums], axis=0)
    row_id = lax.broadcasted_iota(jnp.int32, (EX, EX), 0)
    col_id = lax.broadcasted_iota(jnp.int32, (EX, EX), 1)
    ridge = jnp.where(row_id == col_id, jnp.broadcast_to(ridge_ref[...], (EX, EX)), 0.0)
    system = 0.5 * (diag + jnp.transpose(diag)) + ridge
    factor = jnp.zeros((EX, EX), F32)
    step = 8
    for j in range(0, EX, step):
        sys_cols = [jnp.broadcast_to(system[:, j + k:j + k + 1], (EX, EX)) for k in range(step)]
        pan_cols = [jnp.broadcast_to(panel[:, j + k:j + k + 1], (EX, EX)) for k in range(step)]
        sys_rows = [system[j + k:j + k + 1, :] for k in range(step)]
        for k in range(step):
            scale = lax.rsqrt(sys_cols[k][j + k:j + k + 1, :])
            sys_cols[k], pan_cols[k], sys_rows[k] = sys_cols[k] * scale, pan_cols[k] * scale, sys_rows[k] * scale
            factor = jnp.where(col_id == j + k, pan_cols[k], factor)
            for m in range(k + 1, step):
                entry = sys_cols[k][j + m:j + m + 1, :]
                sys_cols[m] = sys_cols[m] - sys_cols[k] * entry
                pan_cols[m] = pan_cols[m] - pan_cols[k] * entry
                sys_rows[m] = sys_rows[m] - sys_rows[k] * entry
        if j + step < EX:
            for k in range(step):
                system = system - sys_cols[k] * sys_rows[k]
                panel = panel - pan_cols[k] * sys_rows[k]
    factor_ref[...] = factor


def final(terms_of_all, ridge):
    vmem = pl.BlockSpec(memory_space=pltpu.VMEM)
    out = jax.ShapeDtypeStruct((EX, EX), F32)
    return pl.pallas_call(
        final_kernel,
        out_shape=(out, out),
        in_specs=[vmem] * 2,
        out_specs=(vmem, vmem),
        compiler_params=pltpu.CompilerParams(vmem_limit_bytes=8 << 20),
        name="solve",
    )(terms_of_all, ridge)


def exchange(value, count, flip):
    return lax.ppermute(value, "chan", [(i, i ^ flip) for i in range(count)])


def gather(value, count, first, second):
    received = exchange(value, count, first)
    return [value, exchange(value, count, second), received, exchange(received, count, second)]


def exchange_across(value, count):
    pairs = [(g * count + i, (1 - g) * count + i) for g in range(2) for i in range(count)]
    return lax.ppermute(value, ("rows", "chan"), pairs)


def local_packed(count, activations, cotangents, ordering, ridge):
    x = jnp.transpose(activations, (1, 2, 0, 3)).reshape(SPOTS, EX, CH)
    xo, go = prep(x, cotangents)
    own_g = gather(go, count, 8, 4)
    x_all, x_piv = unpack(gather(xo, count, 2, 1), ordering, "unpack_x", (own_g[1],))
    x_cross = exchange_across(x_piv, count)
    g_all, g_piv = unpack(own_g, ordering, "unpack_g", (x_piv,))
    g_cross = exchange_across(g_piv, count)
    flops, product = 6 * 10**9, ((SIDE, ROWB, SIDE * COLB), F32)
    windows = ((SPOTS * EX, 3 * LANES), BF16)
    products, lx = terms(own_inputs_kernel, (x_all, x_piv), (product, windows), 3 * LANES, flops, "own_inputs")
    own_term, = terms(own_kernel, (products, g_all, g_piv), (((EX, LANES), F32),), LANES, flops, "terms_own")
    products, = terms(cross_inputs_kernel, (lx, x_cross), (product,), 3 * LANES, flops, "cross_inputs")
    arrays = (products, g_all, g_cross, own_term, ordering, ridge.reshape(1, EX))
    term, ridge = terms(cross_kernel, arrays, (((8, LANES), F32), ((1, EX), F32)), LANES, flops, "terms_cross")
    copies = jnp.broadcast_to(term, (2 * count, 8, LANES))
    return final(lax.all_to_all(copies, ("rows", "chan"), 0, 0), ridge)


def jacobian_block(grad_rows, input_rows):
    example_count = input_rows.shape[0]
    side_len = input_rows.shape[1]
    channel_count = input_rows.shape[3]
    grad_count = grad_rows.shape[1]
    grid_grads = grad_rows.reshape(example_count, grad_count, side_len, side_len)
    padded_grads = jnp.pad(grid_grads, ((0, 0), (0, 0), (1, 1), (1, 1)))
    shifted = []
    for row_shift in range(3):
        for col_shift in range(3):
            window = padded_grads[
                :,
                :,
                2 - row_shift : 2 - row_shift + side_len,
                2 - col_shift : 2 - col_shift + side_len,
            ]
            shifted.append(window.reshape(example_count, grad_count, side_len * side_len))
    stacked_grads = jnp.stack(shifted, axis=2).reshape(
        example_count, grad_count * 9, side_len * side_len
    )
    flat_inputs = input_rows.reshape(example_count, side_len * side_len, channel_count)
    product = jnp.einsum(
        "nkp,npq->nkq", stacked_grads, flat_inputs, preferred_element_type=jnp.float32
    )
    return product.astype(jnp.bfloat16).reshape(example_count, -1)


def gram_block(left_rows, right_rows):
    return lax.dot_general(
        left_rows, right_rows, (((1,), (1,)), ((), ())), preferred_element_type=jnp.float32
    )


def local(activations, cotangents, ordering, ridge):
    local_order = ordering[0]
    own_inputs = jnp.take(activations, local_order, axis=0)
    own_grads = jnp.take(cotangents, local_order, axis=0)
    pivot_count = PIV_DEV
    pivot_inputs, pivot_grads = (
        lax.all_gather(own_inputs[:pivot_count], "rows", axis=0, tiled=True),
        lax.all_gather(own_grads[:pivot_count], "rows", axis=0, tiled=True),
    )
    full_own, full_pivot = (
        lax.all_gather(own_inputs, "chan", axis=3, tiled=True),
        lax.all_gather(pivot_inputs, "chan", axis=3, tiled=True),
    )
    own_jac = jacobian_block(own_grads, full_own)
    pivot_jac = jacobian_block(pivot_grads, full_pivot)
    partial_panel = gram_block(own_jac, pivot_jac)
    gram_panel = lax.psum(partial_panel, "chan")
    diag_block = lax.all_gather(gram_panel[:pivot_count], "rows", axis=0, tiled=True)
    system = 0.5 * (diag_block + diag_block.T) + jnp.diag(ridge)
    lower = jnp.linalg.cholesky(system)
    factor_panel = jax.scipy.linalg.solve_triangular(lower, gram_panel.T, lower=True).T
    return (gram_panel, factor_panel)


def solution(mesh):
    row_groups, count = mesh.shape["rows"], mesh.shape["chan"]
    packed = row_groups == 2 and count == 16
    return jax.shard_map(
        functools.partial(local_packed, count) if packed else local,
        mesh=mesh,
        in_specs=(P("rows", None, None, "chan"), P("rows", "chan", None), P("rows", None), P()),
        out_specs=(P("rows", None), P("rows", None)),
        check_vma=False,
    )
```

```python
import functools

import jax
import jax.numpy as jnp
from jax import lax
from jax.experimental import pallas as pl
from jax.experimental.pallas import tpu as pltpu
from jax.sharding import PartitionSpec as P

PIV_DEV = 16

SIDE = 7
SPOTS = SIDE * SIDE
PITCH = 8
GROUPS4 = 13
CH = 32
EX = 32
LANES = 128
F32 = jnp.float32
BF16 = jnp.bfloat16


def fetch(sources, targets, sems):
    copies = [pltpu.make_async_copy(a, b, sems.at[i]) for i, (a, b) in enumerate(zip(sources, targets))]
    for copy in copies:
        copy.start()
    return copies


def prep_kernel(order_hbm, x_hbm, g_hbm, xo_ref, go_ref, order_ref, x_ref, g_ref, sems, gs, gt, gout):
    copies = fetch((order_hbm, g_hbm, x_hbm), (order_ref, g_ref, x_ref), sems)
    copies[0].wait()
    copies[1].wait()
    row_id = lax.broadcasted_iota(jnp.int32, (EX, EX), 0)
    col_id = lax.broadcasted_iota(jnp.int32, (EX, EX), 1)
    onehot = jnp.zeros((EX, EX), F32)
    for k in range(EX):
        example = order_ref[0, k]
        onehot = jnp.where((row_id == k) & (col_id == example), 1.0, onehot)
        gs[k * CH:(k + 1) * CH, 0:SPOTS] = g_ref[example].astype(F32)
    gt[SPOTS:, :] = jnp.zeros((4 * GROUPS4 - SPOTS, LANES), F32)
    block_id = lax.broadcasted_iota(jnp.int32, (GROUPS4, LANES), 1) // CH
    for quad in range(EX // 4):
        gt[0:SPOTS, :] = jnp.transpose(gs[quad * LANES:(quad + 1) * LANES, :])[0:SPOTS, :]
        parts = [gt[pl.ds(j, GROUPS4, stride=4), :] for j in range(4)]
        for e in range(4):
            merged = jnp.zeros((GROUPS4, LANES), F32)
            for j in range(4):
                shift = (CH * (j - e)) % LANES
                moved = pltpu.roll(parts[j], shift, 1) if shift else parts[j]
                merged = jnp.where(block_id == j, moved, merged)
            gout[pl.ds(quad * 4 + e, GROUPS4, stride=EX), :] = merged
    for group in range(GROUPS4):
        go_ref[group] = gout[group * EX:(group + 1) * EX, :].astype(BF16)
    copies[2].wait()
    onehot = onehot.astype(BF16)
    zero_block = jnp.zeros((EX, CH), BF16)
    for group in range(GROUPS4):
        spots = [4 * group + j for j in range(4)]
        packed = jnp.concatenate([x_ref[p] if p < SPOTS else zero_block for p in spots], axis=1)
        xo_ref[group] = jnp.dot(onehot, packed, preferred_element_type=F32).astype(BF16)


def prep(order, x, g):
    full = jax.ShapeDtypeStruct((GROUPS4, EX, LANES), BF16)
    vmem = pl.BlockSpec(memory_space=pltpu.VMEM)
    return pl.pallas_call(
        prep_kernel,
        out_shape=(full, full),
        in_specs=[pl.BlockSpec(memory_space=pltpu.HBM)] * 3,
        out_specs=(vmem,) * 2,
        scratch_shapes=[
            pltpu.SMEM(order.shape, order.dtype),
            pltpu.VMEM(x.shape, x.dtype),
            pltpu.VMEM(g.shape, g.dtype),
            pltpu.SemaphoreType.DMA((3,)),
            pltpu.VMEM((EX * CH, LANES), F32),
            pltpu.VMEM((4 * GROUPS4, LANES), F32),
            pltpu.VMEM((GROUPS4 * EX, LANES), F32),
        ],
        compiler_params=pltpu.CompilerParams(vmem_limit_bytes=54848 << 10),
        name="prep",
    )(order, x, g)


ROWB = SIDE * EX
COLB = PITCH * PIV_DEV


def cost(flops, moved):
    return pl.CostEstimate(flops=flops, bytes_accessed=moved, transcendentals=0)


def unpack_kernel(*refs):
    packed, (all_ref, piv_ref) = refs[:4], refs[-2:]
    row = lax.broadcasted_iota(jnp.int32, (4 * LANES, 4 * LANES), 0)
    col = lax.broadcasted_iota(jnp.int32, (4 * LANES, 4 * LANES), 1)
    target = (row // CH) % 4 * LANES + row // LANES * CH + row % CH
    move = jnp.where(col == target, 1.0, 0.0).astype(BF16)
    flat = jnp.concatenate([ref[...].reshape(GROUPS4 * EX, LANES) for ref in packed], axis=1)
    moved = jnp.dot(flat, move, preferred_element_type=F32).astype(BF16)
    for group in range(GROUPS4):
        for j in range(4):
            if 4 * group + j < SPOTS:
                spot = moved[group * EX:(group + 1) * EX, j * LANES:(j + 1) * LANES]
                all_ref[4 * group + j] = spot
                piv_ref[4 * group + j] = spot[:PIV_DEV]


def unpack(arrays, name, after=()):
    vmem = pl.BlockSpec(memory_space=pltpu.VMEM)
    pivots = jax.ShapeDtypeStruct((SPOTS, PIV_DEV, LANES), BF16)
    return pl.pallas_call(
        unpack_kernel,
        out_shape=(jax.ShapeDtypeStruct((SPOTS, EX, LANES), BF16), pivots),
        in_specs=[vmem] * 4 + [pl.BlockSpec(memory_space=pl.ANY)] * len(after),
        out_specs=(vmem,) * 2,
        compiler_params=pltpu.CompilerParams(vmem_limit_bytes=12 << 20),
        cost_estimate=cost(0, 1 << 20),
        name=name,
    )(*arrays, *after)


CONTRACT = (((1,), (1,)), ((), ()))
SPANS = [(qy, min(qy + 2, SIDE)) for qy in range(0, SIDE, 2)]


def place_windows(values, window, pitch):
    count = values.shape[1]
    zero = jnp.zeros((count, LANES), BF16)
    for py in range(SIDE):
        for px in range(pitch):
            first = (py * pitch + px) * count
            for d in range(3):
                from_x = px + d - 1
                inside = 0 <= from_x < SIDE and px < SIDE
                window[first:first + count, d * LANES:(d + 1) * LANES] = values[py * SIDE + from_x] if inside else zero


def input_products(lx, rx, t):
    for start, stop in SPANS:
        right = rx[start * COLB:stop * COLB, :]
        for py in range(SIDE):
            left = lx[py * ROWB:(py + 1) * ROWB, :]
            t[py, :, start * COLB:stop * COLB] = lax.dot_general(left, right, CONTRACT, preferred_element_type=F32)


def panel_terms(g, gp, rg, t):
    for py in range(SIDE):
        for px in range(PITCH):
            col = (py * PITCH + px) * PIV_DEV
            rg[col:col + PIV_DEV, :] = gp[py * SIDE + px] if px < SIDE else jnp.zeros((PIV_DEV, LANES), BF16)
    acc = jnp.zeros((EX, COLB), F32)
    for start, stop in SPANS:
        right = rg[start * COLB:stop * COLB, :]
        for py in range(SIDE):
            left = g[py * SIDE:(py + 1) * SIDE].reshape(ROWB, LANES)
            gg = lax.dot_general(left, right, CONTRACT, preferred_element_type=F32)
            for qy in range(start, stop):
                for px in range(SIDE):
                    rows = slice(px * EX, (px + 1) * EX)
                    total = t[py, rows, qy * COLB:(qy + 1) * COLB]
                    if py > 0 and qy > 0:
                        total = total + t[py - 1, rows, (qy - 1) * COLB:qy * COLB]
                    if py < SIDE - 1 and qy < SIDE - 1:
                        total = total + t[py + 1, rows, (qy + 1) * COLB:(qy + 2) * COLB]
                    acc = acc + gg[rows, (qy - start) * COLB:(qy - start + 1) * COLB] * total
    acc = acc + pltpu.roll(acc, 64, 1)
    acc = acc + pltpu.roll(acc, 32, 1)
    return acc + pltpu.roll(acc, 16, 1)


def own_inputs_kernel(x, xp, t_out, lx_out, rx):
    place_windows(x, lx_out, SIDE)
    place_windows(xp, rx, PITCH)
    input_products(lx_out, rx, t_out)


def cross_inputs_kernel(lx, xp, t_out, rx):
    place_windows(xp, rx, PITCH)
    input_products(lx, rx, t_out)


def own_kernel(t, g, gp, out_ref, rg):
    out_ref[...] = panel_terms(g, gp, rg, t)


def cross_kernel(t, g, gp, own_ref, ridge, out_ref, ridge_out, rg):
    ridge_out[...] = ridge[...]
    across = panel_terms(g, gp, rg, t)
    lane = lax.broadcasted_iota(jnp.int32, (8, LANES), 1)
    is_own = (lane // PIV_DEV) % 2 == lax.axis_index("rows")
    packed = jnp.zeros((8, LANES), F32)
    for j in range(4):
        rows = slice(8 * j, 8 * j + 8)
        packed = jnp.where(lane // EX == j, jnp.where(is_own, own_ref[rows, :], across[rows]), packed)
    out_ref[...] = packed


def terms(kernel, arrays, outs, width, flops, name):
    vmem = pl.BlockSpec(memory_space=pltpu.VMEM)
    return pl.pallas_call(
        kernel,
        out_shape=tuple(jax.ShapeDtypeStruct(*out) for out in outs),
        in_specs=[vmem] * len(arrays),
        out_specs=(vmem,) * len(outs),
        scratch_shapes=[pltpu.VMEM((SIDE * COLB, width), BF16)],
        compiler_params=pltpu.CompilerParams(vmem_limit_bytes=20 << 20),
        cost_estimate=cost(flops, 4 << 20),
        name=name,
    )(*arrays)


def rows_of(packed, count):
    return jnp.concatenate(
        [packed[:, EX * j:EX * (j + 1)] for j in range(count)], axis=0
    )


def tree_sum(values):
    while len(values) > 1:
        values = [a + b for a, b in zip(values[0::2], values[1::2])]
    return values[0]


def final_kernel(terms_ref, ridge_ref, gram_ref, factor_ref):
    count = terms_ref.shape[0] // 2
    sums = [tree_sum([terms_ref[g * count + i] for i in range(count)]) for g in range(2)]
    panel = rows_of(jnp.where(lax.axis_index("rows") == 0, sums[0], sums[1]), 4)
    gram_ref[...] = panel
    diag = jnp.concatenate([rows_of(total, 2) for total in sums], axis=0)
    row_id = lax.broadcasted_iota(jnp.int32, (EX, EX), 0)
    col_id = lax.broadcasted_iota(jnp.int32, (EX, EX), 1)
    ridge = jnp.where(row_id == col_id, jnp.broadcast_to(ridge_ref[...], (EX, EX)), 0.0)
    system = 0.5 * (diag + jnp.transpose(diag)) + ridge
    factor = jnp.zeros((EX, EX), F32)
    step = 8
    for j in range(0, EX, step):
        sys_cols = [jnp.broadcast_to(system[:, j + k:j + k + 1], (EX, EX)) for k in range(step)]
        pan_cols = [jnp.broadcast_to(panel[:, j + k:j + k + 1], (EX, EX)) for k in range(step)]
        sys_rows = [system[j + k:j + k + 1, :] for k in range(step)]
        for k in range(step):
            scale = lax.rsqrt(sys_cols[k][j + k:j + k + 1, :])
            sys_cols[k], pan_cols[k], sys_rows[k] = sys_cols[k] * scale, pan_cols[k] * scale, sys_rows[k] * scale
            factor = jnp.where(col_id == j + k, pan_cols[k], factor)
            for m in range(k + 1, step):
                entry = sys_cols[k][j + m:j + m + 1, :]
                sys_cols[m] = sys_cols[m] - sys_cols[k] * entry
                pan_cols[m] = pan_cols[m] - pan_cols[k] * entry
                sys_rows[m] = sys_rows[m] - sys_rows[k] * entry
        if j + step < EX:
            for k in range(step):
                system = system - sys_cols[k] * sys_rows[k]
                panel = panel - pan_cols[k] * sys_rows[k]
    factor_ref[...] = factor


def final(terms_of_all, ridge):
    vmem = pl.BlockSpec(memory_space=pltpu.VMEM)
    out = jax.ShapeDtypeStruct((EX, EX), F32)
    return pl.pallas_call(
        final_kernel,
        out_shape=(out, out),
        in_specs=[vmem] * 2,
        out_specs=(vmem, vmem),
        compiler_params=pltpu.CompilerParams(vmem_limit_bytes=8 << 20),
        name="solve",
    )(terms_of_all, ridge)


def exchange(value, count, flip):
    return lax.ppermute(value, "chan", [(i, i ^ flip) for i in range(count)])


def gather(value, count, first, second):
    received = exchange(value, count, first)
    return [value, exchange(value, count, second), received, exchange(received, count, second)]


def exchange_across(value, count):
    pairs = [(g * count + i, (1 - g) * count + i) for g in range(2) for i in range(count)]
    return lax.ppermute(value, ("rows", "chan"), pairs)


def local_packed(count, activations, cotangents, ordering, ridge):
    x = jnp.transpose(activations, (1, 2, 0, 3)).reshape(SPOTS, EX, CH)
    xo, go = prep(ordering, x, cotangents)
    own_g = gather(go, count, 8, 4)
    x_all, x_piv = unpack(gather(xo, count, 2, 1), "unpack_x", (own_g[1],))
    x_cross = exchange_across(x_piv, count)
    g_all, g_piv = unpack(own_g, "unpack_g", (x_piv,))
    g_cross = exchange_across(g_piv, count)
    flops, product = 6 * 10**9, ((SIDE, ROWB, SIDE * COLB), F32)
    windows = ((SPOTS * EX, 3 * LANES), BF16)
    products, lx = terms(own_inputs_kernel, (x_all, x_piv), (product, windows), 3 * LANES, flops, "own_inputs")
    own_term, = terms(own_kernel, (products, g_all, g_piv), (((EX, LANES), F32),), LANES, flops, "terms_own")
    products, = terms(cross_inputs_kernel, (lx, x_cross), (product,), 3 * LANES, flops, "cross_inputs")
    arrays = (products, g_all, g_cross, own_term, ridge.reshape(1, EX))
    term, ridge = terms(cross_kernel, arrays, (((8, LANES), F32), ((1, EX), F32)), LANES, flops, "terms_cross")
    copies = jnp.broadcast_to(term, (2 * count, 8, LANES))
    return final(lax.all_to_all(copies, ("rows", "chan"), 0, 0), ridge)


def jacobian_block(grad_rows, input_rows):
    example_count = input_rows.shape[0]
    side_len = input_rows.shape[1]
    channel_count = input_rows.shape[3]
    grad_count = grad_rows.shape[1]
    grid_grads = grad_rows.reshape(example_count, grad_count, side_len, side_len)
    padded_grads = jnp.pad(grid_grads, ((0, 0), (0, 0), (1, 1), (1, 1)))
    shifted = []
    for row_shift in range(3):
        for col_shift in range(3):
            window = padded_grads[
                :,
                :,
                2 - row_shift : 2 - row_shift + side_len,
                2 - col_shift : 2 - col_shift + side_len,
            ]
            shifted.append(window.reshape(example_count, grad_count, side_len * side_len))
    stacked_grads = jnp.stack(shifted, axis=2).reshape(
        example_count, grad_count * 9, side_len * side_len
    )
    flat_inputs = input_rows.reshape(example_count, side_len * side_len, channel_count)
    product = jnp.einsum(
        "nkp,npq->nkq", stacked_grads, flat_inputs, preferred_element_type=jnp.float32
    )
    return product.astype(jnp.bfloat16).reshape(example_count, -1)


def gram_block(left_rows, right_rows):
    return lax.dot_general(
        left_rows, right_rows, (((1,), (1,)), ((), ())), preferred_element_type=jnp.float32
    )


def local(activations, cotangents, ordering, ridge):
    local_order = ordering[0]
    own_inputs = jnp.take(activations, local_order, axis=0)
    own_grads = jnp.take(cotangents, local_order, axis=0)
    pivot_count = PIV_DEV
    pivot_inputs, pivot_grads = (
        lax.all_gather(own_inputs[:pivot_count], "rows", axis=0, tiled=True),
        lax.all_gather(own_grads[:pivot_count], "rows", axis=0, tiled=True),
    )
    full_own, full_pivot = (
        lax.all_gather(own_inputs, "chan", axis=3, tiled=True),
        lax.all_gather(pivot_inputs, "chan", axis=3, tiled=True),
    )
    own_jac = jacobian_block(own_grads, full_own)
    pivot_jac = jacobian_block(pivot_grads, full_pivot)
    partial_panel = gram_block(own_jac, pivot_jac)
    gram_panel = lax.psum(partial_panel, "chan")
    diag_block = lax.all_gather(gram_panel[:pivot_count], "rows", axis=0, tiled=True)
    system = 0.5 * (diag_block + diag_block.T) + jnp.diag(ridge)
    lower = jnp.linalg.cholesky(system)
    factor_panel = jax.scipy.linalg.solve_triangular(lower, gram_panel.T, lower=True).T
    return (gram_panel, factor_panel)


def solution(mesh):
    row_groups, count = mesh.shape["rows"], mesh.shape["chan"]
    packed = row_groups == 2 and count == 16
    return jax.shard_map(
        functools.partial(local_packed, count) if packed else local,
        mesh=mesh,
        in_specs=(P("rows", None, None, "chan"), P("rows", "chan", None), P("rows", None), P()),
        out_specs=(P("rows", None), P("rows", None)),
        check_vma=False,
    )
```

```python
import functools

import jax
import jax.numpy as jnp
from jax import lax
from jax.experimental import pallas as pl
from jax.experimental.pallas import tpu as pltpu
from jax.sharding import PartitionSpec as P

PIV_DEV = 16

SIDE = 7
SPOTS = SIDE * SIDE
PITCH = 8
GROUPS4 = 13
CH = 32
EX = 32
LANES = 128
F32 = jnp.float32
BF16 = jnp.bfloat16


def fetch(sources, targets, sems):
    copies = [pltpu.make_async_copy(a, b, sems.at[i]) for i, (a, b) in enumerate(zip(sources, targets))]
    for copy in copies:
        copy.start()
    return copies


def prep_kernel(order_hbm, x_hbm, g_hbm, xo_ref, go_ref, order_ref, x_ref, g_ref, sems, gs, gt, gout):
    copies = fetch((order_hbm, g_hbm, x_hbm), (order_ref, g_ref, x_ref), sems)
    copies[0].wait()
    copies[1].wait()
    row_id = lax.broadcasted_iota(jnp.int32, (EX, EX), 0)
    col_id = lax.broadcasted_iota(jnp.int32, (EX, EX), 1)
    onehot = jnp.zeros((EX, EX), F32)
    for k in range(EX):
        example = order_ref[0, k]
        onehot = jnp.where((row_id == k) & (col_id == example), 1.0, onehot)
        gs[k * CH:(k + 1) * CH, 0:SPOTS] = g_ref[example].astype(F32)
    gt[SPOTS:, :] = jnp.zeros((4 * GROUPS4 - SPOTS, LANES), F32)
    block_id = lax.broadcasted_iota(jnp.int32, (GROUPS4, LANES), 1) // CH
    for quad in range(EX // 4):
        gt[0:SPOTS, :] = jnp.transpose(gs[quad * LANES:(quad + 1) * LANES, :])[0:SPOTS, :]
        parts = [gt[pl.ds(j, GROUPS4, stride=4), :] for j in range(4)]
        for e in range(4):
            merged = jnp.zeros((GROUPS4, LANES), F32)
            for j in range(4):
                shift = (CH * (j - e)) % LANES
                moved = pltpu.roll(parts[j], shift, 1) if shift else parts[j]
                merged = jnp.where(block_id == j, moved, merged)
            gout[pl.ds(quad * 4 + e, GROUPS4, stride=EX), :] = merged
    for group in range(GROUPS4):
        go_ref[group] = gout[group * EX:(group + 1) * EX, :].astype(BF16)
    copies[2].wait()
    onehot = onehot.astype(BF16)
    zero_block = jnp.zeros((EX, CH), BF16)
    for group in range(GROUPS4):
        spots = [4 * group + j for j in range(4)]
        packed = jnp.concatenate([x_ref[p] if p < SPOTS else zero_block for p in spots], axis=1)
        xo_ref[group] = jnp.dot(onehot, packed, preferred_element_type=F32).astype(BF16)


def prep(order, x, g):
    full = jax.ShapeDtypeStruct((GROUPS4, EX, LANES), BF16)
    vmem = pl.BlockSpec(memory_space=pltpu.VMEM)
    return pl.pallas_call(
        prep_kernel,
        out_shape=(full, full),
        in_specs=[pl.BlockSpec(memory_space=pltpu.HBM)] * 3,
        out_specs=(vmem,) * 2,
        scratch_shapes=[
            pltpu.SMEM(order.shape, order.dtype),
            pltpu.VMEM(x.shape, x.dtype),
            pltpu.VMEM(g.shape, g.dtype),
            pltpu.SemaphoreType.DMA((3,)),
            pltpu.VMEM((EX * CH, LANES), F32),
            pltpu.VMEM((4 * GROUPS4, LANES), F32),
            pltpu.VMEM((GROUPS4 * EX, LANES), F32),
        ],
        compiler_params=pltpu.CompilerParams(vmem_limit_bytes=54848 << 10),
        name="prep",
    )(order, x, g)


ROWB = SIDE * EX
COLB = PITCH * PIV_DEV


def cost(flops, moved):
    return pl.CostEstimate(flops=flops, bytes_accessed=moved, transcendentals=0)


def unpack_kernel(*refs):
    packed, (all_ref, piv_ref) = refs[:4], refs[-2:]
    row = lax.broadcasted_iota(jnp.int32, (4 * LANES, 4 * LANES), 0)
    col = lax.broadcasted_iota(jnp.int32, (4 * LANES, 4 * LANES), 1)
    target = (row // CH) % 4 * LANES + row // LANES * CH + row % CH
    move = jnp.where(col == target, 1.0, 0.0).astype(BF16)
    flat = jnp.concatenate([ref[...].reshape(GROUPS4 * EX, LANES) for ref in packed], axis=1)
    moved = jnp.dot(flat, move, preferred_element_type=F32).astype(BF16)
    for group in range(GROUPS4):
        for j in range(4):
            if 4 * group + j < SPOTS:
                spot = moved[group * EX:(group + 1) * EX, j * LANES:(j + 1) * LANES]
                all_ref[4 * group + j] = spot
                piv_ref[4 * group + j] = spot[:PIV_DEV]


def unpack(arrays, name, after=()):
    vmem = pl.BlockSpec(memory_space=pltpu.VMEM)
    pivots = jax.ShapeDtypeStruct((SPOTS, PIV_DEV, LANES), BF16)
    return pl.pallas_call(
        unpack_kernel,
        out_shape=(jax.ShapeDtypeStruct((SPOTS, EX, LANES), BF16), pivots),
        in_specs=[vmem] * 4 + [pl.BlockSpec(memory_space=pl.ANY)] * len(after),
        out_specs=(vmem,) * 2,
        compiler_params=pltpu.CompilerParams(vmem_limit_bytes=12 << 20),
        cost_estimate=cost(0, 1 << 20),
        name=name,
    )(*arrays, *after)


CONTRACT = (((1,), (1,)), ((), ()))
SPANS = [(qy, min(qy + 2, SIDE)) for qy in range(0, SIDE, 2)]


def place_windows(values, window, pitch):
    count = values.shape[1]
    zero = jnp.zeros((count, LANES), BF16)
    for py in range(SIDE):
        for px in range(pitch):
            first = (py * pitch + px) * count
            for d in range(3):
                from_x = px + d - 1
                inside = 0 <= from_x < SIDE and px < SIDE
                window[first:first + count, d * LANES:(d + 1) * LANES] = values[py * SIDE + from_x] if inside else zero


def input_products(lx, rx, t):
    for start, stop in SPANS:
        right = rx[start * COLB:stop * COLB, :]
        for py in range(SIDE):
            left = lx[py * ROWB:(py + 1) * ROWB, :]
            t[py, :, start * COLB:stop * COLB] = lax.dot_general(left, right, CONTRACT, preferred_element_type=F32)


def panel_terms(g, gp, rg, t):
    for py in range(SIDE):
        for px in range(PITCH):
            col = (py * PITCH + px) * PIV_DEV
            rg[col:col + PIV_DEV, :] = gp[py * SIDE + px] if px < SIDE else jnp.zeros((PIV_DEV, LANES), BF16)
    acc = jnp.zeros((EX, COLB), F32)
    for start, stop in SPANS:
        right = rg[start * COLB:stop * COLB, :]
        for py in range(SIDE):
            left = g[py * SIDE:(py + 1) * SIDE].reshape(ROWB, LANES)
            gg = lax.dot_general(left, right, CONTRACT, preferred_element_type=F32)
            for qy in range(start, stop):
                for px in range(SIDE):
                    rows = slice(px * EX, (px + 1) * EX)
                    total = t[py, rows, qy * COLB:(qy + 1) * COLB]
                    if py > 0 and qy > 0:
                        total = total + t[py - 1, rows, (qy - 1) * COLB:qy * COLB]
                    if py < SIDE - 1 and qy < SIDE - 1:
                        total = total + t[py + 1, rows, (qy + 1) * COLB:(qy + 2) * COLB]
                    acc = acc + gg[rows, (qy - start) * COLB:(qy - start + 1) * COLB] * total
    acc = acc + pltpu.roll(acc, 64, 1)
    acc = acc + pltpu.roll(acc, 32, 1)
    return acc + pltpu.roll(acc, 16, 1)


def own_inputs_kernel(x, xp, after, t_out, lx_out, rx):
    place_windows(x, lx_out, SIDE)
    place_windows(xp, rx, PITCH)
    input_products(lx_out, rx, t_out)


def cross_inputs_kernel(lx, xp, t_out, rx):
    place_windows(xp, rx, PITCH)
    input_products(lx, rx, t_out)


def own_kernel(t, g, gp, out_ref, rg):
    out_ref[...] = panel_terms(g, gp, rg, t)


def cross_kernel(t, g, gp, own_ref, ridge, out_ref, ridge_out, rg):
    ridge_out[...] = ridge[...]
    across = panel_terms(g, gp, rg, t)
    lane = lax.broadcasted_iota(jnp.int32, (8, LANES), 1)
    is_own = (lane // PIV_DEV) % 2 == lax.axis_index("rows")
    packed = jnp.zeros((8, LANES), F32)
    for j in range(4):
        rows = slice(8 * j, 8 * j + 8)
        packed = jnp.where(lane // EX == j, jnp.where(is_own, own_ref[rows, :], across[rows]), packed)
    out_ref[...] = packed


def terms(kernel, arrays, outs, width, flops, name):
    vmem = pl.BlockSpec(memory_space=pltpu.VMEM)
    return pl.pallas_call(
        kernel,
        out_shape=tuple(jax.ShapeDtypeStruct(*out) for out in outs),
        in_specs=[vmem] * len(arrays),
        out_specs=(vmem,) * len(outs),
        scratch_shapes=[pltpu.VMEM((SIDE * COLB, width), BF16)],
        compiler_params=pltpu.CompilerParams(vmem_limit_bytes=20 << 20),
        cost_estimate=cost(flops, 4 << 20),
        name=name,
    )(*arrays)


def rows_of(packed, count):
    return jnp.concatenate(
        [packed[:, EX * j:EX * (j + 1)] for j in range(count)], axis=0
    )


def tree_sum(values):
    while len(values) > 1:
        values = [a + b for a, b in zip(values[0::2], values[1::2])]
    return values[0]


def final_kernel(terms_ref, ridge_ref, gram_ref, factor_ref):
    count = terms_ref.shape[0] // 2
    sums = [tree_sum([terms_ref[g * count + i] for i in range(count)]) for g in range(2)]
    panel = rows_of(jnp.where(lax.axis_index("rows") == 0, sums[0], sums[1]), 4)
    gram_ref[...] = panel
    diag = jnp.concatenate([rows_of(total, 2) for total in sums], axis=0)
    row_id = lax.broadcasted_iota(jnp.int32, (EX, EX), 0)
    col_id = lax.broadcasted_iota(jnp.int32, (EX, EX), 1)
    ridge = jnp.where(row_id == col_id, jnp.broadcast_to(ridge_ref[...], (EX, EX)), 0.0)
    system = 0.5 * (diag + jnp.transpose(diag)) + ridge
    factor = jnp.zeros((EX, EX), F32)
    step = 8
    for j in range(0, EX, step):
        sys_cols = [jnp.broadcast_to(system[:, j + k:j + k + 1], (EX, EX)) for k in range(step)]
        pan_cols = [jnp.broadcast_to(panel[:, j + k:j + k + 1], (EX, EX)) for k in range(step)]
        sys_rows = [system[j + k:j + k + 1, :] for k in range(step)]
        for k in range(step):
            scale = lax.rsqrt(sys_cols[k][j + k:j + k + 1, :])
            sys_cols[k], pan_cols[k], sys_rows[k] = sys_cols[k] * scale, pan_cols[k] * scale, sys_rows[k] * scale
            factor = jnp.where(col_id == j + k, pan_cols[k], factor)
            for m in range(k + 1, step):
                entry = sys_cols[k][j + m:j + m + 1, :]
                sys_cols[m] = sys_cols[m] - sys_cols[k] * entry
                pan_cols[m] = pan_cols[m] - pan_cols[k] * entry
                sys_rows[m] = sys_rows[m] - sys_rows[k] * entry
        if j + step < EX:
            for k in range(step):
                system = system - sys_cols[k] * sys_rows[k]
                panel = panel - pan_cols[k] * sys_rows[k]
    factor_ref[...] = factor


def final(terms_of_all, ridge):
    vmem = pl.BlockSpec(memory_space=pltpu.VMEM)
    out = jax.ShapeDtypeStruct((EX, EX), F32)
    return pl.pallas_call(
        final_kernel,
        out_shape=(out, out),
        in_specs=[vmem] * 2,
        out_specs=(vmem, vmem),
        compiler_params=pltpu.CompilerParams(vmem_limit_bytes=8 << 20),
        name="solve",
    )(terms_of_all, ridge)


def exchange(value, count, flip):
    return lax.ppermute(value, "chan", [(i, i ^ flip) for i in range(count)])


def gather(value, count, first, second):
    received = exchange(value, count, first)
    return [value, exchange(value, count, second), received, exchange(received, count, second)]


def exchange_across(value, count):
    pairs = [(g * count + i, (1 - g) * count + i) for g in range(2) for i in range(count)]
    return lax.ppermute(value, ("rows", "chan"), pairs)


def local_packed(count, activations, cotangents, ordering, ridge):
    x = jnp.transpose(activations, (1, 2, 0, 3)).reshape(SPOTS, EX, CH)
    xo, go = prep(ordering, x, cotangents)
    own_g = gather(go, count, 8, 4)
    x_all, x_piv = unpack(gather(xo, count, 2, 1), "unpack_x", (own_g[1],))
    x_cross = exchange_across(x_piv, count)
    g_all, g_piv = unpack(own_g, "unpack_g", (x_piv,))
    g_cross = exchange_across(g_piv, count)
    flops, product = 6 * 10**9, ((SIDE, ROWB, SIDE * COLB), F32)
    windows = ((SPOTS * EX, 3 * LANES), BF16)
    products, lx = terms(own_inputs_kernel, (x_all, x_piv, g_piv), (product, windows), 3 * LANES, flops, "own_inputs")
    own_term, = terms(own_kernel, (products, g_all, g_piv), (((EX, LANES), F32),), LANES, flops, "terms_own")
    products, = terms(cross_inputs_kernel, (lx, x_cross), (product,), 3 * LANES, flops, "cross_inputs")
    arrays = (products, g_all, g_cross, own_term, ridge.reshape(1, EX))
    term, ridge = terms(cross_kernel, arrays, (((8, LANES), F32), ((1, EX), F32)), LANES, flops, "terms_cross")
    copies = jnp.broadcast_to(term, (2 * count, 8, LANES))
    return final(lax.all_to_all(copies, ("rows", "chan"), 0, 0), ridge)


def jacobian_block(grad_rows, input_rows):
    example_count = input_rows.shape[0]
    side_len = input_rows.shape[1]
    channel_count = input_rows.shape[3]
    grad_count = grad_rows.shape[1]
    grid_grads = grad_rows.reshape(example_count, grad_count, side_len, side_len)
    padded_grads = jnp.pad(grid_grads, ((0, 0), (0, 0), (1, 1), (1, 1)))
    shifted = []
    for row_shift in range(3):
        for col_shift in range(3):
            window = padded_grads[
                :,
                :,
                2 - row_shift : 2 - row_shift + side_len,
                2 - col_shift : 2 - col_shift + side_len,
            ]
            shifted.append(window.reshape(example_count, grad_count, side_len * side_len))
    stacked_grads = jnp.stack(shifted, axis=2).reshape(
        example_count, grad_count * 9, side_len * side_len
    )
    flat_inputs = input_rows.reshape(example_count, side_len * side_len, channel_count)
    product = jnp.einsum(
        "nkp,npq->nkq", stacked_grads, flat_inputs, preferred_element_type=jnp.float32
    )
    return product.astype(jnp.bfloat16).reshape(example_count, -1)


def gram_block(left_rows, right_rows):
    return lax.dot_general(
        left_rows, right_rows, (((1,), (1,)), ((), ())), preferred_element_type=jnp.float32
    )


def local(activations, cotangents, ordering, ridge):
    local_order = ordering[0]
    own_inputs = jnp.take(activations, local_order, axis=0)
    own_grads = jnp.take(cotangents, local_order, axis=0)
    pivot_count = PIV_DEV
    pivot_inputs, pivot_grads = (
        lax.all_gather(own_inputs[:pivot_count], "rows", axis=0, tiled=True),
        lax.all_gather(own_grads[:pivot_count], "rows", axis=0, tiled=True),
    )
    full_own, full_pivot = (
        lax.all_gather(own_inputs, "chan", axis=3, tiled=True),
        lax.all_gather(pivot_inputs, "chan", axis=3, tiled=True),
    )
    own_jac = jacobian_block(own_grads, full_own)
    pivot_jac = jacobian_block(pivot_grads, full_pivot)
    partial_panel = gram_block(own_jac, pivot_jac)
    gram_panel = lax.psum(partial_panel, "chan")
    diag_block = lax.all_gather(gram_panel[:pivot_count], "rows", axis=0, tiled=True)
    system = 0.5 * (diag_block + diag_block.T) + jnp.diag(ridge)
    lower = jnp.linalg.cholesky(system)
    factor_panel = jax.scipy.linalg.solve_triangular(lower, gram_panel.T, lower=True).T
    return (gram_panel, factor_panel)


def solution(mesh):
    row_groups, count = mesh.shape["rows"], mesh.shape["chan"]
    packed = row_groups == 2 and count == 16
    return jax.shard_map(
        functools.partial(local_packed, count) if packed else local,
        mesh=mesh,
        in_specs=(P("rows", None, None, "chan"), P("rows", "chan", None), P("rows", None), P()),
        out_specs=(P("rows", None), P("rows", None)),
        check_vma=False,
    )
```

```python
import functools

import jax
import jax.numpy as jnp
from jax import lax
from jax.experimental import pallas as pl
from jax.experimental.pallas import tpu as pltpu
from jax.sharding import PartitionSpec as P

PIV_DEV = 16

SIDE = 7
SPOTS = SIDE * SIDE
PITCH = 8
GROUPS4 = 13
CH = 32
EX = 32
LANES = 128
F32 = jnp.float32
BF16 = jnp.bfloat16


def fetch(sources, targets, sems):
    copies = [pltpu.make_async_copy(a, b, sems.at[i]) for i, (a, b) in enumerate(zip(sources, targets))]
    for copy in copies:
        copy.start()
    return copies


def prep_kernel(x_hbm, g_hbm, xo_ref, go_ref, x_ref, g_ref, sems, gs, gt, gout):
    copies = fetch((g_hbm, x_hbm), (g_ref, x_ref), sems)
    copies[0].wait()
    for k in range(EX):
        gs[k * CH:(k + 1) * CH, 0:SPOTS] = g_ref[k].astype(F32)
    gt[SPOTS:, :] = jnp.zeros((4 * GROUPS4 - SPOTS, LANES), F32)
    block_id = lax.broadcasted_iota(jnp.int32, (GROUPS4, LANES), 1) // CH
    for quad in range(EX // 4):
        gt[0:SPOTS, :] = jnp.transpose(gs[quad * LANES:(quad + 1) * LANES, :])[0:SPOTS, :]
        parts = [gt[pl.ds(j, GROUPS4, stride=4), :] for j in range(4)]
        for e in range(4):
            merged = jnp.zeros((GROUPS4, LANES), F32)
            for j in range(4):
                shift = (CH * (j - e)) % LANES
                moved = pltpu.roll(parts[j], shift, 1) if shift else parts[j]
                merged = jnp.where(block_id == j, moved, merged)
            gout[pl.ds(quad * 4 + e, GROUPS4, stride=EX), :] = merged
    for group in range(GROUPS4):
        go_ref[group] = gout[group * EX:(group + 1) * EX, :].astype(BF16)
    copies[1].wait()
    zero_block = jnp.zeros((EX, CH), BF16)
    for group in range(GROUPS4):
        spots = [4 * group + j for j in range(4)]
        xo_ref[group] = jnp.concatenate([x_ref[p] if p < SPOTS else zero_block for p in spots], axis=1)


def prep(x, g):
    full = jax.ShapeDtypeStruct((GROUPS4, EX, LANES), BF16)
    vmem = pl.BlockSpec(memory_space=pltpu.VMEM)
    return pl.pallas_call(
        prep_kernel,
        out_shape=(full, full),
        in_specs=[pl.BlockSpec(memory_space=pltpu.HBM)] * 2,
        out_specs=(vmem,) * 2,
        scratch_shapes=[
            pltpu.VMEM(x.shape, x.dtype),
            pltpu.VMEM(g.shape, g.dtype),
            pltpu.SemaphoreType.DMA((2,)),
            pltpu.VMEM((EX * CH, LANES), F32),
            pltpu.VMEM((4 * GROUPS4, LANES), F32),
            pltpu.VMEM((GROUPS4 * EX, LANES), F32),
        ],
        compiler_params=pltpu.CompilerParams(vmem_limit_bytes=54848 << 10),
        name="prep",
    )(x, g)


ROWB = SIDE * EX
COLB = PITCH * PIV_DEV


def cost(flops, moved):
    return pl.CostEstimate(flops=flops, bytes_accessed=moved, transcendentals=0)


def order_matrix(order):
    example = lax.broadcasted_iota(jnp.int32, (EX, EX), 0)
    return jnp.transpose(jnp.where(example == jnp.broadcast_to(order, (EX, EX)), 1.0, 0.0))


def unpack_kernel(*refs):
    packed, order_ref, (all_ref, piv_ref) = refs[:4], refs[4], refs[-2:]
    pick = order_matrix(order_ref[...])[:PIV_DEV].astype(BF16)
    row = lax.broadcasted_iota(jnp.int32, (4 * LANES, 4 * LANES), 0)
    col = lax.broadcasted_iota(jnp.int32, (4 * LANES, 4 * LANES), 1)
    target = (row // CH) % 4 * LANES + row // LANES * CH + row % CH
    move = jnp.where(col == target, 1.0, 0.0).astype(BF16)
    flat = jnp.concatenate([ref[...].reshape(GROUPS4 * EX, LANES) for ref in packed], axis=1)
    moved = jnp.dot(flat, move, preferred_element_type=F32).astype(BF16)
    for group in range(GROUPS4):
        rows = moved[group * EX:(group + 1) * EX]
        pivots = jnp.dot(pick, rows, preferred_element_type=F32).astype(BF16)
        for j in range(4):
            if 4 * group + j < SPOTS:
                all_ref[4 * group + j] = rows[:, j * LANES:(j + 1) * LANES]
                piv_ref[4 * group + j] = pivots[:, j * LANES:(j + 1) * LANES]


def unpack(arrays, order, name, after=()):
    vmem = pl.BlockSpec(memory_space=pltpu.VMEM)
    pivots = jax.ShapeDtypeStruct((SPOTS, PIV_DEV, LANES), BF16)
    return pl.pallas_call(
        unpack_kernel,
        out_shape=(jax.ShapeDtypeStruct((SPOTS, EX, LANES), BF16), pivots),
        in_specs=[vmem] * 5 + [pl.BlockSpec(memory_space=pl.ANY)] * len(after),
        out_specs=(vmem,) * 2,
        compiler_params=pltpu.CompilerParams(vmem_limit_bytes=12 << 20),
        cost_estimate=cost(0, 1 << 20),
        name=name,
    )(*arrays, order, *after)


CONTRACT = (((1,), (1,)), ((), ()))
SPANS = [(qy, min(qy + 2, SIDE)) for qy in range(0, SIDE, 2)]


def place_windows(values, window, pitch):
    count = values.shape[1]
    zero = jnp.zeros((count, LANES), BF16)
    for py in range(SIDE):
        for px in range(pitch):
            first = (py * pitch + px) * count
            for d in range(3):
                from_x = px + d - 1
                inside = 0 <= from_x < SIDE and px < SIDE
                window[first:first + count, d * LANES:(d + 1) * LANES] = values[py * SIDE + from_x] if inside else zero


def input_products(lx, rx, t):
    for start, stop in SPANS:
        right = rx[start * COLB:stop * COLB, :]
        for py in range(SIDE):
            left = lx[py * ROWB:(py + 1) * ROWB, :]
            t[py, :, start * COLB:stop * COLB] = lax.dot_general(left, right, CONTRACT, preferred_element_type=F32)


def panel_terms(g, gp, rg, t):
    for py in range(SIDE):
        for px in range(PITCH):
            col = (py * PITCH + px) * PIV_DEV
            rg[col:col + PIV_DEV, :] = gp[py * SIDE + px] if px < SIDE else jnp.zeros((PIV_DEV, LANES), BF16)
    acc = jnp.zeros((EX, COLB), F32)
    for start, stop in SPANS:
        right = rg[start * COLB:stop * COLB, :]
        for py in range(SIDE):
            left = g[py * SIDE:(py + 1) * SIDE].reshape(ROWB, LANES)
            gg = lax.dot_general(left, right, CONTRACT, preferred_element_type=F32)
            for qy in range(start, stop):
                for px in range(SIDE):
                    rows = slice(px * EX, (px + 1) * EX)
                    total = t[py, rows, qy * COLB:(qy + 1) * COLB]
                    if py > 0 and qy > 0:
                        total = total + t[py - 1, rows, (qy - 1) * COLB:qy * COLB]
                    if py < SIDE - 1 and qy < SIDE - 1:
                        total = total + t[py + 1, rows, (qy + 1) * COLB:(qy + 2) * COLB]
                    acc = acc + gg[rows, (qy - start) * COLB:(qy - start + 1) * COLB] * total
    acc = acc + pltpu.roll(acc, 64, 1)
    acc = acc + pltpu.roll(acc, 32, 1)
    return acc + pltpu.roll(acc, 16, 1)


def own_inputs_kernel(x, xp, after, t_out, lx_out, rx):
    place_windows(x, lx_out, SIDE)
    place_windows(xp, rx, PITCH)
    input_products(lx_out, rx, t_out)


def cross_inputs_kernel(lx, xp, t_out, rx):
    place_windows(xp, rx, PITCH)
    input_products(lx, rx, t_out)


def own_kernel(t, g, gp, out_ref, rg):
    out_ref[...] = panel_terms(g, gp, rg, t)


def cross_kernel(t, g, gp, own_ref, order_ref, ridge, out_ref, ridge_out, rg):
    ridge_out[...] = ridge[...]
    across = panel_terms(g, gp, rg, t)
    lane = lax.broadcasted_iota(jnp.int32, (EX, LANES), 1)
    both = jnp.where((lane // PIV_DEV) % 2 == lax.axis_index("rows"), own_ref[...], across)
    both = jnp.dot(order_matrix(order_ref[...]), both, precision=lax.Precision.HIGHEST, preferred_element_type=F32)
    packed = both[:8]
    for j in range(1, 4):
        packed = jnp.where(lane[:8] // EX == j, both[8 * j:8 * j + 8], packed)
    out_ref[...] = packed


def terms(kernel, arrays, outs, width, flops, name):
    vmem = pl.BlockSpec(memory_space=pltpu.VMEM)
    return pl.pallas_call(
        kernel,
        out_shape=tuple(jax.ShapeDtypeStruct(*out) for out in outs),
        in_specs=[vmem] * len(arrays),
        out_specs=(vmem,) * len(outs),
        scratch_shapes=[pltpu.VMEM((SIDE * COLB, width), BF16)],
        compiler_params=pltpu.CompilerParams(vmem_limit_bytes=20 << 20),
        cost_estimate=cost(flops, 4 << 20),
        name=name,
    )(*arrays)


def rows_of(packed, count):
    return jnp.concatenate(
        [packed[:, EX * j:EX * (j + 1)] for j in range(count)], axis=0
    )


def tree_sum(values):
    while len(values) > 1:
        values = [a + b for a, b in zip(values[0::2], values[1::2])]
    return values[0]


def final_kernel(terms_ref, ridge_ref, gram_ref, factor_ref):
    count = terms_ref.shape[0] // 2
    sums = [tree_sum([terms_ref[g * count + i] for i in range(count)]) for g in range(2)]
    panel = rows_of(jnp.where(lax.axis_index("rows") == 0, sums[0], sums[1]), 4)
    gram_ref[...] = panel
    diag = jnp.concatenate([rows_of(total, 2) for total in sums], axis=0)
    row_id = lax.broadcasted_iota(jnp.int32, (EX, EX), 0)
    col_id = lax.broadcasted_iota(jnp.int32, (EX, EX), 1)
    ridge = jnp.where(row_id == col_id, jnp.broadcast_to(ridge_ref[...], (EX, EX)), 0.0)
    system = 0.5 * (diag + jnp.transpose(diag)) + ridge
    factor = jnp.zeros((EX, EX), F32)
    step = 8
    for j in range(0, EX, step):
        sys_cols = [jnp.broadcast_to(system[:, j + k:j + k + 1], (EX, EX)) for k in range(step)]
        pan_cols = [jnp.broadcast_to(panel[:, j + k:j + k + 1], (EX, EX)) for k in range(step)]
        sys_rows = [system[j + k:j + k + 1, :] for k in range(step)]
        for k in range(step):
            scale = lax.rsqrt(sys_cols[k][j + k:j + k + 1, :])
            sys_cols[k], pan_cols[k], sys_rows[k] = sys_cols[k] * scale, pan_cols[k] * scale, sys_rows[k] * scale
            factor = jnp.where(col_id == j + k, pan_cols[k], factor)
            for m in range(k + 1, step):
                entry = sys_cols[k][j + m:j + m + 1, :]
                sys_cols[m] = sys_cols[m] - sys_cols[k] * entry
                pan_cols[m] = pan_cols[m] - pan_cols[k] * entry
                sys_rows[m] = sys_rows[m] - sys_rows[k] * entry
        if j + step < EX:
            for k in range(step):
                system = system - sys_cols[k] * sys_rows[k]
                panel = panel - pan_cols[k] * sys_rows[k]
    factor_ref[...] = factor


def final(terms_of_all, ridge):
    vmem = pl.BlockSpec(memory_space=pltpu.VMEM)
    out = jax.ShapeDtypeStruct((EX, EX), F32)
    return pl.pallas_call(
        final_kernel,
        out_shape=(out, out),
        in_specs=[vmem] * 2,
        out_specs=(vmem, vmem),
        compiler_params=pltpu.CompilerParams(vmem_limit_bytes=8 << 20),
        name="solve",
    )(terms_of_all, ridge)


def exchange(value, count, flip):
    return lax.ppermute(value, "chan", [(i, i ^ flip) for i in range(count)])


def gather(value, count, first, second):
    received = exchange(value, count, first)
    return [value, exchange(value, count, second), received, exchange(received, count, second)]


def exchange_across(value, count):
    pairs = [(g * count + i, (1 - g) * count + i) for g in range(2) for i in range(count)]
    return lax.ppermute(value, ("rows", "chan"), pairs)


def local_packed(count, activations, cotangents, ordering, ridge):
    x = jnp.transpose(activations, (1, 2, 0, 3)).reshape(SPOTS, EX, CH)
    xo, go = prep(x, cotangents)
    own_g = gather(go, count, 8, 4)
    x_all, x_piv = unpack(gather(xo, count, 2, 1), ordering, "unpack_x", (own_g[1],))
    x_cross = exchange_across(x_piv, count)
    g_all, g_piv = unpack(own_g, ordering, "unpack_g", (x_piv,))
    g_cross = exchange_across(g_piv, count)
    flops, product = 6 * 10**9, ((SIDE, ROWB, SIDE * COLB), F32)
    windows = ((SPOTS * EX, 3 * LANES), BF16)
    products, lx = terms(own_inputs_kernel, (x_all, x_piv, g_piv), (product, windows), 3 * LANES, flops, "own_inputs")
    own_term, = terms(own_kernel, (products, g_all, g_piv), (((EX, LANES), F32),), LANES, flops, "terms_own")
    products, = terms(cross_inputs_kernel, (lx, x_cross), (product,), 3 * LANES, flops, "cross_inputs")
    arrays = (products, g_all, g_cross, own_term, ordering, ridge.reshape(1, EX))
    term, ridge = terms(cross_kernel, arrays, (((8, LANES), F32), ((1, EX), F32)), LANES, flops, "terms_cross")
    copies = jnp.broadcast_to(term, (2 * count, 8, LANES))
    return final(lax.all_to_all(copies, ("rows", "chan"), 0, 0), ridge)


def jacobian_block(grad_rows, input_rows):
    example_count = input_rows.shape[0]
    side_len = input_rows.shape[1]
    channel_count = input_rows.shape[3]
    grad_count = grad_rows.shape[1]
    grid_grads = grad_rows.reshape(example_count, grad_count, side_len, side_len)
    padded_grads = jnp.pad(grid_grads, ((0, 0), (0, 0), (1, 1), (1, 1)))
    shifted = []
    for row_shift in range(3):
        for col_shift in range(3):
            window = padded_grads[
                :,
                :,
                2 - row_shift : 2 - row_shift + side_len,
                2 - col_shift : 2 - col_shift + side_len,
            ]
            shifted.append(window.reshape(example_count, grad_count, side_len * side_len))
    stacked_grads = jnp.stack(shifted, axis=2).reshape(
        example_count, grad_count * 9, side_len * side_len
    )
    flat_inputs = input_rows.reshape(example_count, side_len * side_len, channel_count)
    product = jnp.einsum(
        "nkp,npq->nkq", stacked_grads, flat_inputs, preferred_element_type=jnp.float32
    )
    return product.astype(jnp.bfloat16).reshape(example_count, -1)


def gram_block(left_rows, right_rows):
    return lax.dot_general(
        left_rows, right_rows, (((1,), (1,)), ((), ())), preferred_element_type=jnp.float32
    )


def local(activations, cotangents, ordering, ridge):
    local_order = ordering[0]
    own_inputs = jnp.take(activations, local_order, axis=0)
    own_grads = jnp.take(cotangents, local_order, axis=0)
    pivot_count = PIV_DEV
    pivot_inputs, pivot_grads = (
        lax.all_gather(own_inputs[:pivot_count], "rows", axis=0, tiled=True),
        lax.all_gather(own_grads[:pivot_count], "rows", axis=0, tiled=True),
    )
    full_own, full_pivot = (
        lax.all_gather(own_inputs, "chan", axis=3, tiled=True),
        lax.all_gather(pivot_inputs, "chan", axis=3, tiled=True),
    )
    own_jac = jacobian_block(own_grads, full_own)
    pivot_jac = jacobian_block(pivot_grads, full_pivot)
    partial_panel = gram_block(own_jac, pivot_jac)
    gram_panel = lax.psum(partial_panel, "chan")
    diag_block = lax.all_gather(gram_panel[:pivot_count], "rows", axis=0, tiled=True)
    system = 0.5 * (diag_block + diag_block.T) + jnp.diag(ridge)
    lower = jnp.linalg.cholesky(system)
    factor_panel = jax.scipy.linalg.solve_triangular(lower, gram_panel.T, lower=True).T
    return (gram_panel, factor_panel)


def solution(mesh):
    row_groups, count = mesh.shape["rows"], mesh.shape["chan"]
    packed = row_groups == 2 and count == 16
    return jax.shard_map(
        functools.partial(local_packed, count) if packed else local,
        mesh=mesh,
        in_specs=(P("rows", None, None, "chan"), P("rows", "chan", None), P("rows", None), P()),
        out_specs=(P("rows", None), P("rows", None)),
        check_vma=False,
    )
```

```python
import functools

import jax
import jax.numpy as jnp
from jax import lax
from jax.experimental import pallas as pl
from jax.experimental.pallas import tpu as pltpu
from jax.sharding import PartitionSpec as P

PIV_DEV = 16

SIDE = 7
SPOTS = SIDE * SIDE
PITCH = 8
GROUPS4 = 13
CH = 32
EX = 32
LANES = 128
F32 = jnp.float32
BF16 = jnp.bfloat16


def fetch(sources, targets, sems):
    copies = [pltpu.make_async_copy(a, b, sems.at[i]) for i, (a, b) in enumerate(zip(sources, targets))]
    for copy in copies:
        copy.start()
    return copies


def prep_kernel(order_hbm, x_hbm, g_hbm, xo_ref, go_ref, order_ref, x_ref, g_ref, sems, gs, gt, gout):
    copies = fetch((order_hbm, g_hbm, x_hbm), (order_ref, g_ref, x_ref), sems)
    copies[0].wait()
    copies[1].wait()
    row_id = lax.broadcasted_iota(jnp.int32, (EX, EX), 0)
    col_id = lax.broadcasted_iota(jnp.int32, (EX, EX), 1)
    onehot = jnp.zeros((EX, EX), F32)
    for k in range(EX):
        example = order_ref[0, k]
        onehot = jnp.where((row_id == k) & (col_id == example), 1.0, onehot)
        gs[k * CH:(k + 1) * CH, 0:SPOTS] = g_ref[example].astype(F32)
    gt[SPOTS:, :] = jnp.zeros((4 * GROUPS4 - SPOTS, LANES), F32)
    block_id = lax.broadcasted_iota(jnp.int32, (GROUPS4, LANES), 1) // CH
    for quad in range(EX // 4):
        gt[0:SPOTS, :] = jnp.transpose(gs[quad * LANES:(quad + 1) * LANES, :])[0:SPOTS, :]
        parts = [gt[pl.ds(j, GROUPS4, stride=4), :] for j in range(4)]
        for e in range(4):
            merged = jnp.zeros((GROUPS4, LANES), F32)
            for j in range(4):
                shift = (CH * (j - e)) % LANES
                moved = pltpu.roll(parts[j], shift, 1) if shift else parts[j]
                merged = jnp.where(block_id == j, moved, merged)
            gout[pl.ds(quad * 4 + e, GROUPS4, stride=EX), :] = merged
    for group in range(GROUPS4):
        go_ref[group] = gout[group * EX:(group + 1) * EX, :].astype(BF16)
    copies[2].wait()
    onehot = onehot.astype(BF16)
    zero_block = jnp.zeros((EX, CH), BF16)
    for group in range(GROUPS4):
        spots = [4 * group + j for j in range(4)]
        packed = jnp.concatenate([x_ref[p] if p < SPOTS else zero_block for p in spots], axis=1)
        xo_ref[group] = jnp.dot(onehot, packed, preferred_element_type=F32).astype(BF16)


def prep(order, x, g):
    full = jax.ShapeDtypeStruct((GROUPS4, EX, LANES), BF16)
    vmem = pl.BlockSpec(memory_space=pltpu.VMEM)
    return pl.pallas_call(
        prep_kernel,
        out_shape=(full, full),
        in_specs=[pl.BlockSpec(memory_space=pltpu.HBM)] * 3,
        out_specs=(vmem,) * 2,
        scratch_shapes=[
            pltpu.SMEM(order.shape, order.dtype),
            pltpu.VMEM(x.shape, x.dtype),
            pltpu.VMEM(g.shape, g.dtype),
            pltpu.SemaphoreType.DMA((3,)),
            pltpu.VMEM((EX * CH, LANES), F32),
            pltpu.VMEM((4 * GROUPS4, LANES), F32),
            pltpu.VMEM((GROUPS4 * EX, LANES), F32),
        ],
        compiler_params=pltpu.CompilerParams(vmem_limit_bytes=54848 << 10),
        name="prep",
    )(order, x, g)


ROWB = SIDE * EX
COLB = PITCH * PIV_DEV


def cost(flops, moved):
    return pl.CostEstimate(flops=flops, bytes_accessed=moved, transcendentals=0)


def unpack_kernel(*refs):
    packed, (all_ref, piv_ref) = refs[:4], refs[-2:]
    row = lax.broadcasted_iota(jnp.int32, (4 * LANES, 4 * LANES), 0)
    col = lax.broadcasted_iota(jnp.int32, (4 * LANES, 4 * LANES), 1)
    target = (row // CH) % 4 * LANES + row // LANES * CH + row % CH
    move = jnp.where(col == target, 1.0, 0.0).astype(BF16)
    flat = jnp.concatenate([ref[...].reshape(GROUPS4 * EX, LANES) for ref in packed], axis=1)
    moved = jnp.dot(flat, move, preferred_element_type=F32).astype(BF16)
    for group in range(GROUPS4):
        for j in range(4):
            if 4 * group + j < SPOTS:
                spot = moved[group * EX:(group + 1) * EX, j * LANES:(j + 1) * LANES]
                all_ref[4 * group + j] = spot
                piv_ref[4 * group + j] = spot[:PIV_DEV]


def unpack(arrays, name, after=()):
    vmem = pl.BlockSpec(memory_space=pltpu.VMEM)
    pivots = jax.ShapeDtypeStruct((SPOTS, PIV_DEV, LANES), BF16)
    return pl.pallas_call(
        unpack_kernel,
        out_shape=(jax.ShapeDtypeStruct((SPOTS, EX, LANES), BF16), pivots),
        in_specs=[vmem] * 4 + [pl.BlockSpec(memory_space=pl.ANY)] * len(after),
        out_specs=(vmem,) * 2,
        compiler_params=pltpu.CompilerParams(vmem_limit_bytes=12 << 20),
        cost_estimate=cost(0, 1 << 20),
        name=name,
    )(*arrays, *after)


CONTRACT = (((1,), (1,)), ((), ()))
SPANS = [(qy, min(qy + 2, SIDE)) for qy in range(0, SIDE, 2)]


def place_windows(values, window, pitch):
    count = values.shape[1]
    zero = jnp.zeros((count, LANES), BF16)
    for py in range(SIDE):
        for px in range(pitch):
            first = (py * pitch + px) * count
            for d in range(3):
                from_x = px + d - 1
                inside = 0 <= from_x < SIDE and px < SIDE
                window[first:first + count, d * LANES:(d + 1) * LANES] = values[py * SIDE + from_x] if inside else zero


def input_products(lx, rx, t):
    for start, stop in SPANS:
        right = rx[start * COLB:stop * COLB, :]
        for py in range(SIDE):
            left = lx[py * ROWB:(py + 1) * ROWB, :]
            t[py, :, start * COLB:stop * COLB] = lax.dot_general(left, right, CONTRACT, preferred_element_type=F32)


def panel_terms(g, gp, rg, t):
    for py in range(SIDE):
        for px in range(PITCH):
            col = (py * PITCH + px) * PIV_DEV
            rg[col:col + PIV_DEV, :] = gp[py * SIDE + px] if px < SIDE else jnp.zeros((PIV_DEV, LANES), BF16)
    acc = jnp.zeros((EX, COLB), F32)
    for start, stop in SPANS:
        right = rg[start * COLB:stop * COLB, :]
        for py in range(SIDE):
            left = g[py * SIDE:(py + 1) * SIDE].reshape(ROWB, LANES)
            gg = lax.dot_general(left, right, CONTRACT, preferred_element_type=F32)
            for qy in range(start, stop):
                for px in range(SIDE):
                    rows = slice(px * EX, (px + 1) * EX)
                    total = t[py, rows, qy * COLB:(qy + 1) * COLB]
                    if py > 0 and qy > 0:
                        total = total + t[py - 1, rows, (qy - 1) * COLB:qy * COLB]
                    if py < SIDE - 1 and qy < SIDE - 1:
                        total = total + t[py + 1, rows, (qy + 1) * COLB:(qy + 2) * COLB]
                    acc = acc + gg[rows, (qy - start) * COLB:(qy - start + 1) * COLB] * total
    acc = acc + pltpu.roll(acc, 64, 1)
    acc = acc + pltpu.roll(acc, 32, 1)
    return acc + pltpu.roll(acc, 16, 1)


def own_inputs_kernel(x, xp, t_out, lx_out, rx):
    place_windows(x, lx_out, SIDE)
    place_windows(xp, rx, PITCH)
    input_products(lx_out, rx, t_out)


def cross_inputs_kernel(lx, xp, t_out, rx):
    place_windows(xp, rx, PITCH)
    input_products(lx, rx, t_out)


def own_kernel(t, g, gp, out_ref, rg):
    out_ref[...] = panel_terms(g, gp, rg, t)


def cross_kernel(t, g, gp, own_ref, ridge, out_ref, ridge_out, rg):
    ridge_out[...] = ridge[...]
    across = panel_terms(g, gp, rg, t)
    lane = lax.broadcasted_iota(jnp.int32, (8, LANES), 1)
    is_own = (lane // PIV_DEV) % 2 == lax.axis_index("rows")
    packed = jnp.zeros((8, LANES), F32)
    for j in range(4):
        rows = slice(8 * j, 8 * j + 8)
        packed = jnp.where(lane // EX == j, jnp.where(is_own, own_ref[rows, :], across[rows]), packed)
    out_ref[...] = packed


def terms(kernel, arrays, outs, width, flops, name):
    vmem = pl.BlockSpec(memory_space=pltpu.VMEM)
    return pl.pallas_call(
        kernel,
        out_shape=tuple(jax.ShapeDtypeStruct(*out) for out in outs),
        in_specs=[vmem] * len(arrays),
        out_specs=(vmem,) * len(outs),
        scratch_shapes=[pltpu.VMEM((SIDE * COLB, width), BF16)],
        compiler_params=pltpu.CompilerParams(vmem_limit_bytes=20 << 20),
        cost_estimate=cost(flops, 4 << 20),
        name=name,
    )(*arrays)


def rows_of(packed, count):
    return jnp.concatenate(
        [packed[:, EX * j:EX * (j + 1)] for j in range(count)], axis=0
    )


def tree_sum(values):
    while len(values) > 1:
        values = [a + b for a, b in zip(values[0::2], values[1::2])]
    return values[0]


def final_kernel(terms_ref, ridge_ref, gram_ref, factor_ref):
    count = terms_ref.shape[0] // 2
    sums = [tree_sum([terms_ref[g * count + i] for i in range(count)]) for g in range(2)]
    panel = rows_of(jnp.where(lax.axis_index("rows") == 0, sums[0], sums[1]), 4)
    gram_ref[...] = panel
    diag = jnp.concatenate([rows_of(total, 2) for total in sums], axis=0)
    row_id = lax.broadcasted_iota(jnp.int32, (EX, EX), 0)
    col_id = lax.broadcasted_iota(jnp.int32, (EX, EX), 1)
    ridge = jnp.where(row_id == col_id, jnp.broadcast_to(ridge_ref[...], (EX, EX)), 0.0)
    system = 0.5 * (diag + jnp.transpose(diag)) + ridge
    factor = jnp.zeros((EX, EX), F32)
    step = 16
    for j in range(0, EX, step):
        sys_cols = [jnp.broadcast_to(system[:, j + k:j + k + 1], (EX, EX)) for k in range(step)]
        pan_cols = [jnp.broadcast_to(panel[:, j + k:j + k + 1], (EX, EX)) for k in range(step)]
        sys_rows = [system[j + k:j + k + 1, :] for k in range(step)]
        for k in range(step):
            scale = lax.rsqrt(sys_cols[k][j + k:j + k + 1, :])
            sys_cols[k], pan_cols[k], sys_rows[k] = sys_cols[k] * scale, pan_cols[k] * scale, sys_rows[k] * scale
            factor = jnp.where(col_id == j + k, pan_cols[k], factor)
            for m in range(k + 1, step):
                entry = sys_cols[k][j + m:j + m + 1, :]
                sys_cols[m] = sys_cols[m] - sys_cols[k] * entry
                pan_cols[m] = pan_cols[m] - pan_cols[k] * entry
                sys_rows[m] = sys_rows[m] - sys_rows[k] * entry
        if j + step < EX:
            for k in range(step):
                system = system - sys_cols[k] * sys_rows[k]
                panel = panel - pan_cols[k] * sys_rows[k]
    factor_ref[...] = factor


def final(terms_of_all, ridge):
    vmem = pl.BlockSpec(memory_space=pltpu.VMEM)
    out = jax.ShapeDtypeStruct((EX, EX), F32)
    return pl.pallas_call(
        final_kernel,
        out_shape=(out, out),
        in_specs=[vmem] * 2,
        out_specs=(vmem, vmem),
        compiler_params=pltpu.CompilerParams(vmem_limit_bytes=8 << 20),
        name="solve",
    )(terms_of_all, ridge)


def exchange(value, count, flip):
    return lax.ppermute(value, "chan", [(i, i ^ flip) for i in range(count)])


def gather(value, count, first, second):
    received = exchange(value, count, first)
    return [value, exchange(value, count, second), received, exchange(received, count, second)]


def exchange_across(value, count):
    pairs = [(g * count + i, (1 - g) * count + i) for g in range(2) for i in range(count)]
    return lax.ppermute(value, ("rows", "chan"), pairs)


def local_packed(count, activations, cotangents, ordering, ridge):
    x = jnp.transpose(activations, (1, 2, 0, 3)).reshape(SPOTS, EX, CH)
    xo, go = prep(ordering, x, cotangents)
    own_g = gather(go, count, 8, 4)
    x_all, x_piv = unpack(gather(xo, count, 2, 1), "unpack_x", (own_g[1],))
    x_cross = exchange_across(x_piv, count)
    g_all, g_piv = unpack(own_g, "unpack_g", (x_piv,))
    g_cross = exchange_across(g_piv, count)
    flops, product = 6 * 10**9, ((SIDE, ROWB, SIDE * COLB), F32)
    windows = ((SPOTS * EX, 3 * LANES), BF16)
    products, lx = terms(own_inputs_kernel, (x_all, x_piv), (product, windows), 3 * LANES, flops, "own_inputs")
    own_term, = terms(own_kernel, (products, g_all, g_piv), (((EX, LANES), F32),), LANES, flops, "terms_own")
    products, = terms(cross_inputs_kernel, (lx, x_cross), (product,), 3 * LANES, flops, "cross_inputs")
    arrays = (products, g_all, g_cross, own_term, ridge.reshape(1, EX))
    term, ridge = terms(cross_kernel, arrays, (((8, LANES), F32), ((1, EX), F32)), LANES, flops, "terms_cross")
    copies = jnp.broadcast_to(term, (2 * count, 8, LANES))
    return final(lax.all_to_all(copies, ("rows", "chan"), 0, 0), ridge)


def jacobian_block(grad_rows, input_rows):
    example_count = input_rows.shape[0]
    side_len = input_rows.shape[1]
    channel_count = input_rows.shape[3]
    grad_count = grad_rows.shape[1]
    grid_grads = grad_rows.reshape(example_count, grad_count, side_len, side_len)
    padded_grads = jnp.pad(grid_grads, ((0, 0), (0, 0), (1, 1), (1, 1)))
    shifted = []
    for row_shift in range(3):
        for col_shift in range(3):
            window = padded_grads[
                :,
                :,
                2 - row_shift : 2 - row_shift + side_len,
                2 - col_shift : 2 - col_shift + side_len,
            ]
            shifted.append(window.reshape(example_count, grad_count, side_len * side_len))
    stacked_grads = jnp.stack(shifted, axis=2).reshape(
        example_count, grad_count * 9, side_len * side_len
    )
    flat_inputs = input_rows.reshape(example_count, side_len * side_len, channel_count)
    product = jnp.einsum(
        "nkp,npq->nkq", stacked_grads, flat_inputs, preferred_element_type=jnp.float32
    )
    return product.astype(jnp.bfloat16).reshape(example_count, -1)


def gram_block(left_rows, right_rows):
    return lax.dot_general(
        left_rows, right_rows, (((1,), (1,)), ((), ())), preferred_element_type=jnp.float32
    )


def local(activations, cotangents, ordering, ridge):
    local_order = ordering[0]
    own_inputs = jnp.take(activations, local_order, axis=0)
    own_grads = jnp.take(cotangents, local_order, axis=0)
    pivot_count = PIV_DEV
    pivot_inputs, pivot_grads = (
        lax.all_gather(own_inputs[:pivot_count], "rows", axis=0, tiled=True),
        lax.all_gather(own_grads[:pivot_count], "rows", axis=0, tiled=True),
    )
    full_own, full_pivot = (
        lax.all_gather(own_inputs, "chan", axis=3, tiled=True),
        lax.all_gather(pivot_inputs, "chan", axis=3, tiled=True),
    )
    own_jac = jacobian_block(own_grads, full_own)
    pivot_jac = jacobian_block(pivot_grads, full_pivot)
    partial_panel = gram_block(own_jac, pivot_jac)
    gram_panel = lax.psum(partial_panel, "chan")
    diag_block = lax.all_gather(gram_panel[:pivot_count], "rows", axis=0, tiled=True)
    system = 0.5 * (diag_block + diag_block.T) + jnp.diag(ridge)
    lower = jnp.linalg.cholesky(system)
    factor_panel = jax.scipy.linalg.solve_triangular(lower, gram_panel.T, lower=True).T
    return (gram_panel, factor_panel)


def solution(mesh):
    row_groups, count = mesh.shape["rows"], mesh.shape["chan"]
    packed = row_groups == 2 and count == 16
    return jax.shard_map(
        functools.partial(local_packed, count) if packed else local,
        mesh=mesh,
        in_specs=(P("rows", None, None, "chan"), P("rows", "chan", None), P("rows", None), P()),
        out_specs=(P("rows", None), P("rows", None)),
        check_vma=False,
    )
```
